32 devices in a mesh: batch: 8 (over z, y), seq: 4 (over x, core).
Axes of the slice: x: 2, y: 2, z: 4, core: 2. Of those that a mesh axis runs over, the one named last changes fastest.
Arguments:
- tokens: bfloat16 [24, 1024, 768], P('batch', 'seq'), may hold values from -6 to 6
- lengths: int32 [24], P('batch'), may hold values from 513 to 1024, as said below
- w_query: bfloat16 [2, 768, 768], replicated, may hold values from -0.21875 to 0.21875
- b_query: bfloat16 [2, 768], replicated, may hold values from -3 to 3
- w_key: bfloat16 [2, 768, 768], replicated, may hold values from -0.21875 to 0.21875
- w_value: bfloat16 [2, 768, 768], replicated, may hold values from -0.21875 to 0.21875
- b_value: bfloat16 [2, 768], replicated, may hold values from -3 to 3
- w_out: bfloat16 [2, 768, 768], replicated, may hold values from -2.5 to 2.5
- b_out: bfloat16 [2, 768], replicated, may hold values from -3 to 3
- gain_one: bfloat16 [2, 768], replicated, may hold values from 0.25 to 1.75
- shift_one: bfloat16 [2, 768], replicated, may hold values from -2 to 2
- w_up: bfloat16 [2, 768, 3072], replicated, may hold values from -0.21875 to 0.21875
- b_up: bfloat16 [2, 3072], replicated, may hold values from -3 to 3
- w_down: bfloat16 [2, 3072, 768], replicated, may hold values from -0.109375 to 0.109375
- b_down: bfloat16 [2, 768], replicated, may hold values from -3 to 3
- gain_two: bfloat16 [2, 768], replicated, may hold values from 0.25 to 1.75
- shift_two: bfloat16 [2, 768], replicated, may hold values from -2 to 2
- cotangent: bfloat16 [24, 1024, 768], P('batch', 'seq'), may hold values from -6 to 6
Outputs:
- output: bfloat16 [24, 1024, 768], P('batch', 'seq')
- grad_tokens: float32 [24, 1024, 768], P('batch', 'seq')
- grad_w_query: float32 [2, 768, 768], P(None, ('batch', 'seq'))
- grad_b_query: float32 [2, 768], P(None, ('batch', 'seq'))
- grad_w_key: float32 [2, 768, 768], P(None, ('batch', 'seq'))
- grad_w_value: float32 [2, 768, 768], P(None, ('batch', 'seq'))
- grad_b_value: float32 [2, 768], P(None, ('batch', 'seq'))
- grad_w_out: float32 [2, 768, 768], P(None, ('batch', 'seq'))
- grad_b_out: float32 [2, 768], P(None, ('batch', 'seq'))
- grad_gain_one: float32 [2, 768], P(None, ('batch', 'seq'))
- grad_shift_one: float32 [2, 768], P(None, ('batch', 'seq'))
- grad_w_up: float32 [2, 768, 3072], P(None, ('batch', 'seq'))
- grad_b_up: float32 [2, 3072], P(None, ('batch', 'seq'))
- grad_w_down: float32 [2, 3072, 768], P(None, ('batch', 'seq'))
- grad_b_down: float32 [2, 768], P(None, ('batch', 'seq'))
- grad_gain_two: float32 [2, 768], P(None, ('batch', 'seq'))
- grad_shift_two: float32 [2, 768], P(None, ('batch', 'seq'))
The draws below stay inside these ranges and needn't reach their ends.
Inputs may be any that keep to these rules, and one draw needn't show every extreme that they name: `lengths`: among the 3 consecutive sequences of one index of batch, at least one has length 1024; every length exceeds 512.
All inputs are finite; a program needn't handle non-finite values.
Results may differ from the reference program's by a relative error of at most 0.029.
Values may be sent and summed in bfloat16 or wider, within the bound.
No kernel may reach another device: no remote copies, remote signals or barrier semaphores. Data moves between devices by JAX's collectives and lax.ppermute only.
A program may use at most 320 MiB of HBM per device.

```python
import jax
import jax.numpy as jnp
from jax import lax

D = 768
HEADS = 12
HEAD_DIM = 64
FF = 3072
BLOCK = 512
LAYERS = 2
SEQ_PER = 3
SEQS = 24
SEQ_LEN = 1024


def draw_lengths(key, part):
    key = jax.random.fold_in(key, 11)
    first_key, second_key, third_key = jax.random.split(key, 3)
    first_draw = jax.random.randint(first_key, (SEQS,), 0, BLOCK)
    second_draw = jax.random.randint(second_key, (SEQS,), 0, BLOCK)
    extra = first_draw * second_draw // (BLOCK - 1)
    ragged = BLOCK + 1 + extra
    groups = SEQS // SEQ_PER
    chosen = jax.random.randint(third_key, (groups,), 0, SEQ_PER)
    chosen_each = jnp.repeat(chosen, SEQ_PER)
    within = jnp.arange(SEQS, dtype=jnp.int32) % SEQ_PER
    return jnp.where(within == chosen_each, 2 * BLOCK, ragged).astype(jnp.int32)


def strengthened(values, stream_key, source, target, blocks, factor):
    def block_of(position):
        return (jnp.arange(values.shape[position]) // (values.shape[position] // blocks)).reshape((-1,) + (1,) * (values.ndim - 1 - position))

    one_side = jax.random.permutation(stream_key, blocks)[block_of(target)]
    second = (block_of(target) + blocks // 2) % blocks
    return jnp.where((block_of(source) == one_side) | (block_of(source) == second), factor * values, values)


def block_levels(own_key, dims, cuts, low, top_value):
    loudness = 1.0
    for dim, parts in cuts:
        draws = jax.random.uniform(jax.random.fold_in(jax.random.fold_in(own_key, 6), dim), (parts,), jnp.float32, low / len(cuts), top_value / len(cuts))
        loudness = loudness * jnp.repeat(jnp.exp(draws), dims[dim] // parts).reshape((-1,) + (1,) * (len(dims) - 1 - dim))
    return loudness


def noise(stream_key, extent, deviation, bound, cuts=(), held_as=jnp.bfloat16):
    drawn = deviation * jax.random.normal(stream_key, extent, jnp.float32)
    if cuts:
        drawn = drawn * block_levels(stream_key, extent, cuts, -0.22, 0.18)
    return jnp.clip(drawn, -bound, bound).astype(held_as)


def gaussian_with(own_key, extent, spread, reach, cuts, heavy, kind=jnp.bfloat16):
    values = spread * jax.random.normal(own_key, extent, jnp.float32)
    if cuts:
        values = values * block_levels(own_key, extent, cuts, -0.22, 0.18)
    return jnp.clip(strengthened(values, jax.random.fold_in(own_key, 3), *heavy), -reach, reach).astype(kind)


def setup_inputs(seed: int = 0) -> dict:
    splits = jax.random.split(jax.random.key(seed), 19)
    return {
        "tokens": gaussian_with(splits[0], (SEQS, SEQ_LEN, D), 1.0, 6.0, ((0, 8), (1, 4)), (0, 2, 8, 2.0)),
        "lengths": draw_lengths(jax.random.fold_in(splits[18], 71), 0),
        "w_query": noise(splits[2], (LAYERS, D, D), D ** -0.5, 0.21875),
        "b_query": noise(splits[3], (LAYERS, D), 0.5, 3.0),
        "w_key": noise(splits[4], (LAYERS, D, D), D ** -0.5, 0.21875),
        "w_value": noise(splits[5], (LAYERS, D, D), D ** -0.5, 0.21875),
        "b_value": noise(splits[6], (LAYERS, D), 0.5, 3.0),
        "w_out": noise(splits[7], (LAYERS, D, D), (max(1, D // 128)) ** -0.5, 2.5),
        "b_out": noise(splits[8], (LAYERS, D), 0.5, 3.0),
        "gain_one": jnp.clip(1.0 + 0.15 * jax.random.normal(splits[9], (LAYERS, D), jnp.float32), 0.25, 1.75).astype(jnp.bfloat16),
        "shift_one": noise(splits[10], (LAYERS, D), 0.3, 2.0),
        "w_up": noise(splits[11], (LAYERS, D, FF), D ** -0.5, 0.21875),
        "b_up": noise(splits[12], (LAYERS, FF), 0.5, 3.0),
        "w_down": noise(splits[13], (LAYERS, FF, D), FF ** -0.5, 0.109375),
        "b_down": noise(splits[14], (LAYERS, D), 0.5, 3.0),
        "gain_two": jnp.clip(1.0 + 0.15 * jax.random.normal(splits[15], (LAYERS, D), jnp.float32), 0.25, 1.75).astype(jnp.bfloat16),
        "shift_two": noise(splits[16], (LAYERS, D), 0.3, 2.0),
        "cotangent": noise(splits[17], (SEQS, SEQ_LEN, D), 1.0, 6.0, ((0, 8), (1, 4))),
    }


EPSILON = 1e-06
MASKED = -1e+30
HIGHEST = lax.Precision.HIGHEST

@jax.custom_vjp
def low(v):
    return lax.optimization_barrier(v.astype(jnp.bfloat16)).astype(jnp.float32)

@jax.custom_vjp
def low_back(v):
    return v

def low_keep(v):
    return (low(v), None)

def low_pass(kept, grad):
    return (grad,)

def back_keep(v):
    return (v, None)

def back_low(kept, grad):
    return (low(grad),)
low.defvjp(low_keep, low_pass)
low_back.defvjp(back_keep, back_low)

def layer_norm(value, gain, shift):
    average = lax.optimization_barrier(jnp.mean(value, axis=-1, keepdims=True))
    centred = value - average
    inverse_scale = lax.rsqrt(lax.optimization_barrier(jnp.mean(centred * centred, axis=-1, keepdims=True)) + EPSILON)
    return centred * inverse_scale * gain + shift

def project(value, weight):
    return jnp.dot(value, weight, precision=HIGHEST, preferred_element_type=jnp.float32)

def one_layer(layer_in, params, key_valid, swapped):
    w_query, b_query, w_key, w_value, b_value, w_out, b_out, gain_one, shift_one, w_up, b_up, w_down, b_down, gain_two, shift_two = params
    rounded = low(layer_in)
    queries = low(low_back(project(rounded, w_query) + b_query))
    key_rows = low(low_back(project(rounded, w_key)))
    values = low(low_back(project(rounded, w_value) + b_value))
    head_shape = (2, BLOCK, HEADS, HEAD_DIM)
    query_heads = queries.reshape(head_shape)
    key_heads = key_rows.reshape(head_shape)
    value_heads = values.reshape(head_shape)
    block_valid = key_valid.reshape(2, BLOCK)
    if swapped:
        key_heads = key_heads[::-1]
        value_heads = value_heads[::-1]
        block_valid = block_valid[::-1]
    scores = jnp.einsum('bqhd,bkhd->bhqk', query_heads, key_heads, precision=HIGHEST) * HEAD_DIM ** (-0.5)
    scores = low_back(scores)
    scores = jnp.where(block_valid[:, None, None, :], scores, MASKED)
    row_top = lax.optimization_barrier(jnp.max(scores, axis=-1, keepdims=True))
    exponent = jnp.exp(scores - row_top)
    attention = low(exponent / lax.optimization_barrier(jnp.sum(exponent, axis=-1, keepdims=True)))
    context = jnp.einsum('bhqk,bkhd->bqhd', attention, value_heads, precision=HIGHEST).reshape(SEQ_LEN, D)
    context = low(low_back(context))
    branch = low_back(project(context, w_out) + b_out)
    hidden = layer_norm(branch + layer_in, gain_one, shift_one)
    hidden_low = low(hidden)
    pre_act = low_back(project(hidden_low, w_up) + b_up)
    act_low = low(jax.nn.gelu(pre_act, approximate=False))
    second = low_back(project(act_low, w_down) + b_down)
    return layer_norm(second + hidden, gain_two, shift_two)

def run_sequence(params, sequence, length):
    key_valid = jnp.arange(SEQ_LEN) < length
    current = sequence
    for layer_index in range(LAYERS):
        current = one_layer(current, tuple((tensor[layer_index] for tensor in params)), key_valid, layer_index % 2 == 1)
    return current

def reference(tokens, lengths, w_query, b_query, w_key, w_value, b_value, w_out, b_out, gain_one, shift_one, w_up, b_up, w_down, b_down, gain_two, shift_two, cotangent):
    params = tuple((tensor.astype(jnp.float32) for tensor in (w_query, b_query, w_key, w_value, b_value, w_out, b_out, gain_one, shift_one, w_up, b_up, w_down, b_down, gain_two, shift_two)))
    checked = jax.checkpoint(run_sequence)

    def forward(weights, inputs):
        return lax.map(lambda element: checked(weights, element[0], element[1]), (inputs, lengths))
    result, pullback = jax.vjp(forward, params, tokens.astype(jnp.float32))
    grad_params, grad_tokens = pullback(cotangent.astype(jnp.float32))
    return (result.astype(jnp.bfloat16), grad_tokens, grad_params[0], grad_params[1], grad_params[2], grad_params[3], grad_params[4], grad_params[5], grad_params[6], grad_params[7], grad_params[8], grad_params[9], grad_params[10], grad_params[11], grad_params[12], grad_params[13], grad_params[14])
```

```python
from functools import partial

import jax
import jax.numpy as jnp
from jax import lax
from jax.sharding import PartitionSpec as P

HEADS = 12
HEAD_DIM = 64


EPSILON = 1e-06
MASKED = -1e30


def swapped_2(value, axis, bit):
    return lax.ppermute(value, axis, [(i, i ^ 1 << bit) for i in range(lax.axis_size(axis))])


def layer_norm(value, gain, shift):
    average = jnp.mean(value, axis=-1, keepdims=True)
    centred = value - average
    inverse_scale = lax.rsqrt(jnp.mean(centred * centred, axis=-1, keepdims=True) + EPSILON)
    normed = centred * inverse_scale
    return (normed * gain.astype(jnp.float32) + shift.astype(jnp.float32), normed, inverse_scale)


def norm_back(grad_out, normed, inverse_scale, gain):
    grad_normed = grad_out * gain.astype(jnp.float32)
    grad_value = inverse_scale * (
        grad_normed
        - jnp.mean(grad_normed, axis=-1, keepdims=True)
        - normed * jnp.mean(grad_normed * normed, axis=-1, keepdims=True)
    )
    return (grad_value, jnp.sum(grad_out * normed, axis=(0, 1)), jnp.sum(grad_out, axis=(0, 1)))


def project(value, weight):
    return jnp.einsum("std,de->ste", value, weight, preferred_element_type=jnp.float32)


def project_back(grad_value, weight):
    return jnp.einsum("ste,de->std", grad_value, weight, preferred_element_type=jnp.float32)


def weight_grad(value, grad_value):
    return jnp.einsum("std,ste->de", value, grad_value, preferred_element_type=jnp.float32)


def token_sum(grad_value):
    return jnp.sum(grad_value, axis=(0, 1), dtype=jnp.float32)


def split_heads(value):
    return value.reshape(value.shape[0], value.shape[1], HEADS, HEAD_DIM)


def join_heads(value):
    return value.reshape(value.shape[0], value.shape[1], HEADS * HEAD_DIM)


def masked_scores(queries, key_rows, key_valid):
    scores = jnp.einsum(
        "sqhd,skhd->shqk",
        split_heads(queries),
        split_heads(key_rows),
        preferred_element_type=jnp.float32,
    ) * HEAD_DIM ** (-0.5)
    return jnp.where(key_valid[:, None, None, :], scores, MASKED)


def pair_swap(key_rows, values):
    return swapped_2((key_rows, values), "seq", 0)


def pair_return(grad_keys, grad_values):
    return (
        swapped_2(grad_keys.astype(jnp.bfloat16), "seq", 0).astype(grad_keys.dtype),
        swapped_2(grad_values.astype(jnp.bfloat16), "seq", 0).astype(grad_values.dtype),
    )


def layer_forward(layer_in, lengths, params, swapped):
    (
        w_query,
        b_query,
        w_key,
        w_value,
        b_value,
        w_out,
        b_out,
        gain_one,
        shift_one,
        w_up,
        b_up,
        w_down,
        b_down,
        gain_two,
        shift_two,
    ) = params
    rounded = layer_in.astype(jnp.bfloat16)
    queries = (project(rounded, w_query) + b_query.astype(jnp.float32)).astype(jnp.bfloat16)
    key_rows = project(rounded, w_key).astype(jnp.bfloat16)
    values = (project(rounded, w_value) + b_value.astype(jnp.float32)).astype(jnp.bfloat16)
    seq_index = lax.axis_index("seq")
    half_rows = key_rows.shape[1]
    if swapped:
        near_keys, near_values = swapped_2((key_rows, values), "seq", 1)
        far_keys, far_values = pair_swap(near_keys, near_values)
        first_start = seq_index ^ 2
        second_start = seq_index ^ 3
    else:
        near_keys, near_values = (key_rows, values)
        far_keys, far_values = pair_swap(key_rows, values)
        first_start = seq_index
        second_start = seq_index ^ 1
    all_keys = jnp.concatenate([near_keys, far_keys], axis=1)
    all_values = jnp.concatenate([near_values, far_values], axis=1)
    offsets = jnp.arange(half_rows, dtype=jnp.int32)
    positions = jnp.concatenate(
        [first_start * half_rows + offsets, second_start * half_rows + offsets]
    )
    key_valid = positions[None, :] < lengths[:, None]
    scores = masked_scores(queries, all_keys, key_valid)
    row_top = jnp.max(scores, axis=-1, keepdims=True)
    exponent = jnp.exp(scores - row_top)
    total = jnp.sum(exponent, axis=-1, keepdims=True)
    attention = (exponent / total).astype(jnp.bfloat16)
    log_total = row_top + jnp.log(total)
    context = join_heads(
        jnp.einsum(
            "shqk,skhd->sqhd",
            attention,
            split_heads(all_values),
            preferred_element_type=jnp.float32,
        )
    ).astype(jnp.bfloat16)
    branch = project(context, w_out) + b_out.astype(jnp.float32)
    hidden, normed_one, scale_one = layer_norm(branch + layer_in, gain_one, shift_one)
    hidden_low = hidden.astype(jnp.bfloat16)
    pre_act = project(hidden_low, w_up) + b_up.astype(jnp.float32)
    act_low = jax.nn.gelu(pre_act, approximate=False).astype(jnp.bfloat16)
    second = project(act_low, w_down) + b_down.astype(jnp.float32) + hidden
    result, normed_two, scale_two = layer_norm(second, gain_two, shift_two)
    kept = (
        rounded,
        queries,
        all_keys,
        all_values,
        key_valid,
        log_total,
        context,
        normed_one,
        scale_one,
        hidden_low,
        pre_act,
        act_low,
        normed_two,
        scale_two,
    )
    return (result, kept)


def layer_backward(grad_output, kept, params, swapped):
    (
        w_query,
        b_query,
        w_key,
        w_value,
        b_value,
        w_out,
        b_out,
        gain_one,
        shift_one,
        w_up,
        b_up,
        w_down,
        b_down,
        gain_two,
        shift_two,
    ) = params
    (
        rounded,
        queries,
        all_keys,
        all_values,
        key_valid,
        log_total,
        context,
        normed_one,
        scale_one,
        hidden_low,
        pre_act,
        act_low,
        normed_two,
        scale_two,
    ) = kept
    grad_second, grad_gain_two, grad_shift_two = norm_back(
        grad_output, normed_two, scale_two, gain_two
    )
    grad_down_out = grad_second.astype(jnp.bfloat16)
    grad_b_down = token_sum(grad_down_out)
    grad_w_down = weight_grad(act_low, grad_down_out)
    grad_act = project_back(grad_down_out, w_down)
    gelu_pull = jax.vjp(partial(jax.nn.gelu, approximate=False), pre_act)[1]
    grad_pre = gelu_pull(grad_act)[0].astype(jnp.bfloat16)
    grad_b_up = token_sum(grad_pre)
    grad_w_up = weight_grad(hidden_low, grad_pre)
    grad_hidden = grad_second + project_back(grad_pre, w_up)
    grad_first, grad_gain_one, grad_shift_one = norm_back(
        grad_hidden, normed_one, scale_one, gain_one
    )
    grad_branch = grad_first.astype(jnp.bfloat16)
    grad_b_out = token_sum(grad_branch)
    grad_w_out = weight_grad(context, grad_branch)
    grad_context = project_back(grad_branch, w_out).astype(jnp.bfloat16)
    scores = masked_scores(queries, all_keys, key_valid)
    attention = jnp.exp(scores - log_total)
    grad_attention = jnp.einsum(
        "sqhd,skhd->shqk",
        split_heads(grad_context),
        split_heads(all_values),
        preferred_element_type=jnp.float32,
    )
    inner = jnp.sum(attention * grad_attention, axis=-1, keepdims=True)
    grad_scores = (attention * (grad_attention - inner)).astype(jnp.bfloat16)
    scale_factor = HEAD_DIM ** (-0.5)
    grad_queries = (
        join_heads(
            jnp.einsum(
                "shqk,skhd->sqhd",
                grad_scores,
                split_heads(all_keys),
                preferred_element_type=jnp.float32,
            )
        )
        * scale_factor
    ).astype(jnp.bfloat16)
    grad_keys = (
        join_heads(
            jnp.einsum(
                "shqk,sqhd->skhd",
                grad_scores,
                split_heads(queries),
                preferred_element_type=jnp.float32,
            )
        )
        * scale_factor
    )
    grad_values = join_heads(
        jnp.einsum(
            "shqk,sqhd->skhd",
            attention.astype(jnp.bfloat16),
            split_heads(grad_context),
            preferred_element_type=jnp.float32,
        )
    )
    half_rows = queries.shape[1]
    returned_keys, returned_values = pair_return(
        grad_keys[:, half_rows:], grad_values[:, half_rows:]
    )
    near_keys = grad_keys[:, :half_rows] + returned_keys
    near_values = grad_values[:, :half_rows] + returned_values
    if swapped:
        home_keys, home_values = (
            swapped_2(near_keys.astype(jnp.bfloat16), "seq", 1).astype(near_keys.dtype),
            swapped_2(near_values.astype(jnp.bfloat16), "seq", 1).astype(near_values.dtype),
        )
    else:
        home_keys, home_values = (near_keys, near_values)
    grad_key_low = home_keys.astype(jnp.bfloat16)
    grad_value_low = home_values.astype(jnp.bfloat16)
    grad_b_query = token_sum(grad_queries)
    grad_w_query = weight_grad(rounded, grad_queries)
    grad_w_key = weight_grad(rounded, grad_key_low)
    grad_b_value = token_sum(grad_value_low)
    grad_w_value = weight_grad(rounded, grad_value_low)
    grad_in = (
        grad_first
        + project_back(grad_queries, w_query)
        + project_back(grad_key_low, w_key)
        + project_back(grad_value_low, w_value)
    )
    grads = (
        grad_w_query,
        grad_b_query,
        grad_w_key,
        grad_w_value,
        grad_b_value,
        grad_w_out,
        grad_b_out,
        grad_gain_one,
        grad_shift_one,
        grad_w_up,
        grad_b_up,
        grad_w_down,
        grad_b_down,
        grad_gain_two,
        grad_shift_two,
    )
    return (grad_in, grads)


def local(
    tokens,
    lengths,
    w_query,
    b_query,
    w_key,
    w_value,
    b_value,
    w_out,
    b_out,
    gain_one,
    shift_one,
    w_up,
    b_up,
    w_down,
    b_down,
    gain_two,
    shift_two,
    cotangent,
):
    stacked = (
        w_query,
        b_query,
        w_key,
        w_value,
        b_value,
        w_out,
        b_out,
        gain_one,
        shift_one,
        w_up,
        b_up,
        w_down,
        b_down,
        gain_two,
        shift_two,
    )

    def pick(depth):
        return tuple((tensor[depth] for tensor in stacked))

    first_out, first_kept = layer_forward(tokens.astype(jnp.float32), lengths, pick(0), False)
    final, second_kept = layer_forward(first_out, lengths, pick(1), True)
    grad_middle, grads_two = layer_backward(
        cotangent.astype(jnp.float32), second_kept, pick(1), True
    )
    grad_in, grads_one = layer_backward(grad_middle, first_kept, pick(0), False)
    outs = reduce_grads(grads_one, grads_two)
    return (final.astype(jnp.bfloat16), grad_in) + outs


MATRICES = (0, 2, 3, 5)
VECTORS = (1, 4, 6, 7, 8, 12, 13, 14, 10)


def digit_bits():
    low = lax.axis_size("seq").bit_length() - 1
    high = lax.axis_size("batch").bit_length() - 1
    return [("seq", bit) for bit in range(low)] + [("batch", bit) for bit in range(high)]


def digit_orders():
    digits = digit_bits()
    core, across, rest = digits[0], digits[1], digits[2:]
    if len(rest) < 2:
        return [[core, across] + rest]
    near, far, late = rest[0], rest[1], rest[2:]
    return [
        [core, across, near, far] + late,
        [core, near, far, across] + late,
        [core, far, across, near] + late,
    ]


def shard_sum(value, order):
    digits = digit_bits()
    left = list(reversed(digits))
    groups, _, rows, columns = value.shape
    value = value.reshape((groups,) + (2,) * len(left) + (rows, columns))
    wide = jnp.float32
    for step, (axis, bit) in enumerate(order):
        place = 1 + left.index((axis, bit))
        left.remove((axis, bit))
        mine = lax.axis_index(axis) >> bit & 1
        sent = lax.dynamic_index_in_dim(value, 1 - mine, place, keepdims=False)
        kept = lax.dynamic_index_in_dim(value, mine, place, keepdims=False)
        got = swapped_2(sent, axis, bit)
        value = kept.astype(wide) + got.astype(wide)
        if step < len(order) - 1:
            value = value.astype(got.dtype)
    return value


def matrix_sum(value):
    orders = digit_orders()
    width = value.shape[-1] // len(orders)
    parts = [
        shard_sum(value[..., which * width : (which + 1) * width], order)
        for which, order in enumerate(orders)
    ]
    return jnp.concatenate(parts, axis=-1)


def reduce_grads(*layers):
    devices = lax.axis_size("batch") * lax.axis_size("seq")
    sums = []
    for grads in reversed(layers):
        low = [grad.astype(jnp.bfloat16) for grad in grads]
        down = matrix_sum(low[11].reshape(1, devices, -1, low[11].shape[1]))[0]
        up = matrix_sum(low[9].reshape(1, devices, -1, low[9].shape[1]))[0]
        four = jnp.stack([low[which] for which in MATRICES])
        four = matrix_sum(four.reshape(4, devices, -1, four.shape[2]))
        sums.append((down, up, four))
    sums.reverse()
    vectors = jnp.concatenate(
        [grads[which].reshape(devices, -1) for grads in layers for which in VECTORS], axis=1
    )
    vectors = jnp.pad(vectors, ((0, 0), (0, -vectors.shape[1] % 1024)))
    vectors = shard_sum(vectors.reshape(1, devices, 8, -1), digit_orders()[0]).reshape(-1)
    outs = [None] * 15
    for place, which in enumerate(MATRICES):
        outs[which] = jnp.stack([one[2][place] for one in sums])
    outs[9] = jnp.stack([one[1] for one in sums])
    outs[11] = jnp.stack([one[0] for one in sums])
    start = 0
    pieces = {}
    for depth, grads in enumerate(layers):
        for which in VECTORS:
            width = grads[which].shape[0] // devices
            pieces[depth, which] = vectors[start : start + width]
            start += width
    for which in VECTORS:
        outs[which] = jnp.stack([pieces[depth, which] for depth in range(len(layers))])
    return tuple(outs)


def solution(mesh):
    in_specs = (
        P("batch", "seq", None),
        P("batch"),
        P(),
        P(),
        P(),
        P(),
        P(),
        P(),
        P(),
        P(),
        P(),
        P(),
        P(),
        P(),
        P(),
        P(),
        P(),
        P("batch", "seq", None),
    )
    out_specs = (
        P("batch", "seq", None),
        P("batch", "seq", None),
        P(None, ("batch", "seq"), None),
        P(None, ("batch", "seq")),
        P(None, ("batch", "seq"), None),
        P(None, ("batch", "seq"), None),
        P(None, ("batch", "seq")),
        P(None, ("batch", "seq"), None),
        P(None, ("batch", "seq")),
        P(None, ("batch", "seq")),
        P(None, ("batch", "seq")),
        P(None, ("batch", "seq"), None),
        P(None, ("batch", "seq")),
        P(None, ("batch", "seq"), None),
        P(None, ("batch", "seq")),
        P(None, ("batch", "seq")),
        P(None, ("batch", "seq")),
    )
    return jax.shard_map(local, mesh=mesh, in_specs=in_specs, out_specs=out_specs, check_vma=False)
```

```python
from functools import partial

import jax
import jax.numpy as jnp
from jax import lax
from jax.experimental import pallas as pl
from jax.experimental.pallas import tpu as pltpu
from jax.sharding import PartitionSpec as P

HEADS = 12
HEAD_DIM = 64


EPSILON = 1e-06
MASKED = -1e30


def swapped_2(value, axis, bit):
    return lax.ppermute(value, axis, [(i, i ^ 1 << bit) for i in range(lax.axis_size(axis))])


TOKENS_MINOR = (((1,), (1,)), ((), ()))
TOKENS_MAJOR = (((0,), (0,)), ((), ()))
ROOT_HALF = 0.7071067811865476
ROOT_TAU = 0.3989422804014327
VMEM_BYTES = 56 * 1024 * 1024
FF_PARTS = 4
FAST = jnp.float32
LOW = jnp.bfloat16


COST_SCALE = 10


def cost(microseconds):
    return pl.CostEstimate(flops=int(microseconds * COST_SCALE * 1.15e9), bytes_accessed=1, transcendentals=0)


def mm(left, right):
    return jnp.dot(left, right, preferred_element_type=FAST)


def mm_nt(left, right):
    return lax.dot_general(left, right, TOKENS_MINOR, preferred_element_type=FAST)


def mm_tn(left, right):
    return lax.dot_general(left, right, TOKENS_MAJOR, preferred_element_type=FAST)


def row_norm(value):
    average = jnp.mean(value, axis=-1, keepdims=True)
    centred = value - average
    inverse_scale = lax.rsqrt(jnp.mean(centred * centred, axis=-1, keepdims=True) + EPSILON)
    return centred * inverse_scale, inverse_scale


def gelu_and_slope(value):
    size = jnp.abs(value)
    near = 1.0 / (1.0 + (0.3275911 * ROOT_HALF) * size)
    bell = jnp.exp(value * value * -0.5)
    poly = near * (
        0.127414796
        + near * (-0.142248368 + near * (0.7107068705 + near * (-0.7265760135 + near * 0.5307027145)))
    )
    tail = poly * bell
    below = jnp.where(value >= 0, 1.0 - tail, tail)
    return value * below, below + value * (bell * ROOT_TAU)


VEC_ROWS = dict(b_query=0, b_value=1, b_out=2, gain_one=3, shift_one=4, b_down=5, gain_two=6, shift_two=7)
VEC_UP = 8


def forward_kernel(layer, swapped, facts, own, near, far, top, vecs, *refs):
    weights, refs = refs[:6], refs[6:]
    refs = refs[len(refs) - 25 :]
    outs, scratch = refs[:16], refs[16:]
    (
        o_sent, o_extra, o_low, o_q, o_k, o_v, o_lse, o_ctx, o_n1, o_r1, o_hid, o_act, o_slope, o_n2, o_r2, o_done,
    ) = outs
    o_top = o_near = o_extra
    w_q, w_k, w_v, w_o, w_up, w_down, mix, ctx, sems = scratch
    first = pl.program_id(0) == 0
    held = (w_q, w_k, w_v, w_o, w_up, w_down)
    copies = [
        pltpu.make_async_copy(weights[i].at[layer], held[i], sems.at[i]) for i in range(6)
    ]

    @pl.when(first)
    def _():
        for copy in copies:
            copy.start()

    def ready(*which):
        @pl.when(first)
        def _():
            for i in which:
                copies[i].wait()

    def vec(name):
        row = VEC_ROWS[name]
        return vecs[layer, row : row + 1, :]

    rows = own.shape[1]
    x = own[0]
    ready(0, 1, 2)
    queries = (mm(x, w_q[...]) + vec("b_query")).astype(LOW)
    o_q[0] = queries * jnp.asarray(HEAD_DIM**-0.5, LOW)
    for part, source in ((0, near), (1, far)):
        block = source[0]
        o_k[0, part * rows : (part + 1) * rows, :] = mm(block, w_k[...]).astype(LOW)
        o_v[0, part * rows : (part + 1) * rows, :] = (mm(block, w_v[...]) + vec("b_value")).astype(LOW)
    seq = facts[5] + pl.program_id(0)
    length = facts[seq]
    lane = lax.broadcasted_iota(jnp.int32, (1, 2 * rows), 1)
    place = jnp.where(lane < rows, facts[3] + lane, facts[4] + (lane - rows))
    bias = jnp.where(place < length, 0.0, MASKED).astype(FAST)
    lower = lax.broadcasted_iota(jnp.int32, (1, 128), 1) < HEAD_DIM
    column = lax.broadcasted_iota(jnp.int32, (1, 128), 1)
    logs = jnp.zeros((rows, 128), FAST)
    for pair in range(HEADS // 2):
        lanes = slice(pair * 128, pair * 128 + 128)
        q_pair, k_pair, v_pair = o_q[0, :, lanes], o_k[0, :, lanes], o_v[0, :, lanes]
        got = []
        for side in range(2):
            mask = lower if side == 0 else ~lower
            q_one = jnp.where(mask, q_pair, jnp.zeros_like(q_pair))
            scores = mm_nt(q_one, k_pair) + bias
            high = jnp.max(scores, axis=-1, keepdims=True)
            weight = jnp.exp(scores - high)
            total = jnp.sum(weight, axis=-1, keepdims=True)
            got.append(mm(weight.astype(LOW), v_pair) * (1.0 / total))
            logs = jnp.where(column == 2 * pair + side, high + jnp.log(total), logs)
        ctx[:, lanes] = jnp.where(lower, got[0], got[1]).astype(LOW)
    o_lse[0] = logs.T[:16, :]
    o_ctx[0] = ctx[...]
    ready(3)
    branch = mm(ctx[...], w_o[...]) + vec("b_out") + top[0].astype(FAST)
    n1, r1 = row_norm(branch)
    o_n1[0] = n1.astype(LOW)
    o_r1[0] = r1
    hidden = n1 * vec("gain_one") + vec("shift_one")
    hid = hidden.astype(LOW)
    o_hid[0] = hid
    mix[...] = hidden + vec("b_down")
    ready(4, 5)
    width = w_up.shape[1] // FF_PARTS
    for part in range(FF_PARTS):
        cols = slice(part * width, (part + 1) * width)
        pre = mm(hid, w_up[:, cols]) + vecs[layer, VEC_UP + part : VEC_UP + part + 1, :]
        act, slope = gelu_and_slope(pre)
        act = act.astype(LOW)
        o_act[0, :, cols] = act
        o_slope[0, :, cols] = slope.astype(LOW)
        mix[...] += mm(act, w_down[cols, :])
    n2, r2 = row_norm(mix[...])
    o_n2[0] = n2.astype(LOW)
    o_r2[0] = r2
    result = n2 * vec("gain_two") + vec("shift_two")
    if not swapped:
        o_top[0] = result
    low = result.astype(LOW)
    o_sent[0] = low
    if swapped:
        o_near[0] = near[0]
    o_low[0] = low
    o_done[...] = jnp.zeros_like(o_done)


KEPT = ("extra", "low", "q", "k", "v", "lse", "ctx", "n1", "r1", "hid", "act", "slope", "n2", "r2")


def forward_call(layer, swapped, start, count, facts, own, near, far, top, vecs, weights, kept, sizes):
    seqs, rows, wide, hidden = sizes

    def taken(source):
        array, offset = source
        return pl.BlockSpec((1,) + array.shape[1:], lambda i: (start - offset + i, 0, 0))

    shapes = dict(
        extra=((rows, wide), LOW if swapped else FAST), low=((rows, wide), LOW),
        q=((rows, wide), LOW), k=((2 * rows, wide), LOW), v=((2 * rows, wide), LOW), lse=((16, rows), FAST),
        ctx=((rows, wide), LOW), n1=((rows, wide), LOW), r1=((rows, 1), FAST), hid=((rows, wide), LOW),
        act=((rows, hidden), LOW), slope=((rows, hidden), LOW), n2=((rows, wide), LOW), r2=((rows, 1), FAST),
    )
    out_shape = [jax.ShapeDtypeStruct((count, rows, wide), LOW)] + [
        jax.ShapeDtypeStruct((seqs,) + shapes[name][0], shapes[name][1]) for name in KEPT
    ]
    out_specs = [pl.BlockSpec((1, rows, wide), lambda i: (i, 0, 0))] + [
        pl.BlockSpec((1,) + shapes[name][0], lambda i: (start + i, 0, 0)) for name in KEPT
    ]
    out_shape.append(jax.ShapeDtypeStruct((8, 128), FAST))
    out_specs.append(pl.BlockSpec((8, 128), lambda i: (0, 0)))
    any_spec = pl.BlockSpec(memory_space=pl.ANY)
    ins = [facts, own[0], near[0], far[0], top[0], vecs, *weights]
    in_specs = [
        pl.BlockSpec(memory_space=pltpu.SMEM), taken(own), taken(near), taken(far), taken(top),
        pl.BlockSpec(vecs.shape, lambda i: (0, 0, 0)),
    ] + [any_spec] * 6
    aliases = {}
    if kept is not None:
        for place, name in enumerate(KEPT):
            aliases[len(ins) + place] = 1 + place
        ins += [kept[name] for name in KEPT]
        in_specs += [any_spec] * len(KEPT)
    got = pl.pallas_call(
        partial(forward_kernel, layer, swapped),
        grid=(count,),
        in_specs=in_specs,
        out_specs=out_specs,
        out_shape=out_shape,
        input_output_aliases=aliases,
        scratch_shapes=[
            pltpu.VMEM((wide, wide), LOW), pltpu.VMEM((wide, wide), LOW), pltpu.VMEM((wide, wide), LOW),
            pltpu.VMEM((wide, wide), LOW), pltpu.VMEM((wide, hidden), LOW), pltpu.VMEM((hidden, wide), LOW),
            pltpu.VMEM((rows, wide), FAST), pltpu.VMEM((rows, wide), LOW), pltpu.SemaphoreType.DMA((6,)),
        ],
        compiler_params=pltpu.CompilerParams(vmem_limit_bytes=VMEM_BYTES),
        cost_estimate=cost(14 * count),
        name=f"layer_forward_{layer}",
    )(*ins)
    return got[0], dict(zip(KEPT, got[1:-1], strict=True)), got[-1]


def norm_back_rows(grad, normed, inverse_scale, gain):
    dn = grad * gain
    return inverse_scale * (
        dn - jnp.mean(dn, axis=-1, keepdims=True) - normed * jnp.mean(dn * normed, axis=-1, keepdims=True)
    )


def column_sum(value):
    return jnp.sum(value.astype(FAST), axis=0, keepdims=True)


def ff_back_kernel(layer, top_grad, n2, r2, slope, n1, r1, vecs, *refs):
    weights, refs = refs[:3], refs[3:]
    o_dy, o_df, o_dz1, o_da, o_dc, o_vec, w_down, w_up, w_o, mix, sems = refs
    first = pl.program_id(0) == 0
    held = (w_down, w_up, w_o)
    copies = [pltpu.make_async_copy(weights[i].at[layer], held[i], sems.at[i]) for i in range(3)]

    @pl.when(first)
    def _():
        for copy in copies:
            copy.start()
        o_vec[...] = jnp.zeros_like(o_vec)

    def ready(which):
        @pl.when(first)
        def _():
            copies[which].wait()

    def vec(name):
        row = VEC_ROWS[name]
        return vecs[layer, row : row + 1, :]

    def add(row, value):
        o_vec[row : row + 1, :] += value

    grad = top_grad[0].astype(FAST)
    normed = n2[0].astype(FAST)
    add(VEC_ROWS["gain_two"], column_sum(grad * normed))
    add(VEC_ROWS["shift_two"], column_sum(grad))
    dz2 = norm_back_rows(grad, normed, r2[0], vec("gain_two"))
    dy = dz2.astype(LOW)
    o_dy[0] = dy
    add(VEC_ROWS["b_down"], column_sum(dy))
    mix[...] = dz2
    ready(0)
    width = w_up.shape[1] // FF_PARTS
    for part in range(FF_PARTS):
        cols = slice(part * width, (part + 1) * width)
        if part == 0:
            ready(1)
        df = (mm_nt(dy, w_down[cols, :]) * slope[0, :, cols].astype(FAST)).astype(LOW)
        o_df[0, :, cols] = df
        add(VEC_UP + part, column_sum(df))
        mix[...] += mm_nt(df, w_up[:, cols])
    grad = mix[...]
    normed = n1[0].astype(FAST)
    add(VEC_ROWS["gain_one"], column_sum(grad * normed))
    add(VEC_ROWS["shift_one"], column_sum(grad))
    dz1 = norm_back_rows(grad, normed, r1[0], vec("gain_one"))
    o_dz1[0] = dz1
    da = dz1.astype(LOW)
    o_da[0] = da
    add(VEC_ROWS["b_out"], column_sum(da))
    ready(2)
    o_dc[0] = mm_nt(da, w_o[...]).astype(LOW)


def ff_back_call(layer, top_grad, kept, vecs, w_down, w_up, w_out):
    seqs, rows, wide = top_grad.shape
    hidden = w_up.shape[2]
    ins = [top_grad, kept["n2"], kept["r2"], kept["slope"], kept["n1"], kept["r1"], vecs, w_down, w_up, w_out]
    each = lambda shape: pl.BlockSpec((1,) + tuple(shape[1:]), lambda i: (i, 0, 0))
    any_spec = pl.BlockSpec(memory_space=pl.ANY)
    in_specs = [each(x.shape) for x in ins[:6]] + [pl.BlockSpec(vecs.shape, lambda i: (0, 0, 0))] + [any_spec] * 3
    out_shape = [
        jax.ShapeDtypeStruct((seqs, rows, wide), LOW), jax.ShapeDtypeStruct((seqs, rows, hidden), LOW),
        jax.ShapeDtypeStruct((seqs, rows, wide), FAST), jax.ShapeDtypeStruct((seqs, rows, wide), LOW),
        jax.ShapeDtypeStruct((seqs, rows, wide), LOW), jax.ShapeDtypeStruct((vecs.shape[1], wide), FAST),
    ]
    out_specs = [each(x.shape) for x in out_shape[:5]] + [pl.BlockSpec(out_shape[5].shape, lambda i: (0, 0))]
    return pl.pallas_call(
        partial(ff_back_kernel, layer),
        grid=(seqs,),
        in_specs=in_specs,
        out_specs=out_specs,
        out_shape=out_shape,
        scratch_shapes=[
            pltpu.VMEM((hidden, wide), LOW), pltpu.VMEM((wide, hidden), LOW), pltpu.VMEM((wide, wide), LOW),
            pltpu.VMEM((rows, wide), FAST), pltpu.SemaphoreType.DMA((3,)),
        ],
        compiler_params=pltpu.CompilerParams(vmem_limit_bytes=VMEM_BYTES),
        cost_estimate=cost(19),
        name=f"ff_back_{layer}",
    )(*ins)


def attention_back_kernel(split, facts, q, k, v, lse, dc, *refs):
    o_dq, o_near, o_far, o_vec, bias = refs[len(refs) - 5 :]
    rows, wide = q.shape[1], q.shape[2]

    @pl.when(pl.program_id(0) == 0)
    def _():
        o_vec[...] = jnp.zeros_like(o_vec)

    length = facts[facts[5] + pl.program_id(0)]
    key = lax.broadcasted_iota(jnp.int32, (2 * rows, rows), 0)
    place = jnp.where(key < rows, facts[3] + key, facts[4] + (key - rows))
    bias[...] = jnp.where(place < length, 0.0, MASKED).astype(FAST)
    lower = lax.broadcasted_iota(jnp.int32, (1, 128), 1) < HEAD_DIM
    for pair in range(HEADS // 2):
        lanes = slice(pair * 128, pair * 128 + 128)
        q_pair, k_pair, v_pair, dc_pair = q[0, :, lanes], k[0, :, lanes], v[0, :, lanes], dc[0, :, lanes]
        dk = dv = None
        dq = []
        for side in range(2):
            one = 2 * pair + side
            mask = lower if side == 0 else ~lower
            q_one = jnp.where(mask, q_pair, jnp.zeros_like(q_pair))
            dc_one = jnp.where(mask, dc_pair, jnp.zeros_like(dc_pair))
            weight = jnp.exp(mm_nt(k_pair, q_one) + bias[...] - lse[0, one : one + 1, :])
            product = weight * mm_nt(v_pair, dc_one)
            ds = (product - weight * jnp.sum(product, axis=0, keepdims=True)).astype(LOW)
            dv_one = mm(weight.astype(LOW), dc_one)
            dk_one = mm(ds, q_one)
            dv = dv_one if dv is None else dv + dv_one
            dk = dk_one if dk is None else dk + dk_one
            dq.append(mm_tn(ds, k_pair))
        dq_pair = (jnp.where(lower, dq[0], dq[1]) * HEAD_DIM**-0.5).astype(LOW)
        o_dq[0, :, lanes] = dq_pair
        o_vec[0:1, lanes] += column_sum(dq_pair)
        o_near[0, 0, :, lanes] = dk[:rows].astype(LOW)
        o_far[0, 0, :, lanes] = dk[rows:].astype(LOW)
        o_near[0, 1, :, lanes] = dv[:rows].astype(LOW)
        o_far[0, 1, :, lanes] = dv[rows:].astype(LOW)


def blocks(shape, start):
    rest = len(shape) - 1
    return pl.BlockSpec((1,) + tuple(shape[1:]), lambda i: (start + i,) + (0,) * rest)


def chained(ins, in_specs, earlier, places):
    aliases = {}
    if earlier is not None:
        for array, place in zip(earlier, places, strict=True):
            aliases[len(ins)] = place
            ins.append(array)
            in_specs.append(pl.BlockSpec(memory_space=pl.ANY))
    return aliases


def attention_back_call(layer, split, start, count, facts, kept, dc, earlier):
    seqs, rows, wide = dc.shape
    ins = [facts, kept["q"], kept["k"], kept["v"], kept["lse"], dc]
    in_specs = [pl.BlockSpec(memory_space=pltpu.SMEM)] + [blocks(x.shape, start) for x in ins[1:]]
    whole = jax.ShapeDtypeStruct((seqs, rows, wide), LOW)
    both = jax.ShapeDtypeStruct((seqs, 2, rows, wide), LOW)
    single = jax.ShapeDtypeStruct((count, 2, rows, wide), LOW)
    out_shape = [whole, both, single if split else both, jax.ShapeDtypeStruct((8, wide), FAST)]
    out_specs = [
        blocks(whole.shape, start), blocks(both.shape, start), blocks(both.shape, 0 if split else start),
        pl.BlockSpec((8, wide), lambda i: (0, 0)),
    ]
    places = (0, 1) if split else (0, 1, 2)
    aliases = chained(ins, in_specs, earlier and earlier[: len(places)], places)
    return pl.pallas_call(
        partial(attention_back_kernel, split),
        grid=(count,),
        in_specs=in_specs,
        out_specs=out_specs,
        out_shape=out_shape,
        input_output_aliases=aliases,
        scratch_shapes=[pltpu.VMEM((2 * rows, rows), FAST)],
        compiler_params=pltpu.CompilerParams(vmem_limit_bytes=VMEM_BYTES),
        cost_estimate=cost(8 * count),
        name=f"attention_back_{layer}",
    )(*ins)


def input_back_kernel(layer, split, dq, near, *refs):
    got, refs = (refs[0], refs[1:]) if split else (None, refs)
    dz1, *refs = refs
    weights, refs = refs[:3], refs[3:]
    if split:
        o_own, o_pair, o_sent, o_vec, w_q, w_k, w_v, sems = refs[len(refs) - 8 :]
    else:
        o_own, o_vec, w_q, w_k, w_v, sems = refs
    first = pl.program_id(0) == 0
    held = (w_q, w_k, w_v)
    copies = [pltpu.make_async_copy(weights[i].at[layer], held[i], sems.at[i]) for i in range(3)]

    @pl.when(first)
    def _():
        for copy in copies:
            copy.start()
        o_vec[...] = jnp.zeros_like(o_vec)

    if split:
        dk = (near[0, 0].astype(FAST) + got[0, 0].astype(FAST)).astype(LOW)
        dv = (near[0, 1].astype(FAST) + got[0, 1].astype(FAST)).astype(LOW)
        o_pair[0, 0] = dk
        o_pair[0, 1] = dv
    else:
        dk, dv = near[0, 0], near[0, 1]
    o_vec[0:1, :] += column_sum(dv)

    @pl.when(first)
    def _():
        for copy in copies:
            copy.wait()

    far = mm_nt(dk, w_k[...]) + mm_nt(dv, w_v[...])
    here = dz1[0] + mm_nt(dq[0], w_q[...])
    if split:
        o_sent[0] = far.astype(LOW)
        o_own[0] = here
    else:
        o_own[0] = here + far


def input_back_call(layer, split, start, count, dq, near, got, dz1, weights, earlier):
    seqs, rows, wide = dq.shape
    ins = [dq, near]
    in_specs = [blocks(dq.shape, start), blocks(near.shape, start)]
    if split:
        ins.append(got)
        in_specs.append(blocks(got.shape, 0))
    ins += [dz1, *weights]
    in_specs += [blocks(dz1.shape, start)] + [pl.BlockSpec(memory_space=pl.ANY)] * 3
    out_shape = [jax.ShapeDtypeStruct((seqs, rows, wide), FAST)]
    out_specs = [blocks(dz1.shape, start)]
    if split:
        out_shape += [
            jax.ShapeDtypeStruct((seqs, 2, rows, wide), LOW), jax.ShapeDtypeStruct((count, rows, wide), LOW)
        ]
        out_specs += [blocks(out_shape[1].shape, start), blocks(out_shape[2].shape, 0)]
    out_shape.append(jax.ShapeDtypeStruct((8, wide), FAST))
    out_specs.append(pl.BlockSpec((8, wide), lambda i: (0, 0)))
    aliases = chained(ins, in_specs, earlier and earlier[:2], (0, 1))
    return pl.pallas_call(
        partial(input_back_kernel, layer, split),
        grid=(count,),
        in_specs=in_specs,
        out_specs=out_specs,
        out_shape=out_shape,
        input_output_aliases=aliases,
        scratch_shapes=[pltpu.VMEM((wide, wide), LOW)] * 3 + [pltpu.SemaphoreType.DMA((3,))],
        compiler_params=pltpu.CompilerParams(vmem_limit_bytes=VMEM_BYTES),
        cost_estimate=cost(2 + 3 * count),
        name=f"input_back_{layer}",
    )(*ins)


def wgrad_kernel(count, place_ref, *refs):
    lefts, rights, (o_kept, o_sent, full) = refs[:count], refs[count : 2 * count], refs[2 * count :]
    mine = place_ref[0]
    pairs, rows = o_kept.shape[1], o_kept.shape[2]
    for i in range(count):
        full[...] = mm_tn(lefts[i][...], rights[i][...])
        for pair in range(pairs):
            first = pl.multiple_of((2 * pair + mine) * rows, 8)
            second = pl.multiple_of((2 * pair + 1 - mine) * rows, 8)
            o_kept[i, pair] = full[pl.ds(first, rows), :].astype(LOW)
            o_sent[i, pair] = full[pl.ds(second, rows), :].astype(LOW)


def wgrad_call(name, place, devices, lefts, rights, chunk):
    tokens, height = lefts[0].shape
    width = rights[0].shape[1]
    count = len(lefts)
    rows = height // devices
    steps = height // chunk
    shape = jax.ShapeDtypeStruct((count, devices // 2, rows, width), LOW)
    out_spec = pl.BlockSpec((count, devices // 2 // steps, rows, width), lambda i: (0, i, 0, 0))
    return pl.pallas_call(
        partial(wgrad_kernel, count),
        grid=(steps,),
        in_specs=[pl.BlockSpec(memory_space=pltpu.SMEM)]
        + [pl.BlockSpec((tokens, chunk), lambda i: (0, i))] * count
        + [pl.BlockSpec((tokens, width), lambda i: (0, 0))] * count,
        out_specs=[out_spec] * 2,
        out_shape=[shape] * 2,
        scratch_shapes=[pltpu.VMEM((chunk, width), FAST)],
        compiler_params=pltpu.CompilerParams(vmem_limit_bytes=VMEM_BYTES),
        cost_estimate=cost(3 + 2 * count * height * width / 1e6),
        name=f"wgrad_{name}",
    )(place, *lefts, *rights)


def step_kernel(plan, bits, *refs):
    count = len(plan)
    for i, (outer, inner, digit) in enumerate(plan):
        kept, got = refs[2 * i], refs[2 * i + 1]
        o_kept, o_sent = refs[2 * count + 2 * i], refs[2 * count + 2 * i + 1]
        mine = bits[digit]
        for group in range(kept.shape[0]):
            for a in range(outer):
                for out, side in ((o_kept, mine), (o_sent, 1 - mine)):
                    source = pl.ds((2 * a + side) * inner, inner)
                    total = kept[group, source].astype(FAST) + got[group, source].astype(FAST)
                    out[group, a * inner : (a + 1) * inner] = total.astype(LOW)


def step_call(values, gots, plan, bits):
    steps = 1 if any(value.shape[3] % 384 for value in values) else 3
    ins, in_specs, out_specs, out_shape, moved = [], [], [], [], 0
    for value, got in zip(values, gots, strict=True):
        groups, parts, rows, columns = value.shape
        whole = pl.BlockSpec((groups, parts, rows, columns // steps), lambda i: (0, 0, 0, i))
        half = pl.BlockSpec((groups, parts // 2, rows, columns // steps), lambda i: (0, 0, 0, i))
        ins += [value, got]
        in_specs += [whole] * 2
        out_specs += [half] * 2
        out_shape += [jax.ShapeDtypeStruct((groups, parts // 2, rows, columns), LOW)] * 2
        moved += 6 * value.size
    return pl.pallas_call(
        partial(step_kernel, plan),
        grid=(steps,),
        in_specs=[pl.BlockSpec(memory_space=pltpu.SMEM)] + in_specs,
        out_specs=out_specs,
        out_shape=out_shape,
        compiler_params=pltpu.CompilerParams(vmem_limit_bytes=VMEM_BYTES),
        cost_estimate=cost(1 + moved / 3e6),
        name="exchange_step",
    )(bits, *ins)


def local(
    tokens, lengths, w_query, b_query, w_key, w_value, b_value, w_out, b_out, gain_one, shift_one,
    w_up, b_up, w_down, b_down, gain_two, shift_two, cotangent,
):
    seqs, rows, wide = tokens.shape
    hidden = w_up.shape[2]
    sizes = (seqs, rows, wide, hidden)
    weights = (w_query, w_key, w_value, w_out, w_up, w_down)
    vecs = jnp.stack([b_query, b_value, b_out, gain_one, shift_one, b_down, gain_two, shift_two], axis=1)
    vecs = jnp.concatenate([vecs, b_up.reshape(2, FF_PARTS, wide)], axis=1).astype(FAST)
    seq_index = lax.axis_index("seq").astype(jnp.int32)

    def facts_of(first, second, start):
        tail = jnp.stack([first * rows, second * rows, jnp.int32(start)])
        return jnp.concatenate([lengths, tail]).astype(jnp.int32)

    devices = lax.axis_size("batch") * lax.axis_size("seq")
    flat = lambda value: value.reshape(seqs * rows, value.shape[-1])
    cuts = [(0, 2), (2, seqs - 2)]
    other = swapped_2(tokens, "seq", 0)
    kept_one, sent = None, []
    for start, count in cuts:
        facts = facts_of(seq_index, seq_index ^ 1, start)
        low, kept_one, done = forward_call(
            0, False, start, count, facts, (tokens, 0), (tokens, 0), (other, 0), (tokens, 0), vecs, weights, kept_one, sizes
        )
        sent.append((low, start))
    nears = [(swapped_2(low[i : i + 1], "seq", 1), start + i) for low, start in sent for i in range(low.shape[0])]
    kept_two = None
    groups = [[0], list(range(1, seqs))]
    for number, group in enumerate(groups):
        start, count = group[0], len(group)
        arrived = [nears[i][0] for i in group]
        if number:
            arrived = after(arrived, done)
        near = jnp.concatenate(arrived) if count > 1 else arrived[0]
        far = swapped_2(near, "seq", 0)
        facts = facts_of(seq_index ^ 2, seq_index ^ 3, start)
        _, kept_two, done = forward_call(
            1, True, start, count, facts, (kept_one["low"], 0), (near, start), (far, start),
            (kept_one["extra"], 0), vecs, weights, kept_two, sizes,
        )
    final = kept_two["low"]

    back_weights = (w_query, w_key, w_value)
    digits = digit_orders()
    down_order, late_order, four_order, last_orders = digits
    up_order = down_order
    bits = jnp.stack([lax.axis_index(axis) >> bit & 1 for axis, bit in digit_list()]).astype(jnp.int32)
    wgrad = partial(wgrad_call, place=bits, devices=devices)

    kept = kept_two
    dy, df, dz1, da, dc, vec_two = ff_back_call(1, cotangent, kept, vecs, w_down, w_up, w_out)
    down_two = Sum(wgrad("down", lefts=[flat(kept["act"])], rights=[flat(dy)], chunk=wide), down_order, bits)
    facts = [facts_of(seq_index ^ 2, seq_index ^ 3, start) for start, _ in cuts]
    dc = after(dc, down_two.out)
    att = attention_back_call(1, True, 0, 2, facts[0], kept, dc, None)
    att = join(att, down_two)
    vec_q = att[3]
    advance(down_two)
    got = swapped_2(att[2], "seq", 0)
    dc = after(dc, down_two.out, att[2])
    att = attention_back_call(1, True, 2, seqs - 2, facts[1], kept, dc, att)
    vec_q += att[3]
    att, got = after((att, got))
    got_late = swapped_2(att[2], "seq", 0)
    ends = input_back_call(1, True, 0, 2, att[0], att[1], got, dz1, back_weights, None)
    vec_v = ends[3]
    ends, got_late, df = after((ends, got_late, df))
    arrived = [swapped_2(ends[2], "seq", 1)]
    up_two = Sum(wgrad("up", lefts=[flat(kept["hid"])], rights=[flat(df)], chunk=wide // 2), up_order, bits)
    got_late, ends = after((got_late, ends), up_two.out)
    ends = input_back_call(1, True, 2, seqs - 2, att[0], att[1], got_late, dz1, back_weights, ends)
    vec_v += ends[3]
    ends, da = after((ends, da))
    arrived.append(swapped_2(ends[2], "seq", 1))
    rest_two = wgrad("rest", lefts=[flat(kept["ctx"]), flat(kept_one["low"])], rights=[flat(da), flat(att[0])], chunk=wide // 2)
    rest_two, pair = join((rest_two, ends[1]), up_two, down_two)
    rest_two = Sum(rest_two, four_order, bits)
    advance(up_two, down_two)
    pair = after(pair, up_two.out, down_two.out, rest_two.out)
    pairs_two = wgrad("pair", lefts=[flat(kept["extra"])] * 2, rights=[flat(pair[:, 0]), flat(pair[:, 1])], chunk=wide // 2)
    pairs_two, arrived = join((pairs_two, arrived), rest_two)
    pairs_two = Sum(pairs_two, four_order, bits)
    vec_two = (vec_two, vec_q, vec_v)
    advance(rest_two)
    arrived = after(arrived, pairs_two.out, rest_two.out)
    middle = ends[0] + jnp.concatenate(arrived).astype(FAST)

    kept = kept_one
    ff = ff_back_call(0, middle, kept, vecs, w_down, w_up, w_out)
    ff = join(ff, down_two, pairs_two, rest_two)
    dy, df, dz1, da, dc, vec_one = ff
    advance(down_two, pairs_two, rest_two)
    dy = after(dy, down_two.out, pairs_two.out, rest_two.out)
    down_one = wgrad("down", lefts=[flat(kept["act"])], rights=[flat(dy)], chunk=wide)
    down_one, df = join((down_one, df), up_two, down_two)
    down_one = Sum(down_one, down_order, bits)
    advance(up_two, down_two)
    df = after(df, down_one.out, up_two.out, down_two.out)
    up_one = wgrad("up", lefts=[flat(kept["hid"])], rights=[flat(df)], chunk=wide // 2)
    up_one, dc = join((up_one, dc), down_one, down_two)
    up_one = Sum(up_one, late_order, bits)
    advance(down_one)
    facts = [facts_of(seq_index, seq_index ^ 1, start) for start, _ in cuts]
    dc = after(dc, up_one.out, down_one.out)
    att = attention_back_call(0, False, 0, 2, facts[0], kept, dc, None)
    vec_q = att[3]
    att, dc = join((att, dc), up_one, up_two, pairs_two, rest_two)
    advance(up_one, up_two, pairs_two, rest_two)
    dc = after(dc, up_one.out, up_two.out, pairs_two.out, rest_two.out)
    att = attention_back_call(0, False, 2, seqs - 2, facts[1], kept, dc, att)
    vec_q += att[3]
    att, da = join((att, da), down_one, up_two, pairs_two, rest_two)
    advance(down_one, up_two, pairs_two, rest_two)
    got = swapped_2(att[2], "seq", 0)
    da = after(da, att[2], down_one.out)
    rest_one = wgrad("rest", lefts=[flat(kept["ctx"]), flat(tokens)], rights=[flat(da), flat(att[0])], chunk=wide // 2)
    rest_one, got, dz1 = after((rest_one, got, dz1))
    rest_one = Sum(rest_one, four_order, bits)
    pair = (att[1].astype(FAST) + got.astype(FAST)).astype(LOW)
    pair = after(pair, rest_one.out)
    pairs_one = wgrad("pair", lefts=[flat(tokens)] * 2, rights=[flat(pair[:, 0]), flat(pair[:, 1])], chunk=wide // 2)
    pairs_one, dz1 = join((pairs_one, dz1), rest_one, up_one)
    pairs_one = Sum(pairs_one, last_orders[0], bits)
    advance(rest_one, up_one)
    dz1 = after(dz1, pairs_one.out, rest_one.out, up_one.out)
    ends = input_back_call(0, False, 0, seqs, att[0], pair, None, dz1, back_weights, None)
    ends, vec_q = join((ends, vec_q), pairs_one, down_one)
    vec_one = (vec_one, vec_q, ends[1])
    pieces = pairs_one.split(last_orders)
    advance(down_one)
    vectors = both_sums([vec_one, vec_two])
    live = pieces + [rest_one, down_one, up_one, pairs_two, rest_two, down_two, up_two]
    while any(one.got is not None for one in live):
        advance(*live)
    pairs_one = jnp.concatenate([one.value for one in pieces], axis=-1)
    sums = [
        (down_one.value[0], up_one.value[0], rest_one.value, pairs_one),
        (down_two.value[0], up_two.value[0], rest_two.value, pairs_two.value),
    ]
    return (final, ends[0]) + gathered(sums, vectors, devices)


def after(value, *others):
    return lax.optimization_barrier((value, others))[0]


def digit_list():
    return [
        (axis, bit) for axis in ("seq", "batch") for bit in range(lax.axis_size(axis).bit_length() - 1)
    ]


def digit_orders():
    low = lax.axis_size("seq").bit_length() - 1
    high = lax.axis_size("batch").bit_length() - 1
    core, across = ("seq", 0), [("seq", bit) for bit in range(1, low)]
    near, far, late = [("batch", 0)], [("batch", 1)], [("batch", bit) for bit in range(2, high)]
    first = [core] + near + far + across + late
    second = [core] + far + near + across + late
    third = [core] + across + near + far + late
    return first, second, third, (third, [core] + near + far + across + late, [core] + far + across + near + late)


def join(values, *sums):
    live = [one for one in sums if one.got is not None]
    values, gots = lax.optimization_barrier((values, [one.got for one in live]))
    for one, got in zip(live, gots, strict=True):
        one.got = got
    return values


def advance(*sums):
    live = [one for one in sums if one.got is not None]
    if not live:
        return
    for one in live:
        if not one.order:
            one.value = (one.value.astype(FAST) + one.got.astype(FAST))[:, 0]
            one.got = None
    live = [one for one in live if one.got is not None]
    if not live:
        return
    plan, routes = [], []
    for one in live:
        axis, bit = digit = one.order.pop(0)
        above = one.digits.index(digit)
        one.digits.remove(digit)
        plan.append((1 << above, 1 << len(one.digits) - above, digit_list().index(digit)))
        routes.append((axis, bit))
    halves = step_call([one.value for one in live], [one.got for one in live], tuple(plan), live[0].bits)
    for i, one in enumerate(live):
        one.value, one.out = halves[2 * i], halves[2 * i + 1]
        one.got = swapped_2(one.out, *routes[i])


class Sum:
    def __init__(self, halves, order, bits):
        self.value, self.out = halves
        self.bits = bits
        self.digits = list(reversed(digit_list()))[:-1]
        self.order = list(order[1:])
        self.got = swapped_2(self.out, *order[0])

    def split(self, orders):
        value = (self.value.astype(FAST) + self.got.astype(FAST)).astype(LOW)
        pieces = []
        width = value.shape[-1] // len(orders)
        for i, order in enumerate(orders):
            axis, bit = digit = order[1]
            place = 1 + self.digits.index(digit)
            piece = object.__new__(Sum)
            piece.bits = self.bits
            piece.digits, piece.order = [one for one in self.digits if one != digit], list(order[2:])
            part = value[..., i * width : (i + 1) * width]
            part = part.reshape(part.shape[:1] + (2,) * len(self.digits) + part.shape[2:])
            shape = (part.shape[0], -1) + part.shape[-2:]
            mine = lax.axis_index(axis) >> bit & 1
            piece.out = lax.dynamic_index_in_dim(part, 1 - mine, place, keepdims=False).reshape(shape)
            piece.value = lax.dynamic_index_in_dim(part, mine, place, keepdims=False).reshape(shape)
            piece.got = swapped_2(piece.out, axis, bit)
            pieces.append(piece)
        return pieces


def both_sums(layers):
    value = []
    for vec, vec_q, vec_v in layers:
        value.append(jnp.concatenate([vec_q[:1], vec_v[:1], vec[2:]]))
    value = jnp.stack(value)
    for axis in ("seq", "batch"):
        for bit in range(lax.axis_size(axis).bit_length() - 1):
            value = value + swapped_2(value, axis, bit)
    return value


VECTORS = (1, 4, 6, 7, 8, 12, 13, 14)


def gathered(sums, vectors, devices):
    outs = [None] * 15
    outs[0] = jnp.stack([one[2][1] for one in sums])
    outs[2] = jnp.stack([one[3][0] for one in sums])
    outs[3] = jnp.stack([one[3][1] for one in sums])
    outs[5] = jnp.stack([one[2][0] for one in sums])
    outs[9] = jnp.stack([one[1] for one in sums])
    outs[11] = jnp.stack([one[0] for one in sums])
    mine = lax.axis_index("batch") * lax.axis_size("seq") + lax.axis_index("seq")
    width = vectors.shape[2] // devices
    small = lax.dynamic_slice_in_dim(vectors[:, :8], mine * width, width, axis=2)
    for place, which in enumerate(VECTORS):
        outs[which] = small[:, place]
    large = vectors[:, 8:].reshape(vectors.shape[0], -1)
    width = large.shape[1] // devices
    outs[10] = lax.dynamic_slice_in_dim(large, mine * width, width, axis=1)
    return tuple(outs)


def solution(mesh):
    in_specs = (
        P("batch", "seq", None),
        P("batch"),
        P(),
        P(),
        P(),
        P(),
        P(),
        P(),
        P(),
        P(),
        P(),
        P(),
        P(),
        P(),
        P(),
        P(),
        P(),
        P("batch", "seq", None),
    )
    out_specs = (
        P("batch", "seq", None),
        P("batch", "seq", None),
        P(None, ("batch", "seq"), None),
        P(None, ("batch", "seq")),
        P(None, ("batch", "seq"), None),
        P(None, ("batch", "seq"), None),
        P(None, ("batch", "seq")),
        P(None, ("batch", "seq"), None),
        P(None, ("batch", "seq")),
        P(None, ("batch", "seq")),
        P(None, ("batch", "seq")),
        P(None, ("batch", "seq"), None),
        P(None, ("batch", "seq")),
        P(None, ("batch", "seq"), None),
        P(None, ("batch", "seq")),
        P(None, ("batch", "seq")),
        P(None, ("batch", "seq")),
    )
    return jax.shard_map(local, mesh=mesh, in_specs=in_specs, out_specs=out_specs, check_vma=False)
```

```python
from functools import partial

import jax
import jax.numpy as jnp
from jax import lax
from jax.experimental import pallas as pl
from jax.experimental.pallas import tpu as pltpu
from jax.sharding import PartitionSpec as P

HEADS = 12
HEAD_DIM = 64


EPSILON = 1e-06
MASKED = -1e30


def swapped_2(value, axis, bit):
    return lax.ppermute(value, axis, [(i, i ^ 1 << bit) for i in range(lax.axis_size(axis))])


TOKENS_MINOR = (((1,), (1,)), ((), ()))
TOKENS_MAJOR = (((0,), (0,)), ((), ()))
ROOT_HALF = 0.7071067811865476
ROOT_TAU = 0.3989422804014327
VMEM_MIB = dict(forward=60, ff_back=32, attention_back=16, input_back=18, wgrad=16, step=20, lanes=24)
FF_PARTS = 4
FACTS_TAIL = 4
FAST = jnp.float32
LOW = jnp.bfloat16


COST_SCALE = 10


def cost(microseconds):
    return pl.CostEstimate(flops=int(microseconds * COST_SCALE * 1.15e9), bytes_accessed=1, transcendentals=0)


def mm(left, right):
    return jnp.dot(left, right, preferred_element_type=FAST)


def mm_nt(left, right):
    return lax.dot_general(left, right, TOKENS_MINOR, preferred_element_type=FAST)


def mm_tn(left, right):
    return lax.dot_general(left, right, TOKENS_MAJOR, preferred_element_type=FAST)


def vectors_kernel(*refs):
    *ins, out = refs
    for place, ref in enumerate(ins[:-1]):
        out[:, place, :] = ref[...].astype(FAST)
    wide = out.shape[2]
    for part in range(FF_PARTS):
        out[:, len(ins) - 1 + part, :] = ins[-1][:, part * wide : (part + 1) * wide].astype(FAST)


def vectors_call(*vectors):
    layers, wide = vectors[0].shape
    return pl.pallas_call(
        vectors_kernel,
        out_shape=jax.ShapeDtypeStruct((layers, len(vectors) - 1 + FF_PARTS, wide), FAST),
        name="vectors",
    )(*vectors)


def row_norm(value):
    average = jnp.mean(value, axis=-1, keepdims=True)
    centred = value - average
    inverse_scale = lax.rsqrt(jnp.mean(centred * centred, axis=-1, keepdims=True) + EPSILON)
    return centred * inverse_scale, inverse_scale


def gelu_and_slope(value):
    size = jnp.abs(value)
    near = 1.0 / (1.0 + (0.3275911 * ROOT_HALF) * size)
    bell = jnp.exp(value * value * -0.5)
    poly = near * (
        0.127414796
        + near * (-0.142248368 + near * (0.7107068705 + near * (-0.7265760135 + near * 0.5307027145)))
    )
    tail = poly * bell
    below = jnp.where(value >= 0, 1.0 - tail, tail)
    return value * below, below + value * (bell * ROOT_TAU)


VEC_ROWS = dict(b_query=0, b_value=1, b_out=2, gain_one=3, shift_one=4, b_down=5, gain_two=6, shift_two=7)
VEC_UP = 8


def forward_kernel(layer, swapped, start, facts, own, near, far, top, vecs, *refs):
    weights, refs = refs[:6], refs[6:]
    refs = refs[len(refs) - 25 :]
    outs, scratch = refs[:16], refs[16:]
    (
        o_sent, o_extra, o_low, o_q, o_k, o_v, o_lse, o_ctx, o_n1, o_r1, o_hid, o_act, o_slope, o_n2, o_r2, o_done,
    ) = outs
    o_top = o_near = o_extra
    w_q, w_k, w_v, w_o, w_up, w_down, mix, ctx, sems = scratch
    first = pl.program_id(0) == 0
    held = (w_q, w_k, w_v, w_o, w_up, w_down)
    copies = [
        pltpu.make_async_copy(weights[i].at[layer], held[i], sems.at[i]) for i in range(6)
    ]

    @pl.when(first)
    def _():
        for copy in copies:
            copy.start()

    def ready(*which):
        @pl.when(first)
        def _():
            for i in which:
                copies[i].wait()

    def vec(name):
        row = VEC_ROWS[name]
        return vecs[layer, row : row + 1, :]

    rows = own.shape[1]
    x = own[0]
    ready(0, 1, 2)
    queries = (mm(x, w_q[...]) + vec("b_query")).astype(LOW)
    o_q[0] = queries * jnp.asarray(HEAD_DIM**-0.5, LOW)
    for part, source in ((0, near), (1, far)):
        block = source[0]
        o_k[0, part * rows : (part + 1) * rows, :] = mm(block, w_k[...]).astype(LOW)
        o_v[0, part * rows : (part + 1) * rows, :] = (mm(block, w_v[...]) + vec("b_value")).astype(LOW)
    spots = facts.shape[0] - FACTS_TAIL + 2 * layer
    length = facts[start + pl.program_id(0)]
    lane = lax.broadcasted_iota(jnp.int32, (1, 2 * rows), 1)
    place = jnp.where(lane < rows, facts[spots] + lane, facts[spots + 1] + (lane - rows))
    bias = jnp.where(place < length, 0.0, MASKED).astype(FAST)
    lower = lax.broadcasted_iota(jnp.int32, (1, 128), 1) < HEAD_DIM
    column = lax.broadcasted_iota(jnp.int32, (1, 128), 1)
    logs = jnp.zeros((rows, 128), FAST)
    for pair in range(HEADS // 2):
        lanes = slice(pair * 128, pair * 128 + 128)
        q_pair, k_pair, v_pair = o_q[0, :, lanes], o_k[0, :, lanes], o_v[0, :, lanes]
        got = []
        for side in range(2):
            mask = lower if side == 0 else ~lower
            q_one = jnp.where(mask, q_pair, jnp.zeros_like(q_pair))
            scores = mm_nt(q_one, k_pair) + bias
            high = jnp.max(scores, axis=-1, keepdims=True)
            weight = jnp.exp(scores - high)
            total = jnp.sum(weight, axis=-1, keepdims=True)
            got.append(mm(weight.astype(LOW), v_pair) * (1.0 / total))
            logs = jnp.where(column == 2 * pair + side, high + jnp.log(total), logs)
        ctx[:, lanes] = jnp.where(lower, got[0], got[1]).astype(LOW)
    o_lse[0] = logs.T[:16, :]
    o_ctx[0] = ctx[...]
    ready(3)
    branch = mm(ctx[...], w_o[...]) + vec("b_out") + top[0].astype(FAST)
    n1, r1 = row_norm(branch)
    o_n1[0] = n1.astype(LOW)
    o_r1[0] = r1
    hidden = n1 * vec("gain_one") + vec("shift_one")
    hid = hidden.astype(LOW)
    o_hid[0] = hid
    mix[...] = hidden + vec("b_down")
    ready(4, 5)
    width = w_up.shape[1] // FF_PARTS
    for part in range(FF_PARTS):
        cols = slice(part * width, (part + 1) * width)
        pre = mm(hid, w_up[:, cols]) + vecs[layer, VEC_UP + part : VEC_UP + part + 1, :]
        act, slope = gelu_and_slope(pre)
        act = act.astype(LOW)
        o_act[0, :, cols] = act
        o_slope[0, :, cols] = slope.astype(LOW)
        mix[...] += mm(act, w_down[cols, :])
    n2, r2 = row_norm(mix[...])
    o_n2[0] = n2.astype(LOW)
    o_r2[0] = r2
    result = n2 * vec("gain_two") + vec("shift_two")
    if not swapped:
        o_top[0] = result
    low = result.astype(LOW)
    o_sent[0] = low
    if swapped:
        o_near[0] = near[0]
    o_low[0] = low
    o_done[...] = jnp.zeros_like(o_done)


KEPT = ("extra", "low", "q", "k", "v", "lse", "ctx", "n1", "r1", "hid", "act", "slope", "n2", "r2")


def forward_call(layer, swapped, start, count, facts, own, near, far, top, vecs, weights, kept, sizes):
    seqs, rows, wide, hidden = sizes

    def taken(source):
        array, offset = source
        return pl.BlockSpec((1,) + array.shape[1:], lambda i: (start - offset + i, 0, 0))

    shapes = dict(
        extra=((rows, wide), LOW if swapped else FAST), low=((rows, wide), LOW),
        q=((rows, wide), LOW), k=((2 * rows, wide), LOW), v=((2 * rows, wide), LOW), lse=((16, rows), FAST),
        ctx=((rows, wide), LOW), n1=((rows, wide), LOW), r1=((rows, 1), FAST), hid=((rows, wide), LOW),
        act=((rows, hidden), LOW), slope=((rows, hidden), LOW), n2=((rows, wide), LOW), r2=((rows, 1), FAST),
    )
    out_shape = [jax.ShapeDtypeStruct((count, rows, wide), LOW)] + [
        jax.ShapeDtypeStruct((seqs,) + shapes[name][0], shapes[name][1]) for name in KEPT
    ]
    out_specs = [pl.BlockSpec((1, rows, wide), lambda i: (i, 0, 0))] + [
        pl.BlockSpec((1,) + shapes[name][0], lambda i: (start + i, 0, 0)) for name in KEPT
    ]
    out_shape.append(jax.ShapeDtypeStruct((8, 128), FAST))
    out_specs.append(pl.BlockSpec((8, 128), lambda i: (0, 0)))
    any_spec = pl.BlockSpec(memory_space=pl.ANY)
    ins = [facts, own[0], near[0], far[0], top[0], vecs, *weights]
    in_specs = [
        pl.BlockSpec(memory_space=pltpu.SMEM), taken(own), taken(near), taken(far), taken(top),
        pl.BlockSpec(vecs.shape, lambda i: (0, 0, 0)),
    ] + [any_spec] * 6
    aliases = {}
    if kept is not None:
        for place, name in enumerate(KEPT):
            aliases[len(ins) + place] = 1 + place
        ins += [kept[name] for name in KEPT]
        in_specs += [any_spec] * len(KEPT)
    got = pl.pallas_call(
        partial(forward_kernel, layer, swapped, start),
        grid=(count,),
        in_specs=in_specs,
        out_specs=out_specs,
        out_shape=out_shape,
        input_output_aliases=aliases,
        scratch_shapes=[
            pltpu.VMEM((wide, wide), LOW), pltpu.VMEM((wide, wide), LOW), pltpu.VMEM((wide, wide), LOW),
            pltpu.VMEM((wide, wide), LOW), pltpu.VMEM((wide, hidden), LOW), pltpu.VMEM((hidden, wide), LOW),
            pltpu.VMEM((rows, wide), FAST), pltpu.VMEM((rows, wide), LOW), pltpu.SemaphoreType.DMA((6,)),
        ],
        compiler_params=pltpu.CompilerParams(vmem_limit_bytes=VMEM_MIB["forward"] << 20),
        cost_estimate=cost(14 * count),
        name=f"layer_forward_{layer}",
    )(*ins)
    return got[0], dict(zip(KEPT, got[1:-1], strict=True)), got[-1]


def norm_back_rows(grad, normed, inverse_scale, gain):
    dn = grad * gain
    return inverse_scale * (
        dn - jnp.mean(dn, axis=-1, keepdims=True) - normed * jnp.mean(dn * normed, axis=-1, keepdims=True)
    )


def column_sum(value):
    return jnp.sum(value.astype(FAST), axis=0, keepdims=True)


def ff_back_kernel(layer, top_grad, n2, r2, slope, n1, r1, vecs, *refs):
    weights, refs = refs[:3], refs[3:]
    o_dy, o_df, o_dz1, o_da, o_dc, o_vec, w_down, w_up, w_o, mix, sems = refs
    first = pl.program_id(0) == 0
    held = (w_down, w_up, w_o)
    copies = [pltpu.make_async_copy(weights[i].at[layer], held[i], sems.at[i]) for i in range(3)]

    @pl.when(first)
    def _():
        for copy in copies:
            copy.start()
        o_vec[...] = jnp.zeros_like(o_vec)

    def ready(which):
        @pl.when(first)
        def _():
            copies[which].wait()

    def vec(name):
        row = VEC_ROWS[name]
        return vecs[layer, row : row + 1, :]

    def add(row, value):
        o_vec[row : row + 1, :] += value

    grad = top_grad[0].astype(FAST)
    normed = n2[0].astype(FAST)
    add(VEC_ROWS["gain_two"], column_sum(grad * normed))
    add(VEC_ROWS["shift_two"], column_sum(grad))
    dz2 = norm_back_rows(grad, normed, r2[0], vec("gain_two"))
    dy = dz2.astype(LOW)
    o_dy[0] = dy
    add(VEC_ROWS["b_down"], column_sum(dy))
    mix[...] = dz2
    ready(0)
    width = w_up.shape[1] // FF_PARTS
    for part in range(FF_PARTS):
        cols = slice(part * width, (part + 1) * width)
        if part == 0:
            ready(1)
        df = (mm_nt(dy, w_down[cols, :]) * slope[0, :, cols].astype(FAST)).astype(LOW)
        o_df[0, :, cols] = df
        add(VEC_UP + part, column_sum(df))
        mix[...] += mm_nt(df, w_up[:, cols])
    grad = mix[...]
    normed = n1[0].astype(FAST)
    add(VEC_ROWS["gain_one"], column_sum(grad * normed))
    add(VEC_ROWS["shift_one"], column_sum(grad))
    dz1 = norm_back_rows(grad, normed, r1[0], vec("gain_one"))
    o_dz1[0] = dz1
    da = dz1.astype(LOW)
    o_da[0] = da
    add(VEC_ROWS["b_out"], column_sum(da))
    ready(2)
    o_dc[0] = mm_nt(da, w_o[...]).astype(LOW)


def ff_back_call(layer, top_grad, kept, vecs, w_down, w_up, w_out):
    seqs, rows, wide = top_grad.shape
    hidden = w_up.shape[2]
    ins = [top_grad, kept["n2"], kept["r2"], kept["slope"], kept["n1"], kept["r1"], vecs, w_down, w_up, w_out]
    each = lambda shape: pl.BlockSpec((1,) + tuple(shape[1:]), lambda i: (i, 0, 0))
    any_spec = pl.BlockSpec(memory_space=pl.ANY)
    in_specs = [each(x.shape) for x in ins[:6]] + [pl.BlockSpec(vecs.shape, lambda i: (0, 0, 0))] + [any_spec] * 3
    out_shape = [
        jax.ShapeDtypeStruct((seqs, rows, wide), LOW), jax.ShapeDtypeStruct((seqs, rows, hidden), LOW),
        jax.ShapeDtypeStruct((seqs, rows, wide), FAST), jax.ShapeDtypeStruct((seqs, rows, wide), LOW),
        jax.ShapeDtypeStruct((seqs, rows, wide), LOW), jax.ShapeDtypeStruct((vecs.shape[1], wide), FAST),
    ]
    out_specs = [each(x.shape) for x in out_shape[:5]] + [pl.BlockSpec(out_shape[5].shape, lambda i: (0, 0))]
    return pl.pallas_call(
        partial(ff_back_kernel, layer),
        grid=(seqs,),
        in_specs=in_specs,
        out_specs=out_specs,
        out_shape=out_shape,
        scratch_shapes=[
            pltpu.VMEM((hidden, wide), LOW), pltpu.VMEM((wide, hidden), LOW), pltpu.VMEM((wide, wide), LOW),
            pltpu.VMEM((rows, wide), FAST), pltpu.SemaphoreType.DMA((3,)),
        ],
        compiler_params=pltpu.CompilerParams(vmem_limit_bytes=VMEM_MIB["ff_back"] << 20),
        cost_estimate=cost(19),
        name=f"ff_back_{layer}",
    )(*ins)


def attention_back_kernel(layer, start, facts, q, k, v, lse, dc, *refs):
    o_dq, o_near, o_far, o_vec, bias = refs[len(refs) - 5 :]
    rows, wide = q.shape[1], q.shape[2]

    @pl.when(pl.program_id(0) == 0)
    def _():
        o_vec[...] = jnp.zeros_like(o_vec)

    spots = facts.shape[0] - FACTS_TAIL + 2 * layer
    length = facts[start + pl.program_id(0)]
    key = lax.broadcasted_iota(jnp.int32, (2 * rows, rows), 0)
    place = jnp.where(key < rows, facts[spots] + key, facts[spots + 1] + (key - rows))
    bias[...] = jnp.where(place < length, 0.0, MASKED).astype(FAST)
    lower = lax.broadcasted_iota(jnp.int32, (1, 128), 1) < HEAD_DIM
    for pair in range(HEADS // 2):
        lanes = slice(pair * 128, pair * 128 + 128)
        q_pair, k_pair, v_pair, dc_pair = q[0, :, lanes], k[0, :, lanes], v[0, :, lanes], dc[0, :, lanes]
        dk = dv = None
        dq = []
        for side in range(2):
            one = 2 * pair + side
            mask = lower if side == 0 else ~lower
            q_one = jnp.where(mask, q_pair, jnp.zeros_like(q_pair))
            dc_one = jnp.where(mask, dc_pair, jnp.zeros_like(dc_pair))
            weight = jnp.exp(mm_nt(k_pair, q_one) + bias[...] - lse[0, one : one + 1, :])
            product = weight * mm_nt(v_pair, dc_one)
            ds = (product - weight * jnp.sum(product, axis=0, keepdims=True)).astype(LOW)
            dv_one = mm(weight.astype(LOW), dc_one)
            dk_one = mm(ds, q_one)
            dv = dv_one if dv is None else dv + dv_one
            dk = dk_one if dk is None else dk + dk_one
            dq.append(mm_tn(ds, k_pair))
        dq_pair = (jnp.where(lower, dq[0], dq[1]) * HEAD_DIM**-0.5).astype(LOW)
        o_dq[0, :, lanes] = dq_pair
        o_vec[0:1, lanes] += column_sum(dq_pair)
        o_near[0, 0, :, lanes] = dk[:rows].astype(LOW)
        o_far[0, 0, :, lanes] = dk[rows:].astype(LOW)
        o_near[0, 1, :, lanes] = dv[:rows].astype(LOW)
        o_far[0, 1, :, lanes] = dv[rows:].astype(LOW)


def blocks(shape, start):
    rest = len(shape) - 1
    return pl.BlockSpec((1,) + tuple(shape[1:]), lambda i: (start + i,) + (0,) * rest)


def chained(ins, in_specs, earlier, places):
    aliases = {}
    if earlier is not None:
        for array, place in zip(earlier, places, strict=True):
            aliases[len(ins)] = place
            ins.append(array)
            in_specs.append(pl.BlockSpec(memory_space=pl.ANY))
    return aliases


def attention_back_call(layer, split, start, count, facts, kept, dc, earlier):
    seqs, rows, wide = dc.shape
    ins = [facts, kept["q"], kept["k"], kept["v"], kept["lse"], dc]
    in_specs = [pl.BlockSpec(memory_space=pltpu.SMEM)] + [blocks(x.shape, start) for x in ins[1:]]
    whole = jax.ShapeDtypeStruct((seqs, rows, wide), LOW)
    both = jax.ShapeDtypeStruct((seqs, 2, rows, wide), LOW)
    single = jax.ShapeDtypeStruct((count, 2, rows, wide), LOW)
    out_shape = [whole, both, single if split else both, jax.ShapeDtypeStruct((8, wide), FAST)]
    out_specs = [
        blocks(whole.shape, start), blocks(both.shape, start), blocks(both.shape, 0 if split else start),
        pl.BlockSpec((8, wide), lambda i: (0, 0)),
    ]
    places = (0, 1) if split else (0, 1, 2)
    aliases = chained(ins, in_specs, earlier and earlier[: len(places)], places)
    return pl.pallas_call(
        partial(attention_back_kernel, layer, start),
        grid=(count,),
        in_specs=in_specs,
        out_specs=out_specs,
        out_shape=out_shape,
        input_output_aliases=aliases,
        scratch_shapes=[pltpu.VMEM((2 * rows, rows), FAST)],
        compiler_params=pltpu.CompilerParams(vmem_limit_bytes=VMEM_MIB["attention_back"] << 20),
        cost_estimate=cost(8 * count),
        name=f"attention_back_{layer}",
    )(*ins)


def input_back_kernel(layer, split, dq, near, *refs):
    got, refs = (refs[0], refs[1:]) if split else (None, refs)
    dz1, *refs = refs
    weights, refs = refs[:3], refs[3:]
    if split:
        o_own, o_pair, o_sent, o_vec, w_q, w_k, w_v, sems = refs[len(refs) - 8 :]
    else:
        o_own, o_vec, w_q, w_k, w_v, sems = refs
    first = pl.program_id(0) == 0
    held = (w_q, w_k, w_v)
    copies = [pltpu.make_async_copy(weights[i].at[layer], held[i], sems.at[i]) for i in range(3)]

    @pl.when(first)
    def _():
        for copy in copies:
            copy.start()
        o_vec[...] = jnp.zeros_like(o_vec)

    if split:
        dk = (near[0, 0].astype(FAST) + got[0, 0].astype(FAST)).astype(LOW)
        dv = (near[0, 1].astype(FAST) + got[0, 1].astype(FAST)).astype(LOW)
        o_pair[0, 0] = dk
        o_pair[0, 1] = dv
    else:
        dk, dv = near[0, 0], near[0, 1]
    o_vec[0:1, :] += column_sum(dv)

    @pl.when(first)
    def _():
        for copy in copies:
            copy.wait()

    far = mm_nt(dk, w_k[...]) + mm_nt(dv, w_v[...])
    here = dz1[0] + mm_nt(dq[0], w_q[...])
    if split:
        o_sent[0] = far.astype(LOW)
        o_own[0] = here
    else:
        o_own[0] = here + far


def input_back_call(layer, split, start, count, dq, near, got, dz1, weights, earlier):
    seqs, rows, wide = dq.shape
    ins = [dq, near]
    in_specs = [blocks(dq.shape, start), blocks(near.shape, start)]
    if split:
        ins.append(got)
        in_specs.append(blocks(got.shape, 0))
    ins += [dz1, *weights]
    in_specs += [blocks(dz1.shape, start)] + [pl.BlockSpec(memory_space=pl.ANY)] * 3
    out_shape = [jax.ShapeDtypeStruct((seqs, rows, wide), FAST)]
    out_specs = [blocks(dz1.shape, start)]
    if split:
        out_shape += [
            jax.ShapeDtypeStruct((seqs, 2, rows, wide), LOW), jax.ShapeDtypeStruct((count, rows, wide), LOW)
        ]
        out_specs += [blocks(out_shape[1].shape, start), blocks(out_shape[2].shape, 0)]
    out_shape.append(jax.ShapeDtypeStruct((8, wide), FAST))
    out_specs.append(pl.BlockSpec((8, wide), lambda i: (0, 0)))
    aliases = chained(ins, in_specs, earlier and earlier[:2], (0, 1))
    return pl.pallas_call(
        partial(input_back_kernel, layer, split),
        grid=(count,),
        in_specs=in_specs,
        out_specs=out_specs,
        out_shape=out_shape,
        input_output_aliases=aliases,
        scratch_shapes=[pltpu.VMEM((wide, wide), LOW)] * 3 + [pltpu.SemaphoreType.DMA((3,))],
        compiler_params=pltpu.CompilerParams(vmem_limit_bytes=VMEM_MIB["input_back"] << 20),
        cost_estimate=cost(2 + 3 * count),
        name=f"input_back_{layer}",
    )(*ins)


def wgrad_kernel(count, place_ref, *refs):
    lefts, rights, (o_kept, o_sent) = refs[:count], refs[count : 2 * count], refs[2 * count :]
    pairs, rows = o_kept.shape[1], o_kept.shape[2]

    def write(o_even, o_odd):
        for i in range(count):
            full = mm_tn(lefts[i][...], rights[i][...])
            for pair in range(pairs):
                start = 2 * pair * rows
                o_even[i, pair] = full[start : start + rows].astype(LOW)
                o_odd[i, pair] = full[start + rows : start + 2 * rows].astype(LOW)

    @pl.when(place_ref[0] == 0)
    def _():
        write(o_kept, o_sent)

    @pl.when(place_ref[0] == 1)
    def _():
        write(o_sent, o_kept)


def wgrad_call(name, place, devices, lefts, rights, chunk):
    tokens, height = lefts[0].shape
    width = rights[0].shape[1]
    count = len(lefts)
    rows = height // devices
    steps = height // chunk
    shape = jax.ShapeDtypeStruct((count, devices // 2, rows, width), LOW)
    out_spec = pl.BlockSpec((count, devices // 2 // steps, rows, width), lambda i: (0, i, 0, 0))
    return pl.pallas_call(
        partial(wgrad_kernel, count),
        grid=(steps,),
        in_specs=[pl.BlockSpec(memory_space=pltpu.SMEM)]
        + [pl.BlockSpec((tokens, chunk), lambda i: (0, i))] * count
        + [pl.BlockSpec((tokens, width), lambda i: (0, 0))] * count,
        out_specs=[out_spec] * 2,
        out_shape=[shape] * 2,
        compiler_params=pltpu.CompilerParams(vmem_limit_bytes=VMEM_MIB["wgrad"] << 20),
        cost_estimate=cost(3 + 2 * count * height * width / 1e6),
        name=f"wgrad_{name}",
    )(place, *lefts, *rights)


def step_kernel(plan, bits, *refs):
    count = len(plan)
    for i, (outer, inner, digit) in enumerate(plan):
        kept, got = refs[2 * i], refs[2 * i + 1]
        o_kept, o_sent = refs[2 * count + 2 * i], refs[2 * count + 2 * i + 1]
        mine = bits[digit]
        for group in range(kept.shape[0]):
            for a in range(outer):
                for out, side in ((o_kept, mine), (o_sent, 1 - mine)):
                    source = pl.ds((2 * a + side) * inner, inner)
                    total = kept[group, source].astype(FAST) + got[group, source].astype(FAST)
                    out[group, a * inner : (a + 1) * inner] = total.astype(LOW)


def step_call(values, gots, plan, bits):
    steps = 1 if any(value.shape[3] % 384 for value in values) else 3
    ins, in_specs, out_specs, out_shape, moved = [], [], [], [], 0
    for value, got in zip(values, gots, strict=True):
        groups, parts, rows, columns = value.shape
        whole = pl.BlockSpec((groups, parts, rows, columns // steps), lambda i: (0, 0, 0, i))
        half = pl.BlockSpec((groups, parts // 2, rows, columns // steps), lambda i: (0, 0, 0, i))
        ins += [value, got]
        in_specs += [whole] * 2
        out_specs += [half] * 2
        out_shape += [jax.ShapeDtypeStruct((groups, parts // 2, rows, columns), LOW)] * 2
        moved += 6 * value.size
    return pl.pallas_call(
        partial(step_kernel, plan),
        grid=(steps,),
        in_specs=[pl.BlockSpec(memory_space=pltpu.SMEM)] + in_specs,
        out_specs=out_specs,
        out_shape=out_shape,
        compiler_params=pltpu.CompilerParams(vmem_limit_bytes=VMEM_MIB["step"] << 20),
        cost_estimate=cost(1 + moved / 3e6),
        name="exchange_step",
    )(bits, *ins)


def lanes_kernel(plan, bits, *refs):
    count = len(refs) // 2 - len(plan)
    ins, outs = refs[: 2 * count], refs[2 * count :]
    for lane, (outer, inner, digit) in enumerate(plan):
        mine = bits[digit]
        for out, side in ((outs[2 * lane], mine), (outs[2 * lane + 1], 1 - mine)):
            groups, parts, rows, columns = out.shape
            first = 0
            for i in range(count):
                kept, got = ins[2 * i], ins[2 * i + 1]
                wide = kept.shape[3] // len(plan)
                cols = slice(lane * wide, (lane + 1) * wide)
                for group in range(kept.shape[0]):
                    for part in range(parts):
                        source = (2 * (part // inner) + side) * inner + part % inner
                        total = kept[group, source, :, cols].astype(FAST) + got[group, source, :, cols].astype(FAST)
                        if groups == 1:
                            total = [total[:, at : at + columns] for at in range(0, wide, columns)]
                            total = total[0] if len(total) == 1 else jnp.concatenate(total, axis=0)
                            out[0, part, first : first + total.shape[0], :] = total.astype(LOW)
                        else:
                            out[first + group, part] = total.astype(LOW)
                first += rows // count if groups == 1 else kept.shape[0]


def lanes_call(values, gots, plan, bits, stacked):
    lanes = len(plan)
    parts = values[0].shape[1]
    columns = min(value.shape[3] for value in values) // lanes
    if stacked:
        shape = (1, parts // 2, sum(v.shape[2] * (v.shape[3] // lanes // columns) for v in values), columns)
    else:
        shape = (sum(v.shape[0] for v in values), parts // 2, values[0].shape[2], columns)
    whole = lambda v: pl.BlockSpec((v.shape[0], parts // 2) + v.shape[2:], lambda i: (0, i, 0, 0))
    half = pl.BlockSpec((shape[0], parts // 4) + shape[2:], lambda i: (0, i, 0, 0))
    ins = [array for pair in zip(values, gots, strict=True) for array in pair]
    return pl.pallas_call(
        partial(lanes_kernel, tuple((outer // 2, inner, digit) for outer, inner, digit in plan)),
        grid=(2,),
        in_specs=[pl.BlockSpec(memory_space=pltpu.SMEM)] + [whole(v) for v in ins],
        out_specs=[half] * (2 * lanes),
        out_shape=[jax.ShapeDtypeStruct(shape, LOW)] * (2 * lanes),
        compiler_params=pltpu.CompilerParams(vmem_limit_bytes=VMEM_MIB["lanes"] << 20),
        cost_estimate=cost(6),
        name="exchange_lanes",
    )(bits, *ins)


def local(
    tokens, lengths, w_query, b_query, w_key, w_value, b_value, w_out, b_out, gain_one, shift_one,
    w_up, b_up, w_down, b_down, gain_two, shift_two, cotangent,
):
    seqs, rows, wide = tokens.shape
    hidden = w_up.shape[2]
    sizes = (seqs, rows, wide, hidden)
    weights = (w_query, w_key, w_value, w_out, w_up, w_down)
    vecs = vectors_call(b_query, b_value, b_out, gain_one, shift_one, b_down, gain_two, shift_two, b_up)
    devices = lax.axis_size("batch") * lax.axis_size("seq")
    seq_index = lax.axis_index("seq").astype(jnp.int32)
    spots = [(seq_index ^ flip) * rows for flip in (0, 1, 2, 3)]
    facts = jnp.concatenate([lengths, jnp.stack(spots)]).astype(jnp.int32)
    bits = jnp.stack([lax.axis_index(axis) >> bit & 1 for axis, bit in digit_list()]).astype(jnp.int32)
    flat = lambda value: value.reshape(seqs * rows, value.shape[-1])
    cuts = [(0, 2), (2, seqs - 2)]

    kept_one, kept_two, nears = None, None, []
    other = swapped_2(tokens, "seq", 0)
    for start, count in cuts:
        low, kept_one, _ = forward_call(
            0, False, start, count, facts, (tokens, 0), (tokens, 0), (other, 0), (tokens, 0), vecs, weights, kept_one, sizes
        )
        low, kept_one["r2"] = tie(low, kept_one["r2"])
        nears.append(swapped_2(low, "seq", 1))
    for near, (start, count) in zip(nears, cuts, strict=True):
        if kept_two is not None:
            near, kept_two["r2"] = tie(near, kept_two["r2"])
        else:
            near, kept_one["r2"] = tie(near, kept_one["r2"])
        far = swapped_2(near, "seq", 0)
        _, kept_two, _ = forward_call(
            1, True, start, count, facts, (kept_one["low"], 0), (near, start), (far, start),
            (kept_one["extra"], 0), vecs, weights, kept_two, sizes,
        )
    final = kept_two["low"]

    back_weights = (w_query, w_key, w_value)
    near_first, far_first, across_first = digit_orders()
    wgrad = partial(wgrad_call, place=bits, devices=devices)
    half = wide // 2

    kept = kept_two
    dy, df, dz1, da, dc, vec_two = ff_back_call(1, cotangent, kept, vecs, w_down, w_up, w_out)
    down_two = wgrad("down", lefts=[flat(kept["act"])], rights=[flat(dy)], chunk=wide)
    down_two, dc = Sum.begin(down_two, near_first, bits, dc)
    att = attention_back_call(1, True, 0, 2, facts, kept, dc, None)
    att = join(att, down_two)
    vec_q = att[3]
    (dc, far) = advance((dc, att[2]), down_two)
    got = swapped_2(far, "seq", 0)
    att = attention_back_call(1, True, 2, seqs - 2, facts, kept, dc, att)
    vec_q += att[3]
    att, got, df = tie(att, got, df)
    got_late = swapped_2(att[2], "seq", 0)
    ends = input_back_call(1, True, 0, 2, att[0], att[1], got, dz1, back_weights, None)
    vec_v = ends[3]
    ends, df = tie(ends, df)
    arrived = [swapped_2(ends[2], "seq", 1)]
    up_two = wgrad("up", lefts=[flat(kept["hid"])], rights=[flat(df)], chunk=half)
    up_two, (got_late, dz1) = Sum.begin(up_two, near_first, bits, (got_late, dz1))
    ends = input_back_call(1, True, 2, seqs - 2, att[0], att[1], got_late, dz1, back_weights, ends)
    vec_v += ends[3]
    ends = tie(*ends)
    arrived.append(swapped_2(ends[2], "seq", 1))
    ends = join(ends, up_two, down_two)
    pair = advance(ends[1], up_two, down_two)
    near = kept["extra"]
    four_two = wgrad(
        "four",
        lefts=[flat(kept["ctx"]), flat(kept_one["low"]), flat(near), flat(near)],
        rights=[flat(da), flat(att[0]), flat(pair[:, 0]), flat(pair[:, 1])],
        chunk=half,
    )
    four_two, arrived = Sum.begin(four_two, across_first, bits, arrived)
    vec_two = (vec_two, vec_q, vec_v)
    middle = ends[0] + jnp.concatenate(arrived).astype(FAST)

    kept = kept_one
    ff = ff_back_call(0, middle, kept, vecs, w_down, w_up, w_out)
    dy, df, dz1, da, dc, vec_one = join(ff, down_two, four_two)
    dy = advance(dy, down_two, four_two)
    down_one = wgrad("down", lefts=[flat(kept["act"])], rights=[flat(dy)], chunk=wide)
    down_one, df = Sum.begin(down_one, near_first, bits, df)
    up_one = wgrad("up", lefts=[flat(kept["hid"])], rights=[flat(df)], chunk=half)
    up_one, dc = join((up_one, dc), down_one, down_two, up_two)
    up_one, dc = Sum.begin(up_one, near_first, bits, dc)
    dc = advance(dc, down_two, up_two)
    att = attention_back_call(0, False, 0, 2, facts, kept, dc, None)
    vec_q = att[3]
    att, dc = join((att, dc), up_one, up_two, four_two, down_two)
    lanes_one, dc = lanes_of(dc, down_one, up_one, stacked=True)
    dc = advance(dc, up_two, four_two)
    att = attention_back_call(0, False, 2, seqs - 2, facts, kept, dc, att)
    vec_q += att[3]
    att, da, vec_q = join((att, da, vec_q), up_two)
    got = swapped_2(att[2], "seq", 0)
    rest_one = wgrad("rest", lefts=[flat(kept["ctx"]), flat(tokens)], rights=[flat(da), flat(att[0])], chunk=half)
    rest_one, got = tie(rest_one, got)
    rest_one, got = Sum.begin(rest_one, across_first, bits, got)
    pair = (att[1].astype(FAST) + got.astype(FAST)).astype(LOW)
    vectors = Whole([(vec_one, vec_q, jnp.sum(pair[:, 1].astype(FAST), axis=(0, 1))[None]), vec_two])
    pair = vectors.send(pair)
    pairs_one = wgrad("pair", lefts=[flat(tokens)] * 2, rights=[flat(pair[:, 0]), flat(pair[:, 1])], chunk=half)
    pairs_one, dz1 = Sum.begin(pairs_one, near_first, bits, dz1)
    dz1 = join(dz1, *lanes_one, vectors)
    dz1 = advance(dz1, *lanes_one)
    dz1 = vectors.send(dz1)
    ends = input_back_call(0, False, 0, seqs, att[0], pair, None, dz1, back_weights, None)
    result = join(ends[0], rest_one, pairs_one, vectors)
    last_one, result = lanes_of(result, rest_one, pairs_one, stacked=False)
    result = vectors.send(result)
    live = [*lanes_one, *last_one, four_two, up_two, down_two]
    result = join(result, *lanes_one, four_two, up_two, down_two, vectors)
    result = advance(result, *lanes_one, four_two, up_two, down_two)
    while any(one.got is not None for one in live):
        result = vectors.send(result)
        result = join(result, *live, vectors)
        result = advance(result, *live)
    rows_down = hidden // devices
    both = [one.value[0] for one in lanes_one]
    down_part = jnp.concatenate([one[:rows_down] for one in both], axis=-1)
    up_part = [one[rows_down:].reshape(FF_PARTS, -1, one.shape[-1]) for one in both]
    up_part = jnp.concatenate([one[part] for one in up_part for part in range(FF_PARTS)], axis=-1)
    sums = [
        (down_part, up_part, jnp.concatenate([one.value for one in last_one], axis=-1)),
        (down_two.value[0], up_two.value[0], four_two.value),
    ]
    return (final, result) + gathered(sums, vectors.value, devices)


def tie(*values):
    return lax.optimization_barrier(values)


def digit_list():
    return [
        (axis, bit) for axis in ("seq", "batch") for bit in range(lax.axis_size(axis).bit_length() - 1)
    ]


def digit_orders():
    low = lax.axis_size("seq").bit_length() - 1
    high = lax.axis_size("batch").bit_length() - 1
    core, across = ("seq", 0), [("seq", bit) for bit in range(1, low)]
    near, far, late = [("batch", 0)], [("batch", 1)], [("batch", bit) for bit in range(2, high)]
    return (
        [core] + near + far + across + late,
        [core] + far + near + across + late,
        [core] + across + near + far + late,
    )


def lane_orders():
    digits = digit_list()[1:]
    across, near, far, late = digits[:1], digits[1:2], digits[2:3], digits[3:]
    return across + near + far + late, near + far + across + late, far + across + near + late


def join(values, *sums):
    live = [one for one in sums if one.got is not None]
    values, gots = lax.optimization_barrier((values, [one.got for one in live]))
    for one, got in zip(live, gots, strict=True):
        one.got = got
    return values


def advance(hold, *sums):
    for one in sums:
        if one.got is not None and not one.order:
            one.value = (one.value.astype(FAST) + one.got.astype(FAST))[:, 0]
            one.got = None
    live = [one for one in sums if one.got is not None]
    if not live:
        return hold
    plan, routes = [], []
    for one in live:
        digit = one.order.pop(0)
        above = one.digits.index(digit)
        one.digits.remove(digit)
        plan.append((1 << above, 1 << len(one.digits) - above, digit_list().index(digit)))
        routes.append(digit)
    halves = step_call([one.value for one in live], [one.got for one in live], tuple(plan), live[0].bits)
    outs, hold = tie(halves[1::2], hold)
    for one, value, out, route in zip(live, halves[::2], outs, routes, strict=True):
        one.value = value
        one.got = swapped_2(out, *route)
    return hold


def lanes_of(hold, *sums, stacked):
    digits = sums[0].digits
    plan, lanes = [], []
    for order in lane_orders():
        above = digits.index(order[0])
        plan.append((1 << above, 1 << len(digits) - 1 - above, digit_list().index(order[0])))
    halves = lanes_call([one.value for one in sums], [one.got for one in sums], tuple(plan), sums[0].bits, stacked)
    outs, hold = tie(halves[1::2], hold)
    for value, out, order in zip(halves[::2], outs, lane_orders(), strict=True):
        one = Sum()
        one.value, one.bits, one.order = value, sums[0].bits, list(order[1:])
        one.digits = [digit for digit in digits if digit != order[0]]
        one.got = swapped_2(out, *order[0])
        lanes.append(one)
    return lanes, hold


class Sum:
    @classmethod
    def begin(cls, halves, order, bits, hold):
        one = cls()
        (one.value, out), hold = tie(halves, hold)
        one.bits = bits
        one.digits = list(reversed(digit_list()))[:-1]
        one.order = list(order[1:])
        one.got = swapped_2(out, *order[0])
        return one, hold


class Whole:
    def __init__(self, layers):
        rows = [jnp.concatenate([vec_q[:1], vec_v[:1], vec[2:]]) for vec, vec_q, vec_v in layers]
        self.value = jnp.stack(rows)
        self.got = None
        self.order = digit_list()

    def send(self, hold):
        if self.got is not None:
            self.value = self.value + self.got
            self.got = None
        if self.order:
            self.value, hold = tie(self.value, hold)
            self.got = swapped_2(self.value, *self.order.pop(0))
        return hold


VECTORS = (1, 4, 6, 7, 8, 12, 13, 14)


def gathered(sums, vectors, devices):
    outs = [None] * 15
    for place, which in enumerate((5, 0, 2, 3)):
        outs[which] = jnp.stack([one[2][place] for one in sums])
    outs[9] = jnp.stack([one[1] for one in sums])
    outs[11] = jnp.stack([one[0] for one in sums])
    mine = lax.axis_index("batch") * lax.axis_size("seq") + lax.axis_index("seq")
    width = vectors.shape[2] // devices
    small = lax.dynamic_slice_in_dim(vectors[:, :8], mine * width, width, axis=2)
    for place, which in enumerate(VECTORS):
        outs[which] = small[:, place]
    large = vectors[:, 8:].reshape(vectors.shape[0], -1)
    width = large.shape[1] // devices
    outs[10] = lax.dynamic_slice_in_dim(large, mine * width, width, axis=1)
    return tuple(outs)


def solution(mesh):
    in_specs = (
        P("batch", "seq", None),
        P("batch"),
        P(),
        P(),
        P(),
        P(),
        P(),
        P(),
        P(),
        P(),
        P(),
        P(),
        P(),
        P(),
        P(),
        P(),
        P(),
        P("batch", "seq", None),
    )
    out_specs = (
        P("batch", "seq", None),
        P("batch", "seq", None),
        P(None, ("batch", "seq"), None),
        P(None, ("batch", "seq")),
        P(None, ("batch", "seq"), None),
        P(None, ("batch", "seq"), None),
        P(None, ("batch", "seq")),
        P(None, ("batch", "seq"), None),
        P(None, ("batch", "seq")),
        P(None, ("batch", "seq")),
        P(None, ("batch", "seq")),
        P(None, ("batch", "seq"), None),
        P(None, ("batch", "seq")),
        P(None, ("batch", "seq"), None),
        P(None, ("batch", "seq")),
        P(None, ("batch", "seq")),
        P(None, ("batch", "seq")),
    )
    return jax.shard_map(local, mesh=mesh, in_specs=in_specs, out_specs=out_specs, check_vma=False)
```

```python
from functools import partial

import jax
import jax.numpy as jnp
from jax import lax
from jax.experimental import pallas as pl
from jax.experimental.pallas import tpu as pltpu
from jax.sharding import PartitionSpec as P

HEADS = 12
HEAD_DIM = 64


EPSILON = 1e-06
MASKED = -1e30


def swapped_2(value, axis, bit):
    return lax.ppermute(value, axis, [(i, i ^ 1 << bit) for i in range(lax.axis_size(axis))])


TOKENS_MINOR = (((1,), (1,)), ((), ()))
TOKENS_MAJOR = (((0,), (0,)), ((), ()))
ROOT_HALF = 0.7071067811865476
ROOT_TAU = 0.3989422804014327
VMEM_MIB = dict(forward=60, ff_back=32, attention_back=16, input_back=18, wgrad=16, step=20, lanes=24, finish=16)
FF_PARTS = 4
FACTS_TAIL = 4
FAST = jnp.float32
LOW = jnp.bfloat16


COST_SCALE = 10


def cost(microseconds):
    return pl.CostEstimate(flops=int(microseconds * COST_SCALE * 1.15e9), bytes_accessed=1, transcendentals=0)


def mm(left, right):
    return jnp.dot(left, right, preferred_element_type=FAST)


def mm_nt(left, right):
    return lax.dot_general(left, right, TOKENS_MINOR, preferred_element_type=FAST)


def mm_tn(left, right):
    return lax.dot_general(left, right, TOKENS_MAJOR, preferred_element_type=FAST)


def vectors_kernel(*refs):
    *ins, out = refs
    for place, ref in enumerate(ins[:-1]):
        out[:, place, :] = ref[...].astype(FAST)
    wide = out.shape[2]
    for part in range(FF_PARTS):
        out[:, len(ins) - 1 + part, :] = ins[-1][:, part * wide : (part + 1) * wide].astype(FAST)


def vectors_call(*vectors):
    layers, wide = vectors[0].shape
    return pl.pallas_call(
        vectors_kernel,
        out_shape=jax.ShapeDtypeStruct((layers, len(vectors) - 1 + FF_PARTS, wide), FAST),
        name="vectors",
    )(*vectors)


def row_norm(value):
    average = jnp.mean(value, axis=-1, keepdims=True)
    centred = value - average
    inverse_scale = lax.rsqrt(jnp.mean(centred * centred, axis=-1, keepdims=True) + EPSILON)
    return centred * inverse_scale, inverse_scale


def gelu_and_slope(value):
    size = jnp.abs(value)
    near = 1.0 / (1.0 + (0.3275911 * ROOT_HALF) * size)
    bell = jnp.exp(value * value * -0.5)
    poly = near * (
        0.127414796
        + near * (-0.142248368 + near * (0.7107068705 + near * (-0.7265760135 + near * 0.5307027145)))
    )
    tail = poly * bell
    below = jnp.where(value >= 0, 1.0 - tail, tail)
    return value * below, below + value * (bell * ROOT_TAU)


VEC_ROWS = dict(b_query=0, b_value=1, b_out=2, gain_one=3, shift_one=4, b_down=5, gain_two=6, shift_two=7)
VEC_UP = 8


def forward_kernel(layer, swapped, start, facts, own, near, far, top, vecs, *refs):
    weights, refs = refs[:6], refs[6:]
    refs = refs[len(refs) - 25 :]
    outs, scratch = refs[:16], refs[16:]
    (
        o_sent, o_extra, o_low, o_q, o_k, o_v, o_lse, o_ctx, o_n1, o_r1, o_hid, o_act, o_slope, o_n2, o_r2, o_done,
    ) = outs
    o_top = o_near = o_extra
    w_q, w_k, w_v, w_o, w_up, w_down, mix, ctx, sems = scratch
    first = pl.program_id(0) == 0
    held = (w_q, w_k, w_v, w_o, w_up, w_down)
    copies = [
        pltpu.make_async_copy(weights[i].at[layer], held[i], sems.at[i]) for i in range(6)
    ]

    @pl.when(first)
    def _():
        for copy in copies:
            copy.start()

    def ready(*which):
        @pl.when(first)
        def _():
            for i in which:
                copies[i].wait()

    def vec(name):
        row = VEC_ROWS[name]
        return vecs[layer, row : row + 1, :]

    rows = own.shape[1]
    x = own[0]
    ready(0, 1, 2)
    queries = (mm(x, w_q[...]) + vec("b_query")).astype(LOW)
    o_q[0] = queries * jnp.asarray(HEAD_DIM**-0.5, LOW)
    for part, source in ((0, near), (1, far)):
        block = source[0]
        o_k[0, part * rows : (part + 1) * rows, :] = mm(block, w_k[...]).astype(LOW)
        o_v[0, part * rows : (part + 1) * rows, :] = (mm(block, w_v[...]) + vec("b_value")).astype(LOW)
    spots = facts.shape[0] - FACTS_TAIL + 2 * layer
    length = facts[start + pl.program_id(0)]
    lane = lax.broadcasted_iota(jnp.int32, (1, 2 * rows), 1)
    place = jnp.where(lane < rows, facts[spots] + lane, facts[spots + 1] + (lane - rows))
    bias = jnp.where(place < length, 0.0, MASKED).astype(FAST)
    lower = lax.broadcasted_iota(jnp.int32, (1, 128), 1) < HEAD_DIM
    column = lax.broadcasted_iota(jnp.int32, (1, 128), 1)
    logs = jnp.zeros((rows, 128), FAST)
    for pair in range(HEADS // 2):
        lanes = slice(pair * 128, pair * 128 + 128)
        q_pair, k_pair, v_pair = o_q[0, :, lanes], o_k[0, :, lanes], o_v[0, :, lanes]
        got = []
        for side in range(2):
            mask = lower if side == 0 else ~lower
            q_one = jnp.where(mask, q_pair, jnp.zeros_like(q_pair))
            scores = mm_nt(q_one, k_pair) + bias
            high = jnp.max(scores, axis=-1, keepdims=True)
            weight = jnp.exp(scores - high)
            total = jnp.sum(weight, axis=-1, keepdims=True)
            got.append(mm(weight.astype(LOW), v_pair) * (1.0 / total))
            logs = jnp.where(column == 2 * pair + side, high + jnp.log(total), logs)
        ctx[:, lanes] = jnp.where(lower, got[0], got[1]).astype(LOW)
    o_lse[0] = logs.T[:16, :]
    o_ctx[0] = ctx[...]
    ready(3)
    branch = mm(ctx[...], w_o[...]) + vec("b_out") + top[0].astype(FAST)
    n1, r1 = row_norm(branch)
    o_n1[0] = n1.astype(LOW)
    o_r1[0] = r1
    hidden = n1 * vec("gain_one") + vec("shift_one")
    hid = hidden.astype(LOW)
    o_hid[0] = hid
    mix[...] = hidden + vec("b_down")
    ready(4, 5)
    width = w_up.shape[1] // FF_PARTS
    for part in range(FF_PARTS):
        cols = slice(part * width, (part + 1) * width)
        pre = mm(hid, w_up[:, cols]) + vecs[layer, VEC_UP + part : VEC_UP + part + 1, :]
        act, slope = gelu_and_slope(pre)
        act = act.astype(LOW)
        o_act[0, :, cols] = act
        o_slope[0, :, cols] = slope.astype(LOW)
        mix[...] += mm(act, w_down[cols, :])
    n2, r2 = row_norm(mix[...])
    o_n2[0] = n2.astype(LOW)
    o_r2[0] = r2
    result = n2 * vec("gain_two") + vec("shift_two")
    if not swapped:
        o_top[0] = result
    low = result.astype(LOW)
    o_sent[0] = low
    if swapped:
        o_near[0] = near[0]
    o_low[0] = low
    o_done[...] = jnp.zeros_like(o_done)


KEPT = ("extra", "low", "q", "k", "v", "lse", "ctx", "n1", "r1", "hid", "act", "slope", "n2", "r2")


def forward_call(layer, swapped, start, count, facts, own, near, far, top, vecs, weights, kept, sizes):
    seqs, rows, wide, hidden = sizes

    def taken(source):
        array, offset = source
        return pl.BlockSpec((1,) + array.shape[1:], lambda i: (start - offset + i, 0, 0))

    shapes = dict(
        extra=((rows, wide), LOW if swapped else FAST), low=((rows, wide), LOW),
        q=((rows, wide), LOW), k=((2 * rows, wide), LOW), v=((2 * rows, wide), LOW), lse=((16, rows), FAST),
        ctx=((rows, wide), LOW), n1=((rows, wide), LOW), r1=((rows, 1), FAST), hid=((rows, wide), LOW),
        act=((rows, hidden), LOW), slope=((rows, hidden), LOW), n2=((rows, wide), LOW), r2=((rows, 1), FAST),
    )
    out_shape = [jax.ShapeDtypeStruct((count, rows, wide), LOW)] + [
        jax.ShapeDtypeStruct((seqs,) + shapes[name][0], shapes[name][1]) for name in KEPT
    ]
    out_specs = [pl.BlockSpec((1, rows, wide), lambda i: (i, 0, 0))] + [
        pl.BlockSpec((1,) + shapes[name][0], lambda i: (start + i, 0, 0)) for name in KEPT
    ]
    out_shape.append(jax.ShapeDtypeStruct((8, 128), FAST))
    out_specs.append(pl.BlockSpec((8, 128), lambda i: (0, 0)))
    any_spec = pl.BlockSpec(memory_space=pl.ANY)
    ins = [facts, own[0], near[0], far[0], top[0], vecs, *weights]
    in_specs = [
        pl.BlockSpec(memory_space=pltpu.SMEM), taken(own), taken(near), taken(far), taken(top),
        pl.BlockSpec(vecs.shape, lambda i: (0, 0, 0)),
    ] + [any_spec] * 6
    aliases = {}
    if kept is not None:
        for place, name in enumerate(KEPT):
            aliases[len(ins) + place] = 1 + place
        ins += [kept[name] for name in KEPT]
        in_specs += [any_spec] * len(KEPT)
    got = pl.pallas_call(
        partial(forward_kernel, layer, swapped, start),
        grid=(count,),
        in_specs=in_specs,
        out_specs=out_specs,
        out_shape=out_shape,
        input_output_aliases=aliases,
        scratch_shapes=[
            pltpu.VMEM((wide, wide), LOW), pltpu.VMEM((wide, wide), LOW), pltpu.VMEM((wide, wide), LOW),
            pltpu.VMEM((wide, wide), LOW), pltpu.VMEM((wide, hidden), LOW), pltpu.VMEM((hidden, wide), LOW),
            pltpu.VMEM((rows, wide), FAST), pltpu.VMEM((rows, wide), LOW), pltpu.SemaphoreType.DMA((6,)),
        ],
        compiler_params=pltpu.CompilerParams(vmem_limit_bytes=VMEM_MIB["forward"] << 20),
        cost_estimate=cost(14 * count),
        name=f"layer_forward_{layer}",
    )(*ins)
    return got[0], dict(zip(KEPT, got[1:-1], strict=True)), got[-1]


def norm_back_rows(grad, normed, inverse_scale, gain):
    dn = grad * gain
    return inverse_scale * (
        dn - jnp.mean(dn, axis=-1, keepdims=True) - normed * jnp.mean(dn * normed, axis=-1, keepdims=True)
    )


def column_sum(value):
    return jnp.sum(value.astype(FAST), axis=0, keepdims=True)


def ff_back_kernel(layer, top_grad, n2, r2, slope, n1, r1, vecs, *refs):
    weights, refs = refs[:3], refs[3:]
    o_dy, o_df, o_dz1, o_da, o_dc, o_vec, w_down, w_up, w_o, mix, sems = refs
    first = pl.program_id(0) == 0
    held = (w_down, w_up, w_o)
    copies = [pltpu.make_async_copy(weights[i].at[layer], held[i], sems.at[i]) for i in range(3)]

    @pl.when(first)
    def _():
        for copy in copies:
            copy.start()
        o_vec[...] = jnp.zeros_like(o_vec)

    def ready(which):
        @pl.when(first)
        def _():
            copies[which].wait()

    def vec(name):
        row = VEC_ROWS[name]
        return vecs[layer, row : row + 1, :]

    def add(row, value):
        o_vec[row : row + 1, :] += value

    grad = top_grad[0].astype(FAST)
    normed = n2[0].astype(FAST)
    add(VEC_ROWS["gain_two"], column_sum(grad * normed))
    add(VEC_ROWS["shift_two"], column_sum(grad))
    dz2 = norm_back_rows(grad, normed, r2[0], vec("gain_two"))
    dy = dz2.astype(LOW)
    o_dy[0] = dy
    add(VEC_ROWS["b_down"], column_sum(dy))
    mix[...] = dz2
    ready(0)
    width = w_up.shape[1] // FF_PARTS
    for part in range(FF_PARTS):
        cols = slice(part * width, (part + 1) * width)
        if part == 0:
            ready(1)
        df = (mm_nt(dy, w_down[cols, :]) * slope[0, :, cols].astype(FAST)).astype(LOW)
        o_df[0, :, cols] = df
        add(VEC_UP + part, column_sum(df))
        mix[...] += mm_nt(df, w_up[:, cols])
    grad = mix[...]
    normed = n1[0].astype(FAST)
    add(VEC_ROWS["gain_one"], column_sum(grad * normed))
    add(VEC_ROWS["shift_one"], column_sum(grad))
    dz1 = norm_back_rows(grad, normed, r1[0], vec("gain_one"))
    o_dz1[0] = dz1
    da = dz1.astype(LOW)
    o_da[0] = da
    add(VEC_ROWS["b_out"], column_sum(da))
    ready(2)
    o_dc[0] = mm_nt(da, w_o[...]).astype(LOW)


def ff_back_call(layer, top_grad, kept, vecs, w_down, w_up, w_out):
    seqs, rows, wide = top_grad.shape
    hidden = w_up.shape[2]
    ins = [top_grad, kept["n2"], kept["r2"], kept["slope"], kept["n1"], kept["r1"], vecs, w_down, w_up, w_out]
    each = lambda shape: pl.BlockSpec((1,) + tuple(shape[1:]), lambda i: (i, 0, 0))
    any_spec = pl.BlockSpec(memory_space=pl.ANY)
    in_specs = [each(x.shape) for x in ins[:6]] + [pl.BlockSpec(vecs.shape, lambda i: (0, 0, 0))] + [any_spec] * 3
    out_shape = [
        jax.ShapeDtypeStruct((seqs, rows, wide), LOW), jax.ShapeDtypeStruct((seqs, rows, hidden), LOW),
        jax.ShapeDtypeStruct((seqs, rows, wide), FAST), jax.ShapeDtypeStruct((seqs, rows, wide), LOW),
        jax.ShapeDtypeStruct((seqs, rows, wide), LOW), jax.ShapeDtypeStruct((vecs.shape[1], wide), FAST),
    ]
    out_specs = [each(x.shape) for x in out_shape[:5]] + [pl.BlockSpec(out_shape[5].shape, lambda i: (0, 0))]
    return pl.pallas_call(
        partial(ff_back_kernel, layer),
        grid=(seqs,),
        in_specs=in_specs,
        out_specs=out_specs,
        out_shape=out_shape,
        scratch_shapes=[
            pltpu.VMEM((hidden, wide), LOW), pltpu.VMEM((wide, hidden), LOW), pltpu.VMEM((wide, wide), LOW),
            pltpu.VMEM((rows, wide), FAST), pltpu.SemaphoreType.DMA((3,)),
        ],
        compiler_params=pltpu.CompilerParams(vmem_limit_bytes=VMEM_MIB["ff_back"] << 20),
        cost_estimate=cost(19),
        name=f"ff_back_{layer}",
    )(*ins)


def attention_back_kernel(layer, start, facts, q, k, v, lse, dc, *refs):
    o_dq, o_near, o_far, o_vec, bias = refs[len(refs) - 5 :]
    rows, wide = q.shape[1], q.shape[2]

    @pl.when(pl.program_id(0) == 0)
    def _():
        o_vec[...] = jnp.zeros_like(o_vec)

    spots = facts.shape[0] - FACTS_TAIL + 2 * layer
    length = facts[start + pl.program_id(0)]
    key = lax.broadcasted_iota(jnp.int32, (2 * rows, rows), 0)
    place = jnp.where(key < rows, facts[spots] + key, facts[spots + 1] + (key - rows))
    bias[...] = jnp.where(place < length, 0.0, MASKED).astype(FAST)
    lower = lax.broadcasted_iota(jnp.int32, (1, 128), 1) < HEAD_DIM
    for pair in range(HEADS // 2):
        lanes = slice(pair * 128, pair * 128 + 128)
        q_pair, k_pair, v_pair, dc_pair = q[0, :, lanes], k[0, :, lanes], v[0, :, lanes], dc[0, :, lanes]
        dk = dv = None
        dq = []
        for side in range(2):
            one = 2 * pair + side
            mask = lower if side == 0 else ~lower
            q_one = jnp.where(mask, q_pair, jnp.zeros_like(q_pair))
            dc_one = jnp.where(mask, dc_pair, jnp.zeros_like(dc_pair))
            weight = jnp.exp(mm_nt(k_pair, q_one) + bias[...] - lse[0, one : one + 1, :])
            product = weight * mm_nt(v_pair, dc_one)
            ds = (product - weight * jnp.sum(product, axis=0, keepdims=True)).astype(LOW)
            dv_one = mm(weight.astype(LOW), dc_one)
            dk_one = mm(ds, q_one)
            dv = dv_one if dv is None else dv + dv_one
            dk = dk_one if dk is None else dk + dk_one
            dq.append(mm_tn(k_pair, ds)[side * HEAD_DIM : (side + 1) * HEAD_DIM])
        dq_pair = (jnp.concatenate(dq, axis=0).T * HEAD_DIM**-0.5).astype(LOW)
        o_dq[0, :, lanes] = dq_pair
        o_vec[0:1, lanes] += column_sum(dq_pair)
        o_vec[1:2, lanes] += column_sum(dv)
        o_near[0, 0, :, lanes] = dk[:rows].astype(LOW)
        o_far[0, 0, :, lanes] = dk[rows:].astype(LOW)
        o_near[0, 1, :, lanes] = dv[:rows].astype(LOW)
        o_far[0, 1, :, lanes] = dv[rows:].astype(LOW)


def blocks(shape, start):
    rest = len(shape) - 1
    return pl.BlockSpec((1,) + tuple(shape[1:]), lambda i: (start + i,) + (0,) * rest)


def chained(ins, in_specs, earlier, places):
    aliases = {}
    if earlier is not None:
        for array, place in zip(earlier, places, strict=True):
            aliases[len(ins)] = place
            ins.append(array)
            in_specs.append(pl.BlockSpec(memory_space=pl.ANY))
    return aliases


def attention_back_call(layer, split, start, count, facts, kept, dc, earlier):
    seqs, rows, wide = dc.shape
    ins = [facts, kept["q"], kept["k"], kept["v"], kept["lse"], dc]
    in_specs = [pl.BlockSpec(memory_space=pltpu.SMEM)] + [blocks(x.shape, start) for x in ins[1:]]
    whole = jax.ShapeDtypeStruct((seqs, rows, wide), LOW)
    both = jax.ShapeDtypeStruct((seqs, 2, rows, wide), LOW)
    single = jax.ShapeDtypeStruct((count, 2, rows, wide), LOW)
    out_shape = [whole, both, single if split else both, jax.ShapeDtypeStruct((8, wide), FAST)]
    out_specs = [
        blocks(whole.shape, start), blocks(both.shape, start), blocks(both.shape, 0 if split else start),
        pl.BlockSpec((8, wide), lambda i: (0, 0)),
    ]
    places = (0, 1) if split else (0, 1, 2)
    aliases = chained(ins, in_specs, earlier and earlier[: len(places)], places)
    return pl.pallas_call(
        partial(attention_back_kernel, layer, start),
        grid=(count,),
        in_specs=in_specs,
        out_specs=out_specs,
        out_shape=out_shape,
        input_output_aliases=aliases,
        scratch_shapes=[pltpu.VMEM((2 * rows, rows), FAST)],
        compiler_params=pltpu.CompilerParams(vmem_limit_bytes=VMEM_MIB["attention_back"] << 20),
        cost_estimate=cost(8 * count),
        name=f"attention_back_{layer}",
    )(*ins)


def input_back_kernel(layer, split, dq, near, *refs):
    got, refs = (refs[0], refs[1:]) if split else (None, refs)
    dz1, *refs = refs
    weights, refs = refs[:3], refs[3:]
    if split:
        o_own, o_pair, o_sent, w_q, w_k, w_v, sems = refs[len(refs) - 7 :]
    else:
        o_own, w_q, w_k, w_v, sems = refs[len(refs) - 5 :]
    first = pl.program_id(0) == 0
    held = (w_q, w_k, w_v)
    copies = [pltpu.make_async_copy(weights[i].at[layer], held[i], sems.at[i]) for i in range(3)]

    @pl.when(first)
    def _():
        for copy in copies:
            copy.start()

    if split:
        dk = (near[0, 0].astype(FAST) + got[0, 0].astype(FAST)).astype(LOW)
        dv = (near[0, 1].astype(FAST) + got[0, 1].astype(FAST)).astype(LOW)
        o_pair[0, 0] = dk
        o_pair[0, 1] = dv
    else:
        dk, dv = near[0, 0], near[0, 1]

    @pl.when(first)
    def _():
        for copy in copies:
            copy.wait()

    far = mm_nt(dk, w_k[...]) + mm_nt(dv, w_v[...])
    here = dz1[0] + mm_nt(dq[0], w_q[...])
    if split:
        o_sent[0] = far.astype(LOW)
        o_own[0] = here
    else:
        o_own[0] = here + far


def input_back_call(layer, split, start, count, dq, near, got, dz1, weights, earlier):
    seqs, rows, wide = dq.shape
    ins = [dq, near]
    in_specs = [blocks(dq.shape, start), blocks(near.shape, start)]
    if split:
        ins.append(got)
        in_specs.append(blocks(got.shape, 0))
    ins += [dz1, *weights]
    in_specs += [blocks(dz1.shape, start)] + [pl.BlockSpec(memory_space=pl.ANY)] * 3
    out_shape = [jax.ShapeDtypeStruct((seqs, rows, wide), FAST)]
    out_specs = [blocks(dz1.shape, start)]
    if split:
        out_shape += [
            jax.ShapeDtypeStruct((seqs, 2, rows, wide), LOW), jax.ShapeDtypeStruct((count, rows, wide), LOW)
        ]
        out_specs += [blocks(out_shape[1].shape, start), blocks(out_shape[2].shape, 0)]
    places = (0, 1) if split else (0,)
    aliases = chained(ins, in_specs, earlier and earlier[: len(places)], places)
    return pl.pallas_call(
        partial(input_back_kernel, layer, split),
        grid=(count,),
        in_specs=in_specs,
        out_specs=out_specs,
        out_shape=out_shape,
        input_output_aliases=aliases,
        scratch_shapes=[pltpu.VMEM((wide, wide), LOW)] * 3 + [pltpu.SemaphoreType.DMA((3,))],
        compiler_params=pltpu.CompilerParams(vmem_limit_bytes=VMEM_MIB["input_back"] << 20),
        cost_estimate=cost(2 + 3 * count),
        name=f"input_back_{layer}",
    )(*ins)


def wgrad_kernel(count, place_ref, *refs):
    lefts, rights, (o_kept, o_sent) = refs[:count], refs[count : 2 * count], refs[2 * count :]
    pairs, rows = o_kept.shape[1], o_kept.shape[2]

    def write(o_even, o_odd):
        for i in range(count):
            full = mm_tn(lefts[i][...], rights[i][...])
            for pair in range(pairs):
                start = 2 * pair * rows
                o_even[i, pair] = full[start : start + rows].astype(LOW)
                o_odd[i, pair] = full[start + rows : start + 2 * rows].astype(LOW)

    @pl.when(place_ref[0] == 0)
    def _():
        write(o_kept, o_sent)

    @pl.when(place_ref[0] == 1)
    def _():
        write(o_sent, o_kept)


def wgrad_call(name, place, devices, lefts, rights, chunk):
    tokens, height = lefts[0].shape
    width = rights[0].shape[1]
    count = len(lefts)
    rows = height // devices
    steps = height // chunk
    shape = jax.ShapeDtypeStruct((count, devices // 2, rows, width), LOW)
    out_spec = pl.BlockSpec((count, devices // 2 // steps, rows, width), lambda i: (0, i, 0, 0))
    return pl.pallas_call(
        partial(wgrad_kernel, count),
        grid=(steps,),
        in_specs=[pl.BlockSpec(memory_space=pltpu.SMEM)]
        + [pl.BlockSpec((tokens, chunk), lambda i: (0, i))] * count
        + [pl.BlockSpec((tokens, width), lambda i: (0, 0))] * count,
        out_specs=[out_spec] * 2,
        out_shape=[shape] * 2,
        compiler_params=pltpu.CompilerParams(vmem_limit_bytes=VMEM_MIB["wgrad"] << 20),
        cost_estimate=cost(3 + 2 * count * height * width / 1e6),
        name=f"wgrad_{name}",
    )(place, *lefts, *rights)


def step_kernel(plan, bits, *refs):
    count = len(plan)
    for i, (outer, inner, digit) in enumerate(plan):
        kept, got = refs[2 * i], refs[2 * i + 1]
        o_kept, o_sent = refs[2 * count + 2 * i], refs[2 * count + 2 * i + 1]
        mine = bits[digit]
        for group in range(kept.shape[0]):
            for a in range(outer):
                for out, side in ((o_kept, mine), (o_sent, 1 - mine)):
                    source = pl.ds((2 * a + side) * inner, inner)
                    total = kept[group, source].astype(FAST) + got[group, source].astype(FAST)
                    out[group, a * inner : (a + 1) * inner] = total.astype(LOW)


def step_call(values, gots, plan, bits):
    steps = 1 if any(value.shape[3] % 384 for value in values) else 3
    ins, in_specs, out_specs, out_shape, moved = [], [], [], [], 0
    for value, got in zip(values, gots, strict=True):
        groups, parts, rows, columns = value.shape
        whole = pl.BlockSpec((groups, parts, rows, columns // steps), lambda i: (0, 0, 0, i))
        half = pl.BlockSpec((groups, parts // 2, rows, columns // steps), lambda i: (0, 0, 0, i))
        ins += [value, got]
        in_specs += [whole] * 2
        out_specs += [half] * 2
        out_shape += [jax.ShapeDtypeStruct((groups, parts // 2, rows, columns), LOW)] * 2
        moved += 6 * value.size
    return pl.pallas_call(
        partial(step_kernel, plan),
        grid=(steps,),
        in_specs=[pl.BlockSpec(memory_space=pltpu.SMEM)] + in_specs,
        out_specs=out_specs,
        out_shape=out_shape,
        compiler_params=pltpu.CompilerParams(vmem_limit_bytes=VMEM_MIB["step"] << 20),
        cost_estimate=cost(1 + moved / 3e6),
        name="exchange_step",
    )(bits, *ins)


def lanes_kernel(plan, bits, *refs):
    count = len(refs) // 2 - len(plan)
    ins, outs = refs[: 2 * count], refs[2 * count :]
    for lane, (outer, inner, digit) in enumerate(plan):
        mine = bits[digit]
        for out, side in ((outs[2 * lane], mine), (outs[2 * lane + 1], 1 - mine)):
            groups, parts, rows, columns = out.shape
            first = 0
            for i in range(count):
                kept, got = ins[2 * i], ins[2 * i + 1]
                wide = kept.shape[3] // len(plan)
                cols = slice(lane * wide, (lane + 1) * wide)
                for group in range(kept.shape[0]):
                    for part in range(parts):
                        source = (2 * (part // inner) + side) * inner + part % inner
                        total = kept[group, source, :, cols].astype(FAST) + got[group, source, :, cols].astype(FAST)
                        if groups == 1:
                            total = [total[:, at : at + columns] for at in range(0, wide, columns)]
                            total = total[0] if len(total) == 1 else jnp.concatenate(total, axis=0)
                            out[0, part, first : first + total.shape[0], :] = total.astype(LOW)
                        else:
                            out[first + group, part] = total.astype(LOW)
                first += rows // count if groups == 1 else kept.shape[0]


def lanes_call(values, gots, plan, bits, stacked):
    lanes = len(plan)
    parts = values[0].shape[1]
    columns = min(value.shape[3] for value in values) // lanes
    if stacked:
        shape = (1, parts // 2, sum(v.shape[2] * (v.shape[3] // lanes // columns) for v in values), columns)
    else:
        shape = (sum(v.shape[0] for v in values), parts // 2, values[0].shape[2], columns)
    whole = lambda v: pl.BlockSpec((v.shape[0], parts // 2) + v.shape[2:], lambda i: (0, i, 0, 0))
    half = pl.BlockSpec((shape[0], parts // 4) + shape[2:], lambda i: (0, i, 0, 0))
    ins = [array for pair in zip(values, gots, strict=True) for array in pair]
    return pl.pallas_call(
        partial(lanes_kernel, tuple((outer // 2, inner, digit) for outer, inner, digit in plan)),
        grid=(2,),
        in_specs=[pl.BlockSpec(memory_space=pltpu.SMEM)] + [whole(v) for v in ins],
        out_specs=[half] * (2 * lanes),
        out_shape=[jax.ShapeDtypeStruct(shape, LOW)] * (2 * lanes),
        compiler_params=pltpu.CompilerParams(vmem_limit_bytes=VMEM_MIB["lanes"] << 20),
        cost_estimate=cost(6),
        name="exchange_lanes",
    )(bits, *ins)


def finish_kernel(lanes, *refs):
    ins, (o_down, o_up, *o_four) = refs[: 4 * lanes + 6], refs[4 * lanes + 6 :]
    total = lambda i, group: ins[2 * i][group, 0].astype(FAST) + ins[2 * i + 1][group, 0].astype(FAST)
    rows_down, rows, wide = o_down.shape[1], o_up.shape[1], o_down.shape[2] // lanes
    for lane in range(lanes):
        both = total(lane, 0)
        cols = slice(lane * wide, (lane + 1) * wide)
        o_down[0, :, cols] = both[:rows_down]
        for part in range(FF_PARTS):
            at = (lane * FF_PARTS + part) * wide
            first = rows_down + part * rows
            o_up[0, :, at : at + wide] = both[first : first + rows]
        for group, out in enumerate(o_four):
            out[0, :, cols] = total(lanes + lane, group)
    o_down[1] = total(2 * lanes, 0)
    o_up[1] = total(2 * lanes + 1, 0)
    for group, out in enumerate(o_four):
        out[1] = total(2 * lanes + 2, group)


def finish_call(both, four, down_two, up_two, four_two):
    rows_down, wide = down_two.value.shape[2:]
    rows, hidden = up_two.value.shape[2:]
    sums = [*both, *four, down_two, up_two, four_two]
    square = jax.ShapeDtypeStruct((2, rows, wide), FAST)
    return pl.pallas_call(
        partial(finish_kernel, len(both)),
        out_shape=[
            jax.ShapeDtypeStruct((2, rows_down, wide), FAST), jax.ShapeDtypeStruct((2, rows, hidden), FAST),
            *[square] * four_two.value.shape[0],
        ],
        compiler_params=pltpu.CompilerParams(vmem_limit_bytes=VMEM_MIB["finish"] << 20),
        name="finish",
    )(*[array for one in sums for array in (one.value, one.got)])


def local(
    tokens, lengths, w_query, b_query, w_key, w_value, b_value, w_out, b_out, gain_one, shift_one,
    w_up, b_up, w_down, b_down, gain_two, shift_two, cotangent,
):
    seqs, rows, wide = tokens.shape
    hidden = w_up.shape[2]
    sizes = (seqs, rows, wide, hidden)
    weights = (w_query, w_key, w_value, w_out, w_up, w_down)
    vecs = vectors_call(b_query, b_value, b_out, gain_one, shift_one, b_down, gain_two, shift_two, b_up)
    devices = lax.axis_size("batch") * lax.axis_size("seq")
    seq_index = lax.axis_index("seq").astype(jnp.int32)
    spots = [(seq_index ^ flip) * rows for flip in (0, 1, 2, 3)]
    facts = jnp.concatenate([lengths, jnp.stack(spots)]).astype(jnp.int32)
    bits = jnp.stack([lax.axis_index(axis) >> bit & 1 for axis, bit in digit_list()]).astype(jnp.int32)
    flat = lambda value: value.reshape(seqs * rows, value.shape[-1])
    cuts = [(0, 2), (2, seqs - 2)]

    kept_one, kept_two, nears = None, None, []
    other = swapped_2(tokens, "seq", 0)
    for start, count in cuts:
        low, kept_one, _ = forward_call(
            0, False, start, count, facts, (tokens, 0), (tokens, 0), (other, 0), (tokens, 0), vecs, weights, kept_one, sizes
        )
        low, kept_one["r2"] = tie(low, kept_one["r2"])
        nears.append(swapped_2(low, "seq", 1))
    for near, (start, count) in zip(nears, cuts, strict=True):
        if kept_two is not None:
            near, kept_two["r2"] = tie(near, kept_two["r2"])
        else:
            near, kept_one["r2"] = tie(near, kept_one["r2"])
        far = swapped_2(near, "seq", 0)
        _, kept_two, _ = forward_call(
            1, True, start, count, facts, (kept_one["low"], 0), (near, start), (far, start),
            (kept_one["extra"], 0), vecs, weights, kept_two, sizes,
        )
    final = kept_two["low"]

    back_weights = (w_query, w_key, w_value)
    near_first, far_first, across_first = digit_orders()
    wgrad = partial(wgrad_call, place=bits, devices=devices)
    half = wide // 2

    kept = kept_two
    dy, df, dz1, da, dc, vec_two = ff_back_call(1, cotangent, kept, vecs, w_down, w_up, w_out)
    down_two = wgrad("down", lefts=[flat(kept["act"])], rights=[flat(dy)], chunk=wide)
    down_two, dc = Sum.begin(down_two, near_first, bits, dc)
    att = attention_back_call(1, True, 0, 2, facts, kept, dc, None)
    att = join(att, down_two)
    vec_q = att[3]
    (dc, far) = advance((dc, att[2]), down_two)
    got = swapped_2(far, "seq", 0)
    att = attention_back_call(1, True, 2, seqs - 2, facts, kept, dc, att)
    vec_q += att[3]
    att, got, df = tie(att, got, df)
    got_late = swapped_2(att[2], "seq", 0)
    ends = input_back_call(1, True, 0, 2, att[0], att[1], got, dz1, back_weights, None)
    ends, df = tie(ends, df)
    arrived = [swapped_2(ends[2], "seq", 1)]
    up_two = wgrad("up", lefts=[flat(kept["hid"])], rights=[flat(df)], chunk=half)
    up_two, (got_late, dz1) = Sum.begin(up_two, near_first, bits, (got_late, dz1))
    ends = input_back_call(1, True, 2, seqs - 2, att[0], att[1], got_late, dz1, back_weights, ends)
    ends = tie(*ends)
    arrived.append(swapped_2(ends[2], "seq", 1))
    ends = join(ends, up_two, down_two)
    pair = advance(ends[1], up_two, down_two)
    near = kept["extra"]
    four_two = wgrad(
        "four",
        lefts=[flat(kept["ctx"]), flat(kept_one["low"]), flat(near), flat(near)],
        rights=[flat(da), flat(att[0]), flat(pair[:, 0]), flat(pair[:, 1])],
        chunk=half,
    )
    four_two, arrived = Sum.begin(four_two, across_first, bits, arrived)
    vec_two = (vec_two, vec_q)
    middle = ends[0] + jnp.concatenate(arrived).astype(FAST)

    kept = kept_one
    ff = ff_back_call(0, middle, kept, vecs, w_down, w_up, w_out)
    dy, df, dz1, da, dc, vec_one = join(ff, down_two, four_two)
    dy = advance(dy, down_two, four_two)
    down_one = wgrad("down", lefts=[flat(kept["act"])], rights=[flat(dy)], chunk=wide)
    down_one, df = Sum.begin(down_one, near_first, bits, df)
    up_one = wgrad("up", lefts=[flat(kept["hid"])], rights=[flat(df)], chunk=half)
    up_one, dc = join((up_one, dc), down_one, down_two, up_two)
    up_one, dc = Sum.begin(up_one, near_first, bits, dc)
    dc = advance(dc, down_two, up_two)
    att = attention_back_call(0, False, 0, 1, facts, kept, dc, None)
    vec_q = att[3]
    att, dc = join((att, dc), up_one, up_two, down_two)
    lanes_one, dc = lanes_of(dc, down_one, up_one, stacked=True)
    dc = advance(dc, up_two)
    att = attention_back_call(0, False, 1, seqs - 1, facts, kept, dc, att)
    vec_q += att[3]
    early = [four_two, up_two, down_two]
    att, da, vec_q = join((att, da, vec_q), *lanes_one, *early)
    vectors = Whole([(vec_one, vec_q), vec_two])
    far, da = advance((att[2], da), *lanes_one, *early)
    far, da = vectors.send((far, da))
    got = swapped_2(far, "seq", 0)
    rest_one = wgrad("rest", lefts=[flat(kept["ctx"]), flat(tokens)], rights=[flat(da), flat(att[0])], chunk=half)
    rest_one, got = join((rest_one, got), vectors)
    rest_one, got = Sum.begin(rest_one, across_first, bits, got)
    got = vectors.send(got)
    pair = (att[1].astype(FAST) + got.astype(FAST)).astype(LOW)
    pairs_one = wgrad("pair", lefts=[flat(tokens)] * 2, rights=[flat(pair[:, 0]), flat(pair[:, 1])], chunk=half)
    pairs_one, dz1 = join((pairs_one, dz1), *lanes_one, rest_one, vectors, *early)
    pairs_one, dz1 = Sum.begin(pairs_one, near_first, bits, dz1)
    dz1 = advance(dz1, *lanes_one, *early)
    dz1 = vectors.send(dz1)
    ends = input_back_call(0, False, 0, 2, att[0], pair, None, dz1, back_weights, None)
    (dz1, ends) = join((dz1, ends), *lanes_one, pairs_one, vectors, *early)
    last_one, dz1 = lanes_of(dz1, rest_one, pairs_one, stacked=False)
    dz1 = advance(dz1, *lanes_one, *early)
    dz1 = vectors.send(dz1)
    ends = input_back_call(0, False, 2, seqs - 2, att[0], pair, None, dz1, back_weights, ends)
    live = [*last_one, *lanes_one, *early]
    result = join(ends[0], *live, vectors)
    while any(one.order for one in live):
        result = advance(result, *live)
        result = vectors.send(result)
        result = join(result, *live, vectors)
    vectors.send(())
    sums = finish_call(lanes_one, last_one, down_two, up_two, four_two)
    return (final, result) + gathered(sums, vectors.value, devices)


def tie(*values):
    return lax.optimization_barrier(values)


def digit_list():
    return [
        (axis, bit) for axis in ("seq", "batch") for bit in range(lax.axis_size(axis).bit_length() - 1)
    ]


def digit_orders():
    low = lax.axis_size("seq").bit_length() - 1
    high = lax.axis_size("batch").bit_length() - 1
    core, across = ("seq", 0), [("seq", bit) for bit in range(1, low)]
    near, far, late = [("batch", 0)], [("batch", 1)], [("batch", bit) for bit in range(2, high)]
    return (
        [core] + near + far + across + late,
        [core] + far + near + across + late,
        [core] + across + near + far + late,
    )


def lane_orders():
    digits = digit_list()[1:]
    across, near, far, late = digits[:1], digits[1:2], digits[2:3], digits[3:]
    return across + near + far + late, near + far + across + late, far + across + near + late


def join(values, *sums):
    live = [one for one in sums if one.got is not None]
    values, gots = lax.optimization_barrier((values, [one.got for one in live]))
    for one, got in zip(live, gots, strict=True):
        one.got = got
    return values


def advance(hold, *sums):
    live = [one for one in sums if one.order]
    if not live:
        return hold
    plan, routes = [], []
    for one in live:
        digit = one.order.pop(0)
        above = one.digits.index(digit)
        one.digits.remove(digit)
        plan.append((1 << above, 1 << len(one.digits) - above, digit_list().index(digit)))
        routes.append(digit)
    halves = step_call([one.value for one in live], [one.got for one in live], tuple(plan), live[0].bits)
    outs, hold = tie(halves[1::2], hold)
    for one, value, out, route in zip(live, halves[::2], outs, routes, strict=True):
        one.value = value
        one.got = swapped_2(out, *route)
    return hold


def lanes_of(hold, *sums, stacked):
    digits = sums[0].digits
    plan, lanes = [], []
    for order in lane_orders():
        above = digits.index(order[0])
        plan.append((1 << above, 1 << len(digits) - 1 - above, digit_list().index(order[0])))
    halves = lanes_call([one.value for one in sums], [one.got for one in sums], tuple(plan), sums[0].bits, stacked)
    outs, hold = tie(halves[1::2], hold)
    for value, out, order in zip(halves[::2], outs, lane_orders(), strict=True):
        one = Sum()
        one.value, one.bits, one.order = value, sums[0].bits, list(order[1:])
        one.digits = [digit for digit in digits if digit != order[0]]
        one.got = swapped_2(out, *order[0])
        lanes.append(one)
    return lanes, hold


class Sum:
    @classmethod
    def begin(cls, halves, order, bits, hold):
        one = cls()
        (one.value, out), hold = tie(halves, hold)
        one.bits = bits
        one.digits = list(reversed(digit_list()))[:-1]
        one.order = list(order[1:])
        one.got = swapped_2(out, *order[0])
        return one, hold


class Whole:
    def __init__(self, layers):
        rows = [jnp.concatenate([vec_low[:2], vec[2:]]) for vec, vec_low in layers]
        self.value = jnp.stack(rows)
        self.got = None
        self.order = digit_list()

    def send(self, hold):
        if self.got is not None:
            self.value = self.value + self.got
            self.got = None
        if self.order:
            self.value, hold = tie(self.value, hold)
            self.got = swapped_2(self.value, *self.order.pop(0))
        return hold


VECTORS = (1, 4, 6, 7, 8, 12, 13, 14)


def gathered(sums, vectors, devices):
    outs = [None] * 15
    for which, value in zip((11, 9, 5, 0, 2, 3), sums, strict=True):
        outs[which] = value
    mine = lax.axis_index("batch") * lax.axis_size("seq") + lax.axis_index("seq")
    width = vectors.shape[2] // devices
    small = lax.dynamic_slice_in_dim(vectors[:, :8], mine * width, width, axis=2)
    for place, which in enumerate(VECTORS):
        outs[which] = small[:, place]
    large = vectors[:, 8:].reshape(vectors.shape[0], -1)
    width = large.shape[1] // devices
    outs[10] = lax.dynamic_slice_in_dim(large, mine * width, width, axis=1)
    return tuple(outs)


def solution(mesh):
    in_specs = (
        P("batch", "seq", None),
        P("batch"),
        P(),
        P(),
        P(),
        P(),
        P(),
        P(),
        P(),
        P(),
        P(),
        P(),
        P(),
        P(),
        P(),
        P(),
        P(),
        P("batch", "seq", None),
    )
    out_specs = (
        P("batch", "seq", None),
        P("batch", "seq", None),
        P(None, ("batch", "seq"), None),
        P(None, ("batch", "seq")),
        P(None, ("batch", "seq"), None),
        P(None, ("batch", "seq"), None),
        P(None, ("batch", "seq")),
        P(None, ("batch", "seq"), None),
        P(None, ("batch", "seq")),
        P(None, ("batch", "seq")),
        P(None, ("batch", "seq")),
        P(None, ("batch", "seq"), None),
        P(None, ("batch", "seq")),
        P(None, ("batch", "seq"), None),
        P(None, ("batch", "seq")),
        P(None, ("batch", "seq")),
        P(None, ("batch", "seq")),
    )
    return jax.shard_map(local, mesh=mesh, in_specs=in_specs, out_specs=out_specs, check_vma=False)
```

```python
from functools import partial

import jax
import jax.numpy as jnp
from jax import lax
from jax.experimental import pallas as pl
from jax.experimental.pallas import tpu as pltpu
from jax.sharding import PartitionSpec as P

HEADS = 12
HEAD_DIM = 64


EPSILON = 1e-06
MASKED = -1e30


def swapped_2(value, axis, bit):
    return lax.ppermute(value, axis, [(i, i ^ 1 << bit) for i in range(lax.axis_size(axis))])


TOKENS_MINOR = (((1,), (1,)), ((), ()))
TOKENS_MAJOR = (((0,), (0,)), ((), ()))
ROOT_HALF = 0.7071067811865476
ROOT_TAU = 0.3989422804014327
VMEM_MIB = dict(forward=60, ff_back=28, attention_back=12, input_back=14, wgrad=12, step=16, lanes=20, finish=12)
FF_PARTS = 4
FACTS_TAIL = 4
FAST = jnp.float32
LOW = jnp.bfloat16


COST_SCALE = 10


def cost(microseconds):
    return pl.CostEstimate(flops=int(microseconds * COST_SCALE * 1.15e9), bytes_accessed=1, transcendentals=0)


def mm(left, right):
    return jnp.dot(left, right, preferred_element_type=FAST)


def mm_nt(left, right):
    return lax.dot_general(left, right, TOKENS_MINOR, preferred_element_type=FAST)


def mm_tn(left, right):
    return lax.dot_general(left, right, TOKENS_MAJOR, preferred_element_type=FAST)


def vectors_kernel(*refs):
    *ins, out = refs
    for place, ref in enumerate(ins[:-1]):
        out[:, place, :] = ref[...].astype(FAST)
    wide = out.shape[2]
    for part in range(FF_PARTS):
        out[:, len(ins) - 1 + part, :] = ins[-1][:, part * wide : (part + 1) * wide].astype(FAST)


def vectors_call(*vectors):
    layers, wide = vectors[0].shape
    return pl.pallas_call(
        vectors_kernel,
        out_shape=jax.ShapeDtypeStruct((layers, len(vectors) - 1 + FF_PARTS, wide), FAST),
        name="vectors",
    )(*vectors)


def row_norm(value):
    average = jnp.mean(value, axis=-1, keepdims=True)
    centred = value - average
    inverse_scale = lax.rsqrt(jnp.mean(centred * centred, axis=-1, keepdims=True) + EPSILON)
    return centred * inverse_scale, inverse_scale


def gelu_and_slope(value):
    size = jnp.abs(value)
    near = 1.0 / (1.0 + (0.3275911 * ROOT_HALF) * size)
    bell = jnp.exp(value * value * -0.5)
    poly = near * (
        0.127414796
        + near * (-0.142248368 + near * (0.7107068705 + near * (-0.7265760135 + near * 0.5307027145)))
    )
    tail = poly * bell
    below = jnp.where(value >= 0, 1.0 - tail, tail)
    return value * below, below + value * (bell * ROOT_TAU)


VEC_ROWS = dict(b_query=0, b_value=1, b_out=2, gain_one=3, shift_one=4, b_down=5, gain_two=6, shift_two=7)
VEC_UP = 8


def forward_kernel(layer, swapped, start, facts, own, near, far, top, vecs, *refs):
    weights, refs = refs[:6], refs[6:]
    refs = refs[len(refs) - 25 :]
    outs, scratch = refs[:16], refs[16:]
    (
        o_sent, o_extra, o_low, o_q, o_k, o_v, o_lse, o_ctx, o_n1, o_r1, o_hid, o_act, o_slope, o_n2, o_r2, o_done,
    ) = outs
    o_top = o_near = o_extra
    w_q, w_k, w_v, w_o, w_up, w_down, mix, ctx, sems = scratch
    first = pl.program_id(0) == 0
    held = (w_q, w_k, w_v, w_o, w_up, w_down)
    copies = [
        pltpu.make_async_copy(weights[i].at[layer], held[i], sems.at[i]) for i in range(6)
    ]

    @pl.when(first)
    def _():
        for copy in copies:
            copy.start()

    def ready(*which):
        @pl.when(first)
        def _():
            for i in which:
                copies[i].wait()

    def vec(name):
        row = VEC_ROWS[name]
        return vecs[layer, row : row + 1, :]

    rows = own.shape[1]
    x = own[0]
    ready(0, 1, 2)
    queries = (mm(x, w_q[...]) + vec("b_query")).astype(LOW)
    o_q[0] = queries * jnp.asarray(HEAD_DIM**-0.5, LOW)
    for part, source in ((0, near), (1, far)):
        block = source[0]
        o_k[0, part * rows : (part + 1) * rows, :] = mm(block, w_k[...]).astype(LOW)
        o_v[0, part * rows : (part + 1) * rows, :] = (mm(block, w_v[...]) + vec("b_value")).astype(LOW)
    spots = facts.shape[0] - FACTS_TAIL + 2 * layer
    length = facts[start + pl.program_id(0)]
    lane = lax.broadcasted_iota(jnp.int32, (1, 2 * rows), 1)
    place = jnp.where(lane < rows, facts[spots] + lane, facts[spots + 1] + (lane - rows))
    bias = jnp.where(place < length, 0.0, MASKED).astype(FAST)
    lower = lax.broadcasted_iota(jnp.int32, (1, 128), 1) < HEAD_DIM
    column = lax.broadcasted_iota(jnp.int32, (1, 128), 1)
    logs = jnp.zeros((rows, 128), FAST)
    for pair in range(HEADS // 2):
        lanes = slice(pair * 128, pair * 128 + 128)
        q_pair, k_pair, v_pair = o_q[0, :, lanes], o_k[0, :, lanes], o_v[0, :, lanes]
        got = []
        for side in range(2):
            mask = lower if side == 0 else ~lower
            q_one = jnp.where(mask, q_pair, jnp.zeros_like(q_pair))
            scores = mm_nt(q_one, k_pair) + bias
            high = jnp.max(scores, axis=-1, keepdims=True)
            weight = jnp.exp(scores - high)
            total = jnp.sum(weight, axis=-1, keepdims=True)
            got.append(mm(weight.astype(LOW), v_pair) * (1.0 / total))
            logs = jnp.where(column == 2 * pair + side, high + jnp.log(total), logs)
        ctx[:, lanes] = jnp.where(lower, got[0], got[1]).astype(LOW)
    o_lse[0] = logs.T[:16, :]
    o_ctx[0] = ctx[...]
    ready(3)
    branch = mm(ctx[...], w_o[...]) + vec("b_out") + top[0].astype(FAST)
    n1, r1 = row_norm(branch)
    o_n1[0] = n1.astype(LOW)
    o_r1[0] = r1
    hidden = n1 * vec("gain_one") + vec("shift_one")
    hid = hidden.astype(LOW)
    o_hid[0] = hid
    mix[...] = hidden + vec("b_down")
    ready(4, 5)
    width = w_up.shape[1] // FF_PARTS
    for part in range(FF_PARTS):
        cols = slice(part * width, (part + 1) * width)
        pre = mm(hid, w_up[:, cols]) + vecs[layer, VEC_UP + part : VEC_UP + part + 1, :]
        act, slope = gelu_and_slope(pre)
        act = act.astype(LOW)
        o_act[0, :, cols] = act
        o_slope[0, :, cols] = slope.astype(LOW)
        mix[...] += mm(act, w_down[cols, :])
    n2, r2 = row_norm(mix[...])
    o_n2[0] = n2.astype(LOW)
    o_r2[0] = r2
    result = n2 * vec("gain_two") + vec("shift_two")
    if not swapped:
        o_top[0] = result
    low = result.astype(LOW)
    o_sent[0] = low
    if swapped:
        o_near[0] = near[0]
    o_low[0] = low
    o_done[...] = jnp.zeros_like(o_done)


KEPT = ("extra", "low", "q", "k", "v", "lse", "ctx", "n1", "r1", "hid", "act", "slope", "n2", "r2")


def forward_call(layer, swapped, start, count, facts, own, near, far, top, vecs, weights, kept, sizes):
    seqs, rows, wide, hidden = sizes

    def taken(source):
        array, offset = source
        return pl.BlockSpec((1,) + array.shape[1:], lambda i: (start - offset + i, 0, 0))

    shapes = dict(
        extra=((rows, wide), LOW if swapped else FAST), low=((rows, wide), LOW),
        q=((rows, wide), LOW), k=((2 * rows, wide), LOW), v=((2 * rows, wide), LOW), lse=((16, rows), FAST),
        ctx=((rows, wide), LOW), n1=((rows, wide), LOW), r1=((rows, 1), FAST), hid=((rows, wide), LOW),
        act=((rows, hidden), LOW), slope=((rows, hidden), LOW), n2=((rows, wide), LOW), r2=((rows, 1), FAST),
    )
    out_shape = [jax.ShapeDtypeStruct((count, rows, wide), LOW)] + [
        jax.ShapeDtypeStruct((seqs,) + shapes[name][0], shapes[name][1]) for name in KEPT
    ]
    out_specs = [pl.BlockSpec((1, rows, wide), lambda i: (i, 0, 0))] + [
        pl.BlockSpec((1,) + shapes[name][0], lambda i: (start + i, 0, 0)) for name in KEPT
    ]
    out_shape.append(jax.ShapeDtypeStruct((8, 128), FAST))
    out_specs.append(pl.BlockSpec((8, 128), lambda i: (0, 0)))
    any_spec = pl.BlockSpec(memory_space=pl.ANY)
    ins = [facts, own[0], near[0], far[0], top[0], vecs, *weights]
    in_specs = [
        pl.BlockSpec(memory_space=pltpu.SMEM), taken(own), taken(near), taken(far), taken(top),
        pl.BlockSpec(vecs.shape, lambda i: (0, 0, 0)),
    ] + [any_spec] * 6
    aliases = {}
    if kept is not None:
        for place, name in enumerate(KEPT):
            aliases[len(ins) + place] = 1 + place
        ins += [kept[name] for name in KEPT]
        in_specs += [any_spec] * len(KEPT)
    got = pl.pallas_call(
        partial(forward_kernel, layer, swapped, start),
        grid=(count,),
        in_specs=in_specs,
        out_specs=out_specs,
        out_shape=out_shape,
        input_output_aliases=aliases,
        scratch_shapes=[
            pltpu.VMEM((wide, wide), LOW), pltpu.VMEM((wide, wide), LOW), pltpu.VMEM((wide, wide), LOW),
            pltpu.VMEM((wide, wide), LOW), pltpu.VMEM((wide, hidden), LOW), pltpu.VMEM((hidden, wide), LOW),
            pltpu.VMEM((rows, wide), FAST), pltpu.VMEM((rows, wide), LOW), pltpu.SemaphoreType.DMA((6,)),
        ],
        compiler_params=pltpu.CompilerParams(vmem_limit_bytes=VMEM_MIB["forward"] << 20),
        cost_estimate=cost(14 * count),
        name=f"layer_forward_{layer}",
    )(*ins)
    return got[0], dict(zip(KEPT, got[1:-1], strict=True)), got[-1]


def norm_back_rows(grad, normed, inverse_scale, gain):
    dn = grad * gain
    return inverse_scale * (
        dn - jnp.mean(dn, axis=-1, keepdims=True) - normed * jnp.mean(dn * normed, axis=-1, keepdims=True)
    )


def column_sum(value):
    return jnp.sum(value.astype(FAST), axis=0, keepdims=True)


def ff_back_kernel(layer, top_grad, n2, r2, slope, n1, r1, vecs, *refs):
    weights, refs = refs[:3], refs[3:]
    o_dy, o_df, o_dz1, o_da, o_dc, o_vec, w_down, w_up, w_o, mix, sems = refs
    first = pl.program_id(0) == 0
    held = (w_down, w_up, w_o)
    copies = [pltpu.make_async_copy(weights[i].at[layer], held[i], sems.at[i]) for i in range(3)]

    @pl.when(first)
    def _():
        for copy in copies:
            copy.start()
        o_vec[...] = jnp.zeros_like(o_vec)

    def ready(which):
        @pl.when(first)
        def _():
            copies[which].wait()

    def vec(name):
        row = VEC_ROWS[name]
        return vecs[layer, row : row + 1, :]

    def add(row, value):
        o_vec[row : row + 1, :] += value

    grad = top_grad[0].astype(FAST)
    normed = n2[0].astype(FAST)
    add(VEC_ROWS["gain_two"], column_sum(grad * normed))
    add(VEC_ROWS["shift_two"], column_sum(grad))
    dz2 = norm_back_rows(grad, normed, r2[0], vec("gain_two"))
    dy = dz2.astype(LOW)
    o_dy[0] = dy
    add(VEC_ROWS["b_down"], column_sum(dy))
    mix[...] = dz2
    ready(0)
    width = w_up.shape[1] // FF_PARTS
    for part in range(FF_PARTS):
        cols = slice(part * width, (part + 1) * width)
        if part == 0:
            ready(1)
        df = (mm_nt(dy, w_down[cols, :]) * slope[0, :, cols].astype(FAST)).astype(LOW)
        o_df[0, :, cols] = df
        add(VEC_UP + part, column_sum(df))
        mix[...] += mm_nt(df, w_up[:, cols])
    grad = mix[...]
    normed = n1[0].astype(FAST)
    add(VEC_ROWS["gain_one"], column_sum(grad * normed))
    add(VEC_ROWS["shift_one"], column_sum(grad))
    dz1 = norm_back_rows(grad, normed, r1[0], vec("gain_one"))
    o_dz1[0] = dz1
    da = dz1.astype(LOW)
    o_da[0] = da
    add(VEC_ROWS["b_out"], column_sum(da))
    ready(2)
    o_dc[0] = mm_nt(da, w_o[...]).astype(LOW)


def ff_back_call(layer, top_grad, kept, vecs, w_down, w_up, w_out):
    seqs, rows, wide = top_grad.shape
    hidden = w_up.shape[2]
    ins = [top_grad, kept["n2"], kept["r2"], kept["slope"], kept["n1"], kept["r1"], vecs, w_down, w_up, w_out]
    each = lambda shape: pl.BlockSpec((1,) + tuple(shape[1:]), lambda i: (i, 0, 0))
    any_spec = pl.BlockSpec(memory_space=pl.ANY)
    in_specs = [each(x.shape) for x in ins[:6]] + [pl.BlockSpec(vecs.shape, lambda i: (0, 0, 0))] + [any_spec] * 3
    out_shape = [
        jax.ShapeDtypeStruct((seqs, rows, wide), LOW), jax.ShapeDtypeStruct((seqs, rows, hidden), LOW),
        jax.ShapeDtypeStruct((seqs, rows, wide), FAST), jax.ShapeDtypeStruct((seqs, rows, wide), LOW),
        jax.ShapeDtypeStruct((seqs, rows, wide), LOW), jax.ShapeDtypeStruct((vecs.shape[1], wide), FAST),
    ]
    out_specs = [each(x.shape) for x in out_shape[:5]] + [pl.BlockSpec(out_shape[5].shape, lambda i: (0, 0))]
    return pl.pallas_call(
        partial(ff_back_kernel, layer),
        grid=(seqs,),
        in_specs=in_specs,
        out_specs=out_specs,
        out_shape=out_shape,
        scratch_shapes=[
            pltpu.VMEM((hidden, wide), LOW), pltpu.VMEM((wide, hidden), LOW), pltpu.VMEM((wide, wide), LOW),
            pltpu.VMEM((rows, wide), FAST), pltpu.SemaphoreType.DMA((3,)),
        ],
        compiler_params=pltpu.CompilerParams(vmem_limit_bytes=VMEM_MIB["ff_back"] << 20),
        cost_estimate=cost(19),
        name=f"ff_back_{layer}",
    )(*ins)


def attention_back_kernel(layer, start, facts, q, k, v, lse, dc, *refs):
    o_dq, o_near, o_far, o_vec, bias = refs[len(refs) - 5 :]
    rows, wide = q.shape[1], q.shape[2]

    @pl.when(pl.program_id(0) == 0)
    def _():
        o_vec[...] = jnp.zeros_like(o_vec)

    spots = facts.shape[0] - FACTS_TAIL + 2 * layer
    length = facts[start + pl.program_id(0)]
    key = lax.broadcasted_iota(jnp.int32, (2 * rows, rows), 0)
    place = jnp.where(key < rows, facts[spots] + key, facts[spots + 1] + (key - rows))
    bias[...] = jnp.where(place < length, 0.0, MASKED).astype(FAST)
    lower = lax.broadcasted_iota(jnp.int32, (1, 128), 1) < HEAD_DIM
    for pair in range(HEADS // 2):
        lanes = slice(pair * 128, pair * 128 + 128)
        q_pair, k_pair, v_pair, dc_pair = q[0, :, lanes], k[0, :, lanes], v[0, :, lanes], dc[0, :, lanes]
        dk = dv = None
        dq = []
        for side in range(2):
            one = 2 * pair + side
            mask = lower if side == 0 else ~lower
            q_one = jnp.where(mask, q_pair, jnp.zeros_like(q_pair))
            dc_one = jnp.where(mask, dc_pair, jnp.zeros_like(dc_pair))
            weight = jnp.exp(mm_nt(k_pair, q_one) + bias[...] - lse[0, one : one + 1, :])
            product = weight * mm_nt(v_pair, dc_one)
            ds = (product - weight * jnp.sum(product, axis=0, keepdims=True)).astype(LOW)
            dv_one = mm(weight.astype(LOW), dc_one)
            dk_one = mm(ds, q_one)
            dv = dv_one if dv is None else dv + dv_one
            dk = dk_one if dk is None else dk + dk_one
            dq.append(mm_tn(k_pair, ds)[side * HEAD_DIM : (side + 1) * HEAD_DIM])
        dq_pair = (jnp.concatenate(dq, axis=0).T * HEAD_DIM**-0.5).astype(LOW)
        o_dq[0, :, lanes] = dq_pair
        o_vec[0:1, lanes] += column_sum(dq_pair)
        o_vec[1:2, lanes] += column_sum(dv)
        o_near[0, 0, :, lanes] = dk[:rows].astype(LOW)
        o_far[0, 0, :, lanes] = dk[rows:].astype(LOW)
        o_near[0, 1, :, lanes] = dv[:rows].astype(LOW)
        o_far[0, 1, :, lanes] = dv[rows:].astype(LOW)


def blocks(shape, start):
    rest = len(shape) - 1
    return pl.BlockSpec((1,) + tuple(shape[1:]), lambda i: (start + i,) + (0,) * rest)


def chained(ins, in_specs, earlier, places):
    aliases = {}
    if earlier is not None:
        for array, place in zip(earlier, places, strict=True):
            aliases[len(ins)] = place
            ins.append(array)
            in_specs.append(pl.BlockSpec(memory_space=pl.ANY))
    return aliases


def attention_back_call(layer, split, start, count, facts, kept, dc, earlier):
    seqs, rows, wide = dc.shape
    ins = [facts, kept["q"], kept["k"], kept["v"], kept["lse"], dc]
    in_specs = [pl.BlockSpec(memory_space=pltpu.SMEM)] + [blocks(x.shape, start) for x in ins[1:]]
    whole = jax.ShapeDtypeStruct((seqs, rows, wide), LOW)
    both = jax.ShapeDtypeStruct((seqs, 2, rows, wide), LOW)
    single = jax.ShapeDtypeStruct((count, 2, rows, wide), LOW)
    out_shape = [whole, both, single if split else both, jax.ShapeDtypeStruct((8, wide), FAST)]
    out_specs = [
        blocks(whole.shape, start), blocks(both.shape, start), blocks(both.shape, 0 if split else start),
        pl.BlockSpec((8, wide), lambda i: (0, 0)),
    ]
    places = (0, 1) if split else (0, 1, 2)
    aliases = chained(ins, in_specs, earlier and earlier[: len(places)], places)
    return pl.pallas_call(
        partial(attention_back_kernel, layer, start),
        grid=(count,),
        in_specs=in_specs,
        out_specs=out_specs,
        out_shape=out_shape,
        input_output_aliases=aliases,
        scratch_shapes=[pltpu.VMEM((2 * rows, rows), FAST)],
        compiler_params=pltpu.CompilerParams(vmem_limit_bytes=VMEM_MIB["attention_back"] << 20),
        cost_estimate=cost(8 * count),
        name=f"attention_back_{layer}",
    )(*ins)


def input_back_kernel(layer, split, dq, near, *refs):
    got, refs = (refs[0], refs[1:]) if split else (None, refs)
    dz1, *refs = refs
    weights, refs = refs[:3], refs[3:]
    if split:
        o_own, o_pair, o_sent, w_q, w_k, w_v, sems = refs[len(refs) - 7 :]
    else:
        o_own, w_q, w_k, w_v, sems = refs[len(refs) - 5 :]
    first = pl.program_id(0) == 0
    held = (w_q, w_k, w_v)
    copies = [pltpu.make_async_copy(weights[i].at[layer], held[i], sems.at[i]) for i in range(3)]

    @pl.when(first)
    def _():
        for copy in copies:
            copy.start()

    if split:
        dk = (near[0, 0].astype(FAST) + got[0, 0].astype(FAST)).astype(LOW)
        dv = (near[0, 1].astype(FAST) + got[0, 1].astype(FAST)).astype(LOW)
        o_pair[0, 0] = dk
        o_pair[0, 1] = dv
    else:
        dk, dv = near[0, 0], near[0, 1]

    @pl.when(first)
    def _():
        for copy in copies:
            copy.wait()

    far = mm_nt(dk, w_k[...]) + mm_nt(dv, w_v[...])
    here = dz1[0] + mm_nt(dq[0], w_q[...])
    if split:
        o_sent[0] = far.astype(LOW)
        o_own[0] = here
    else:
        o_own[0] = here + far


def input_back_call(layer, split, start, count, dq, near, got, dz1, weights, earlier):
    seqs, rows, wide = dq.shape
    ins = [dq, near]
    in_specs = [blocks(dq.shape, start), blocks(near.shape, start)]
    if split:
        ins.append(got)
        in_specs.append(blocks(got.shape, 0))
    ins += [dz1, *weights]
    in_specs += [blocks(dz1.shape, start)] + [pl.BlockSpec(memory_space=pl.ANY)] * 3
    out_shape = [jax.ShapeDtypeStruct((seqs, rows, wide), FAST)]
    out_specs = [blocks(dz1.shape, start)]
    if split:
        out_shape += [
            jax.ShapeDtypeStruct((seqs, 2, rows, wide), LOW), jax.ShapeDtypeStruct((count, rows, wide), LOW)
        ]
        out_specs += [blocks(out_shape[1].shape, start), blocks(out_shape[2].shape, 0)]
    places = (0, 1) if split else (0,)
    aliases = chained(ins, in_specs, earlier and earlier[: len(places)], places)
    return pl.pallas_call(
        partial(input_back_kernel, layer, split),
        grid=(count,),
        in_specs=in_specs,
        out_specs=out_specs,
        out_shape=out_shape,
        input_output_aliases=aliases,
        scratch_shapes=[pltpu.VMEM((wide, wide), LOW)] * 3 + [pltpu.SemaphoreType.DMA((3,))],
        compiler_params=pltpu.CompilerParams(vmem_limit_bytes=VMEM_MIB["input_back"] << 20),
        cost_estimate=cost(2 + 3 * count),
        name=f"input_back_{layer}",
    )(*ins)


def wgrad_kernel(count, place_ref, *refs):
    lefts, rights, (o_kept, o_sent) = refs[:count], refs[count : 2 * count], refs[2 * count :]
    pairs, rows = o_kept.shape[1], o_kept.shape[2]

    def write(o_even, o_odd):
        for i in range(count):
            full = mm_tn(lefts[i][...], rights[i][...])
            for pair in range(pairs):
                start = 2 * pair * rows
                o_even[i, pair] = full[start : start + rows].astype(LOW)
                o_odd[i, pair] = full[start + rows : start + 2 * rows].astype(LOW)

    @pl.when(place_ref[0] == 0)
    def _():
        write(o_kept, o_sent)

    @pl.when(place_ref[0] == 1)
    def _():
        write(o_sent, o_kept)


def wgrad_call(name, place, devices, lefts, rights, chunk):
    tokens, height = lefts[0].shape
    width = rights[0].shape[1]
    count = len(lefts)
    rows = height // devices
    steps = height // chunk
    shape = jax.ShapeDtypeStruct((count, devices // 2, rows, width), LOW)
    out_spec = pl.BlockSpec((count, devices // 2 // steps, rows, width), lambda i: (0, i, 0, 0))
    return pl.pallas_call(
        partial(wgrad_kernel, count),
        grid=(steps,),
        in_specs=[pl.BlockSpec(memory_space=pltpu.SMEM)]
        + [pl.BlockSpec((tokens, chunk), lambda i: (0, i))] * count
        + [pl.BlockSpec((tokens, width), lambda i: (0, 0))] * count,
        out_specs=[out_spec] * 2,
        out_shape=[shape] * 2,
        compiler_params=pltpu.CompilerParams(vmem_limit_bytes=VMEM_MIB["wgrad"] << 20),
        cost_estimate=cost(3 + 2 * count * height * width / 1e6),
        name=f"wgrad_{name}",
    )(place, *lefts, *rights)


def step_kernel(plan, bits, *refs):
    count = len(plan)
    for i, (outer, inner, digit) in enumerate(plan):
        kept, got = refs[2 * i], refs[2 * i + 1]
        o_kept, o_sent = refs[2 * count + 2 * i], refs[2 * count + 2 * i + 1]
        mine = bits[digit]
        for group in range(kept.shape[0]):
            for a in range(outer):
                for out, side in ((o_kept, mine), (o_sent, 1 - mine)):
                    source = pl.ds((2 * a + side) * inner, inner)
                    total = kept[group, source].astype(FAST) + got[group, source].astype(FAST)
                    out[group, a * inner : (a + 1) * inner] = total.astype(LOW)


def step_call(values, gots, plan, bits):
    steps = 1 if any(value.shape[3] % 384 for value in values) else 3
    ins, in_specs, out_specs, out_shape, moved = [], [], [], [], 0
    for value, got in zip(values, gots, strict=True):
        groups, parts, rows, columns = value.shape
        whole = pl.BlockSpec((groups, parts, rows, columns // steps), lambda i: (0, 0, 0, i))
        half = pl.BlockSpec((groups, parts // 2, rows, columns // steps), lambda i: (0, 0, 0, i))
        ins += [value, got]
        in_specs += [whole] * 2
        out_specs += [half] * 2
        out_shape += [jax.ShapeDtypeStruct((groups, parts // 2, rows, columns), LOW)] * 2
        moved += 6 * value.size
    return pl.pallas_call(
        partial(step_kernel, plan),
        grid=(steps,),
        in_specs=[pl.BlockSpec(memory_space=pltpu.SMEM)] + in_specs,
        out_specs=out_specs,
        out_shape=out_shape,
        compiler_params=pltpu.CompilerParams(vmem_limit_bytes=VMEM_MIB["step"] << 20),
        cost_estimate=cost(1 + moved / 3e6),
        name="exchange_step",
    )(bits, *ins)


def lanes_kernel(plan, bits, *refs):
    count = len(refs) // 2 - len(plan)
    ins, outs = refs[: 2 * count], refs[2 * count :]
    for lane, (outer, inner, digit) in enumerate(plan):
        mine = bits[digit]
        for out, side in ((outs[2 * lane], mine), (outs[2 * lane + 1], 1 - mine)):
            groups, parts, rows, columns = out.shape
            first = 0
            for i in range(count):
                kept, got = ins[2 * i], ins[2 * i + 1]
                wide = kept.shape[3] // len(plan)
                cols = slice(lane * wide, (lane + 1) * wide)
                for group in range(kept.shape[0]):
                    for part in range(parts):
                        source = (2 * (part // inner) + side) * inner + part % inner
                        total = kept[group, source, :, cols].astype(FAST) + got[group, source, :, cols].astype(FAST)
                        if groups == 1:
                            total = [total[:, at : at + columns] for at in range(0, wide, columns)]
                            total = total[0] if len(total) == 1 else jnp.concatenate(total, axis=0)
                            out[0, part, first : first + total.shape[0], :] = total.astype(LOW)
                        else:
                            out[first + group, part] = total.astype(LOW)
                first += rows // count if groups == 1 else kept.shape[0]


def lanes_call(values, gots, plan, bits, stacked):
    lanes = len(plan)
    parts = values[0].shape[1]
    columns = min(value.shape[3] for value in values) // lanes
    if stacked:
        shape = (1, parts // 2, sum(v.shape[2] * (v.shape[3] // lanes // columns) for v in values), columns)
    else:
        shape = (sum(v.shape[0] for v in values), parts // 2, values[0].shape[2], columns)
    whole = lambda v: pl.BlockSpec((v.shape[0], parts // 2) + v.shape[2:], lambda i: (0, i, 0, 0))
    half = pl.BlockSpec((shape[0], parts // 4) + shape[2:], lambda i: (0, i, 0, 0))
    ins = [array for pair in zip(values, gots, strict=True) for array in pair]
    return pl.pallas_call(
        partial(lanes_kernel, tuple((outer // 2, inner, digit) for outer, inner, digit in plan)),
        grid=(2,),
        in_specs=[pl.BlockSpec(memory_space=pltpu.SMEM)] + [whole(v) for v in ins],
        out_specs=[half] * (2 * lanes),
        out_shape=[jax.ShapeDtypeStruct(shape, LOW)] * (2 * lanes),
        compiler_params=pltpu.CompilerParams(vmem_limit_bytes=VMEM_MIB["lanes"] << 20),
        cost_estimate=cost(6),
        name="exchange_lanes",
    )(bits, *ins)


def finish_kernel(lanes, *refs):
    ins, (o_down, o_up, *o_four) = refs[: 4 * lanes + 6], refs[4 * lanes + 6 :]
    total = lambda i, group: ins[2 * i][group, 0].astype(FAST) + ins[2 * i + 1][group, 0].astype(FAST)
    rows_down, rows, wide = o_down.shape[1], o_up.shape[1], o_down.shape[2] // lanes
    for lane in range(lanes):
        both = total(lane, 0)
        cols = slice(lane * wide, (lane + 1) * wide)
        o_down[0, :, cols] = both[:rows_down]
        for part in range(FF_PARTS):
            at = (lane * FF_PARTS + part) * wide
            first = rows_down + part * rows
            o_up[0, :, at : at + wide] = both[first : first + rows]
        for group, out in enumerate(o_four):
            out[0, :, cols] = total(lanes + lane, group)
    o_down[1] = total(2 * lanes, 0)
    o_up[1] = total(2 * lanes + 1, 0)
    for group, out in enumerate(o_four):
        out[1] = total(2 * lanes + 2, group)


def finish_call(both, four, down_two, up_two, four_two):
    rows_down, wide = down_two.value.shape[2:]
    rows, hidden = up_two.value.shape[2:]
    sums = [*both, *four, down_two, up_two, four_two]
    square = jax.ShapeDtypeStruct((2, rows, wide), FAST)
    return pl.pallas_call(
        partial(finish_kernel, len(both)),
        out_shape=[
            jax.ShapeDtypeStruct((2, rows_down, wide), FAST), jax.ShapeDtypeStruct((2, rows, hidden), FAST),
            *[square] * four_two.value.shape[0],
        ],
        compiler_params=pltpu.CompilerParams(vmem_limit_bytes=VMEM_MIB["finish"] << 20),
        name="finish",
    )(*[array for one in sums for array in (one.value, one.got)])


def local(
    tokens, lengths, w_query, b_query, w_key, w_value, b_value, w_out, b_out, gain_one, shift_one,
    w_up, b_up, w_down, b_down, gain_two, shift_two, cotangent,
):
    seqs, rows, wide = tokens.shape
    hidden = w_up.shape[2]
    sizes = (seqs, rows, wide, hidden)
    weights = (w_query, w_key, w_value, w_out, w_up, w_down)
    vecs = vectors_call(b_query, b_value, b_out, gain_one, shift_one, b_down, gain_two, shift_two, b_up)
    devices = lax.axis_size("batch") * lax.axis_size("seq")
    seq_index = lax.axis_index("seq").astype(jnp.int32)
    spots = [(seq_index ^ flip) * rows for flip in (0, 1, 2, 3)]
    facts = jnp.concatenate([lengths, jnp.stack(spots)]).astype(jnp.int32)
    bits = jnp.stack([lax.axis_index(axis) >> bit & 1 for axis, bit in digit_list()]).astype(jnp.int32)
    flat = lambda value: value.reshape(seqs * rows, value.shape[-1])
    cuts = [(0, 2), (2, seqs - 2)]

    kept_one, kept_two, nears = None, None, []
    other = swapped_2(tokens, "seq", 0)
    for start, count in cuts:
        low, kept_one, _ = forward_call(
            0, False, start, count, facts, (tokens, 0), (tokens, 0), (other, 0), (tokens, 0), vecs, weights, kept_one, sizes
        )
        low, kept_one["r2"] = tie(low, kept_one["r2"])
        nears.append(swapped_2(low, "seq", 1))
    for near, (start, count) in zip(nears, cuts, strict=True):
        if kept_two is not None:
            near, kept_two["r2"] = tie(near, kept_two["r2"])
        else:
            near, kept_one["r2"] = tie(near, kept_one["r2"])
        far = swapped_2(near, "seq", 0)
        _, kept_two, _ = forward_call(
            1, True, start, count, facts, (kept_one["low"], 0), (near, start), (far, start),
            (kept_one["extra"], 0), vecs, weights, kept_two, sizes,
        )
    final = kept_two["low"]

    back_weights = (w_query, w_key, w_value)
    near_first, far_first, across_first = digit_orders()
    wgrad = partial(wgrad_call, place=bits, devices=devices)
    half = wide // 2

    kept = kept_two
    dy, df, dz1, da, dc, vec_two = ff_back_call(1, cotangent, kept, vecs, w_down, w_up, w_out)
    down_two = wgrad("down", lefts=[flat(kept["act"])], rights=[flat(dy)], chunk=wide)
    down_two, dc = Sum.begin(down_two, near_first, bits, dc)
    att = attention_back_call(1, True, 0, 2, facts, kept, dc, None)
    att = join(att, down_two)
    vec_q = att[3]
    (dc, far) = advance((dc, att[2]), down_two)
    got = swapped_2(far, "seq", 0)
    att = attention_back_call(1, True, 2, seqs - 2, facts, kept, dc, att)
    vec_q += att[3]
    att, got, df = tie(att, got, df)
    got_late = swapped_2(att[2], "seq", 0)
    ends = input_back_call(1, True, 0, 2, att[0], att[1], got, dz1, back_weights, None)
    ends, df = tie(ends, df)
    arrived = [swapped_2(ends[2], "seq", 1)]
    up_two = wgrad("up", lefts=[flat(kept["hid"])], rights=[flat(df)], chunk=half)
    up_two, (got_late, dz1) = Sum.begin(up_two, near_first, bits, (got_late, dz1))
    ends = input_back_call(1, True, 2, seqs - 2, att[0], att[1], got_late, dz1, back_weights, ends)
    ends = tie(*ends)
    arrived.append(swapped_2(ends[2], "seq", 1))
    ends = join(ends, up_two, down_two)
    pair = advance(ends[1], up_two, down_two)
    near = kept["extra"]
    four_two = wgrad(
        "four",
        lefts=[flat(kept["ctx"]), flat(kept_one["low"]), flat(near), flat(near)],
        rights=[flat(da), flat(att[0]), flat(pair[:, 0]), flat(pair[:, 1])],
        chunk=half,
    )
    four_two, arrived = Sum.begin(four_two, across_first, bits, arrived)
    vec_two = (vec_two, vec_q)
    middle = ends[0] + jnp.concatenate(arrived).astype(FAST)

    kept = kept_one
    ff = ff_back_call(0, middle, kept, vecs, w_down, w_up, w_out)
    dy, df, dz1, da, dc, vec_one = join(ff, down_two, four_two)
    dy = advance(dy, down_two, four_two)
    down_one = wgrad("down", lefts=[flat(kept["act"])], rights=[flat(dy)], chunk=wide)
    down_one, df = Sum.begin(down_one, near_first, bits, df)
    up_one = wgrad("up", lefts=[flat(kept["hid"])], rights=[flat(df)], chunk=half)
    up_one, dc = join((up_one, dc), down_one, down_two, up_two)
    up_one, dc = Sum.begin(up_one, near_first, bits, dc)
    dc = advance(dc, down_two, up_two)
    att = attention_back_call(0, False, 0, 1, facts, kept, dc, None)
    vec_q = att[3]
    att, dc = join((att, dc), up_one, up_two, down_two)
    lanes_one, dc = lanes_of(dc, down_one, up_one, stacked=True)
    dc = advance(dc, up_two)
    att = attention_back_call(0, False, 1, seqs - 1, facts, kept, dc, att)
    vec_q += att[3]
    early = [four_two, up_two, down_two]
    att, da, vec_q = join((att, da, vec_q), *lanes_one, *early)
    vectors = Whole([(vec_one, vec_q), vec_two])
    far, da = advance((att[2], da), *lanes_one, *early)
    far, da = vectors.send((far, da))
    got = swapped_2(far, "seq", 0)
    rest_one = wgrad("rest", lefts=[flat(kept["ctx"]), flat(tokens)], rights=[flat(da), flat(att[0])], chunk=half)
    rest_one, got = join((rest_one, got), vectors)
    rest_one, got = Sum.begin(rest_one, across_first, bits, got)
    got = vectors.send(got)
    pair = (att[1].astype(FAST) + got.astype(FAST)).astype(LOW)
    pairs_one = wgrad("pair", lefts=[flat(tokens)] * 2, rights=[flat(pair[:, 0]), flat(pair[:, 1])], chunk=half)
    pairs_one, dz1 = join((pairs_one, dz1), *lanes_one, rest_one, vectors, *early)
    pairs_one, dz1 = Sum.begin(pairs_one, near_first, bits, dz1)
    dz1 = advance(dz1, *lanes_one, *early)
    dz1 = vectors.send(dz1)
    ends = input_back_call(0, False, 0, 2, att[0], pair, None, dz1, back_weights, None)
    (dz1, ends) = join((dz1, ends), *lanes_one, pairs_one, vectors, *early)
    last_one, dz1 = lanes_of(dz1, rest_one, pairs_one, stacked=False)
    dz1 = advance(dz1, *lanes_one, *early)
    dz1 = vectors.send(dz1)
    ends = input_back_call(0, False, 2, seqs - 2, att[0], pair, None, dz1, back_weights, ends)
    live = [*last_one, *lanes_one, *early]
    result = join(ends[0], *live, vectors)
    while any(one.order for one in live):
        result = advance(result, *live)
        result = vectors.send(result)
        result = join(result, *live, vectors)
    vectors.send(())
    sums = finish_call(lanes_one, last_one, down_two, up_two, four_two)
    return (final, result) + gathered(sums, vectors.value, devices)


def tie(*values):
    return lax.optimization_barrier(values)


def digit_list():
    return [
        (axis, bit) for axis in ("seq", "batch") for bit in range(lax.axis_size(axis).bit_length() - 1)
    ]


def digit_orders():
    low = lax.axis_size("seq").bit_length() - 1
    high = lax.axis_size("batch").bit_length() - 1
    core, across = ("seq", 0), [("seq", bit) for bit in range(1, low)]
    near, far, late = [("batch", 0)], [("batch", 1)], [("batch", bit) for bit in range(2, high)]
    return (
        [core] + near + far + across + late,
        [core] + far + near + across + late,
        [core] + across + near + far + late,
    )


def lane_orders():
    digits = digit_list()[1:]
    across, near, far, late = digits[:1], digits[1:2], digits[2:3], digits[3:]
    return across + near + far + late, near + far + across + late, far + across + near + late


def join(values, *sums):
    live = [one for one in sums if one.got is not None]
    values, gots = lax.optimization_barrier((values, [one.got for one in live]))
    for one, got in zip(live, gots, strict=True):
        one.got = got
    return values


def advance(hold, *sums):
    live = [one for one in sums if one.order]
    if not live:
        return hold
    plan, routes = [], []
    for one in live:
        digit = one.order.pop(0)
        above = one.digits.index(digit)
        one.digits.remove(digit)
        plan.append((1 << above, 1 << len(one.digits) - above, digit_list().index(digit)))
        routes.append(digit)
    halves = step_call([one.value for one in live], [one.got for one in live], tuple(plan), live[0].bits)
    outs, hold = tie(halves[1::2], hold)
    for one, value, out, route in zip(live, halves[::2], outs, routes, strict=True):
        one.value = value
        one.got = swapped_2(out, *route)
    return hold


def lanes_of(hold, *sums, stacked):
    digits = sums[0].digits
    plan, lanes = [], []
    for order in lane_orders():
        above = digits.index(order[0])
        plan.append((1 << above, 1 << len(digits) - 1 - above, digit_list().index(order[0])))
    halves = lanes_call([one.value for one in sums], [one.got for one in sums], tuple(plan), sums[0].bits, stacked)
    outs, hold = tie(halves[1::2], hold)
    for value, out, order in zip(halves[::2], outs, lane_orders(), strict=True):
        one = Sum()
        one.value, one.bits, one.order = value, sums[0].bits, list(order[1:])
        one.digits = [digit for digit in digits if digit != order[0]]
        one.got = swapped_2(out, *order[0])
        lanes.append(one)
    return lanes, hold


class Sum:
    @classmethod
    def begin(cls, halves, order, bits, hold):
        one = cls()
        (one.value, out), hold = tie(halves, hold)
        one.bits = bits
        one.digits = list(reversed(digit_list()))[:-1]
        one.order = list(order[1:])
        one.got = swapped_2(out, *order[0])
        return one, hold


class Whole:
    def __init__(self, layers):
        rows = [jnp.concatenate([vec_low[:2], vec[2:]]) for vec, vec_low in layers]
        self.value = jnp.stack(rows)
        self.got = None
        self.order = digit_list()

    def send(self, hold):
        if self.got is not None:
            self.value = self.value + self.got
            self.got = None
        if self.order:
            self.value, hold = tie(self.value, hold)
            self.got = swapped_2(self.value, *self.order.pop(0))
        return hold


VECTORS = (1, 4, 6, 7, 8, 12, 13, 14)


def gathered(sums, vectors, devices):
    outs = [None] * 15
    for which, value in zip((11, 9, 5, 0, 2, 3), sums, strict=True):
        outs[which] = value
    mine = lax.axis_index("batch") * lax.axis_size("seq") + lax.axis_index("seq")
    width = vectors.shape[2] // devices
    small = lax.dynamic_slice_in_dim(vectors[:, :8], mine * width, width, axis=2)
    for place, which in enumerate(VECTORS):
        outs[which] = small[:, place]
    large = vectors[:, 8:].reshape(vectors.shape[0], -1)
    width = large.shape[1] // devices
    outs[10] = lax.dynamic_slice_in_dim(large, mine * width, width, axis=1)
    return tuple(outs)


def solution(mesh):
    in_specs = (
        P("batch", "seq", None),
        P("batch"),
        P(),
        P(),
        P(),
        P(),
        P(),
        P(),
        P(),
        P(),
        P(),
        P(),
        P(),
        P(),
        P(),
        P(),
        P(),
        P("batch", "seq", None),
    )
    out_specs = (
        P("batch", "seq", None),
        P("batch", "seq", None),
        P(None, ("batch", "seq"), None),
        P(None, ("batch", "seq")),
        P(None, ("batch", "seq"), None),
        P(None, ("batch", "seq"), None),
        P(None, ("batch", "seq")),
        P(None, ("batch", "seq"), None),
        P(None, ("batch", "seq")),
        P(None, ("batch", "seq")),
        P(None, ("batch", "seq")),
        P(None, ("batch", "seq"), None),
        P(None, ("batch", "seq")),
        P(None, ("batch", "seq"), None),
        P(None, ("batch", "seq")),
        P(None, ("batch", "seq")),
        P(None, ("batch", "seq")),
    )
    return jax.shard_map(local, mesh=mesh, in_specs=in_specs, out_specs=out_specs, check_vma=False)
```

```python
from functools import partial

import jax
import jax.numpy as jnp
from jax import lax
from jax.experimental import pallas as pl
from jax.experimental.pallas import tpu as pltpu
from jax.sharding import PartitionSpec as P

HEADS = 12
HEAD_DIM = 64


EPSILON = 1e-06
MASKED = -1e30


def swapped_2(value, axis, bit):
    return lax.ppermute(value, axis, [(i, i ^ 1 << bit) for i in range(lax.axis_size(axis))])


TOKENS_MINOR = (((1,), (1,)), ((), ()))
TOKENS_MAJOR = (((0,), (0,)), ((), ()))
ROOT_HALF = 0.7071067811865476
ROOT_TAU = 0.3989422804014327
VMEM_MIB = dict(forward=60, ff_back=28, attention_back=12, input_back=14, wgrad=12, step=16, lanes=20, finish=12)
FF_PARTS = 4
FACTS_TAIL = 4
FAST = jnp.float32
LOW = jnp.bfloat16


COST_SCALE = 10


def cost(microseconds):
    return pl.CostEstimate(flops=int(microseconds * COST_SCALE * 1.15e9), bytes_accessed=1, transcendentals=0)


def mm(left, right):
    return jnp.dot(left, right, preferred_element_type=FAST)


def mm_nt(left, right):
    return lax.dot_general(left, right, TOKENS_MINOR, preferred_element_type=FAST)


def mm_tn(left, right):
    return lax.dot_general(left, right, TOKENS_MAJOR, preferred_element_type=FAST)


def vectors_kernel(*refs):
    *ins, out = refs
    for place, ref in enumerate(ins[:-1]):
        out[:, place, :] = ref[...].astype(FAST)
    wide = out.shape[2]
    for part in range(FF_PARTS):
        out[:, len(ins) - 1 + part, :] = ins[-1][:, part * wide : (part + 1) * wide].astype(FAST)


def vectors_call(*vectors):
    layers, wide = vectors[0].shape
    return pl.pallas_call(
        vectors_kernel,
        out_shape=jax.ShapeDtypeStruct((layers, len(vectors) - 1 + FF_PARTS, wide), FAST),
        name="vectors",
    )(*vectors)


def row_norm(value):
    average = jnp.mean(value, axis=-1, keepdims=True)
    centred = value - average
    inverse_scale = lax.rsqrt(jnp.mean(centred * centred, axis=-1, keepdims=True) + EPSILON)
    return centred * inverse_scale, inverse_scale


def gelu_and_slope(value):
    size = jnp.abs(value)
    near = 1.0 / (1.0 + (0.3275911 * ROOT_HALF) * size)
    bell = jnp.exp(value * value * -0.5)
    poly = near * (
        0.127414796
        + near * (-0.142248368 + near * (0.7107068705 + near * (-0.7265760135 + near * 0.5307027145)))
    )
    tail = poly * bell
    below = jnp.where(value >= 0, 1.0 - tail, tail)
    return value * below, below + value * (bell * ROOT_TAU)


VEC_ROWS = dict(b_query=0, b_value=1, b_out=2, gain_one=3, shift_one=4, b_down=5, gain_two=6, shift_two=7)
VEC_UP = 8


def forward_kernel(layer, swapped, start, facts, own, near, far, top, vecs, *refs):
    weights, refs = refs[:6], refs[6:]
    refs = refs[len(refs) - 25 :]
    outs, scratch = refs[:16], refs[16:]
    (
        o_sent, o_extra, o_low, o_q, o_k, o_v, o_lse, o_ctx, o_n1, o_r1, o_hid, o_act, o_slope, o_n2, o_r2, o_done,
    ) = outs
    o_top = o_near = o_extra
    w_q, w_k, w_v, w_o, w_up, w_down, mix, ctx, sems = scratch
    first = pl.program_id(0) == 0
    held = (w_q, w_k, w_v, w_o, w_up, w_down)
    copies = [
        pltpu.make_async_copy(weights[i].at[layer], held[i], sems.at[i]) for i in range(6)
    ]

    @pl.when(first)
    def _():
        for copy in copies:
            copy.start()

    def ready(*which):
        @pl.when(first)
        def _():
            for i in which:
                copies[i].wait()

    def vec(name):
        row = VEC_ROWS[name]
        return vecs[layer, row : row + 1, :]

    rows = own.shape[1]
    x = own[0]
    ready(0, 1, 2)
    queries = (mm(x, w_q[...]) + vec("b_query")).astype(LOW)
    o_q[0] = queries * jnp.asarray(HEAD_DIM**-0.5, LOW)
    for part, source in ((0, near), (1, far)):
        block = source[0]
        o_k[0, part * rows : (part + 1) * rows, :] = mm(block, w_k[...]).astype(LOW)
        o_v[0, part * rows : (part + 1) * rows, :] = (mm(block, w_v[...]) + vec("b_value")).astype(LOW)
    spots = facts.shape[0] - FACTS_TAIL + 2 * layer
    length = facts[start + pl.program_id(0)]
    lane = lax.broadcasted_iota(jnp.int32, (1, 2 * rows), 1)
    place = jnp.where(lane < rows, facts[spots] + lane, facts[spots + 1] + (lane - rows))
    bias = jnp.where(place < length, 0.0, MASKED).astype(FAST)
    lower = lax.broadcasted_iota(jnp.int32, (1, 128), 1) < HEAD_DIM
    column = lax.broadcasted_iota(jnp.int32, (1, 128), 1)
    logs = jnp.zeros((rows, 128), FAST)
    for pair in range(HEADS // 2):
        lanes = slice(pair * 128, pair * 128 + 128)
        q_pair, k_pair, v_pair = o_q[0, :, lanes], o_k[0, :, lanes], o_v[0, :, lanes]
        got = []
        for side in range(2):
            mask = lower if side == 0 else ~lower
            q_one = jnp.where(mask, q_pair, jnp.zeros_like(q_pair))
            scores = mm_nt(q_one, k_pair) + bias
            high = jnp.max(scores, axis=-1, keepdims=True)
            weight = jnp.exp(scores - high)
            total = jnp.sum(weight, axis=-1, keepdims=True)
            got.append(mm(weight.astype(LOW), v_pair) * (1.0 / total))
            logs = jnp.where(column == 2 * pair + side, high + jnp.log(total), logs)
        ctx[:, lanes] = jnp.where(lower, got[0], got[1]).astype(LOW)
    o_lse[0] = logs.T[:16, :]
    o_ctx[0] = ctx[...]
    ready(3)
    branch = mm(ctx[...], w_o[...]) + vec("b_out") + top[0].astype(FAST)
    n1, r1 = row_norm(branch)
    o_n1[0] = n1.astype(LOW)
    o_r1[0] = r1
    hidden = n1 * vec("gain_one") + vec("shift_one")
    hid = hidden.astype(LOW)
    o_hid[0] = hid
    mix[...] = hidden + vec("b_down")
    ready(4, 5)
    width = w_up.shape[1] // FF_PARTS
    for part in range(FF_PARTS):
        cols = slice(part * width, (part + 1) * width)
        pre = mm(hid, w_up[:, cols]) + vecs[layer, VEC_UP + part : VEC_UP + part + 1, :]
        act, slope = gelu_and_slope(pre)
        act = act.astype(LOW)
        o_act[0, :, cols] = act
        o_slope[0, :, cols] = slope.astype(LOW)
        mix[...] += mm(act, w_down[cols, :])
    n2, r2 = row_norm(mix[...])
    o_n2[0] = n2.astype(LOW)
    o_r2[0] = r2
    result = n2 * vec("gain_two") + vec("shift_two")
    if not swapped:
        o_top[0] = result
    low = result.astype(LOW)
    o_sent[0] = low
    if swapped:
        o_near[0] = near[0]
    o_low[0] = low
    o_done[...] = jnp.zeros_like(o_done)


KEPT = ("extra", "low", "q", "k", "v", "lse", "ctx", "n1", "r1", "hid", "act", "slope", "n2", "r2")


def first_forward_kernel(layer, swapped, start, facts, own, far, vecs, *refs):
    forward_kernel(layer, swapped, start, facts, own, own, far, own, vecs, *refs)


def forward_call(layer, swapped, start, count, facts, own, near, far, top, vecs, weights, kept, sizes):
    seqs, rows, wide, hidden = sizes

    def taken(source):
        array, offset = source
        return pl.BlockSpec((1,) + array.shape[1:], lambda i: (start - offset + i, 0, 0))

    shapes = dict(
        extra=((rows, wide), LOW if swapped else FAST), low=((rows, wide), LOW),
        q=((rows, wide), LOW), k=((2 * rows, wide), LOW), v=((2 * rows, wide), LOW), lse=((16, rows), FAST),
        ctx=((rows, wide), LOW), n1=((rows, wide), LOW), r1=((rows, 1), FAST), hid=((rows, wide), LOW),
        act=((rows, hidden), LOW), slope=((rows, hidden), LOW), n2=((rows, wide), LOW), r2=((rows, 1), FAST),
    )
    out_shape = [jax.ShapeDtypeStruct((count, rows, wide), LOW)] + [
        jax.ShapeDtypeStruct((seqs,) + shapes[name][0], shapes[name][1]) for name in KEPT
    ]
    out_specs = [pl.BlockSpec((1, rows, wide), lambda i: (i, 0, 0))] + [
        pl.BlockSpec((1,) + shapes[name][0], lambda i: (start + i, 0, 0)) for name in KEPT
    ]
    out_shape.append(jax.ShapeDtypeStruct((8, 128), FAST))
    out_specs.append(pl.BlockSpec((8, 128), lambda i: (0, 0)))
    any_spec = pl.BlockSpec(memory_space=pl.ANY)
    ins = [facts, own[0], near[0], far[0], top[0], vecs, *weights]
    in_specs = [
        pl.BlockSpec(memory_space=pltpu.SMEM), taken(own), taken(near), taken(far), taken(top),
        pl.BlockSpec(vecs.shape, lambda i: (0, 0, 0)),
    ] + [any_spec] * 6
    kernel = forward_kernel
    if own[0] is near[0] and own[0] is top[0]:
        kernel = first_forward_kernel
        for place in (4, 2):
            del ins[place], in_specs[place]
    aliases = {}
    if kept is not None:
        for place, name in enumerate(KEPT):
            aliases[len(ins) + place] = 1 + place
        ins += [kept[name] for name in KEPT]
        in_specs += [any_spec] * len(KEPT)
    got = pl.pallas_call(
        partial(kernel, layer, swapped, start),
        grid=(count,),
        in_specs=in_specs,
        out_specs=out_specs,
        out_shape=out_shape,
        input_output_aliases=aliases,
        scratch_shapes=[
            pltpu.VMEM((wide, wide), LOW), pltpu.VMEM((wide, wide), LOW), pltpu.VMEM((wide, wide), LOW),
            pltpu.VMEM((wide, wide), LOW), pltpu.VMEM((wide, hidden), LOW), pltpu.VMEM((hidden, wide), LOW),
            pltpu.VMEM((rows, wide), FAST), pltpu.VMEM((rows, wide), LOW), pltpu.SemaphoreType.DMA((6,)),
        ],
        compiler_params=pltpu.CompilerParams(vmem_limit_bytes=VMEM_MIB["forward"] << 20),
        cost_estimate=cost(14 * count),
        name=f"layer_forward_{layer}",
    )(*ins)
    return got[0], dict(zip(KEPT, got[1:-1], strict=True)), got[-1]


def norm_back_rows(grad, normed, inverse_scale, gain):
    dn = grad * gain
    return inverse_scale * (
        dn - jnp.mean(dn, axis=-1, keepdims=True) - normed * jnp.mean(dn * normed, axis=-1, keepdims=True)
    )


def column_sum(value):
    return jnp.sum(value.astype(FAST), axis=0, keepdims=True)


def ff_back_kernel(layer, top_grad, n2, r2, slope, n1, r1, vecs, *refs):
    weights, refs = refs[:3], refs[3:]
    o_dy, o_df, o_dz1, o_da, o_dc, o_vec, w_down, w_up, w_o, mix, sems = refs
    first = pl.program_id(0) == 0
    held = (w_down, w_up, w_o)
    copies = [pltpu.make_async_copy(weights[i].at[layer], held[i], sems.at[i]) for i in range(3)]

    @pl.when(first)
    def _():
        for copy in copies:
            copy.start()
        o_vec[...] = jnp.zeros_like(o_vec)

    def ready(which):
        @pl.when(first)
        def _():
            copies[which].wait()

    def vec(name):
        row = VEC_ROWS[name]
        return vecs[layer, row : row + 1, :]

    def add(row, value):
        o_vec[row : row + 1, :] += value

    grad = top_grad[0].astype(FAST)
    normed = n2[0].astype(FAST)
    add(VEC_ROWS["gain_two"], column_sum(grad * normed))
    add(VEC_ROWS["shift_two"], column_sum(grad))
    dz2 = norm_back_rows(grad, normed, r2[0], vec("gain_two"))
    dy = dz2.astype(LOW)
    o_dy[0] = dy
    add(VEC_ROWS["b_down"], column_sum(dy))
    mix[...] = dz2
    ready(0)
    width = w_up.shape[1] // FF_PARTS
    for part in range(FF_PARTS):
        cols = slice(part * width, (part + 1) * width)
        if part == 0:
            ready(1)
        df = (mm_nt(dy, w_down[cols, :]) * slope[0, :, cols].astype(FAST)).astype(LOW)
        o_df[0, :, cols] = df
        add(VEC_UP + part, column_sum(df))
        mix[...] += mm_nt(df, w_up[:, cols])
    grad = mix[...]
    normed = n1[0].astype(FAST)
    add(VEC_ROWS["gain_one"], column_sum(grad * normed))
    add(VEC_ROWS["shift_one"], column_sum(grad))
    dz1 = norm_back_rows(grad, normed, r1[0], vec("gain_one"))
    o_dz1[0] = dz1
    da = dz1.astype(LOW)
    o_da[0] = da
    add(VEC_ROWS["b_out"], column_sum(da))
    ready(2)
    o_dc[0] = mm_nt(da, w_o[...]).astype(LOW)


def ff_back_call(layer, top_grad, kept, vecs, w_down, w_up, w_out):
    seqs, rows, wide = top_grad.shape
    hidden = w_up.shape[2]
    ins = [top_grad, kept["n2"], kept["r2"], kept["slope"], kept["n1"], kept["r1"], vecs, w_down, w_up, w_out]
    each = lambda shape: pl.BlockSpec((1,) + tuple(shape[1:]), lambda i: (i, 0, 0))
    any_spec = pl.BlockSpec(memory_space=pl.ANY)
    in_specs = [each(x.shape) for x in ins[:6]] + [pl.BlockSpec(vecs.shape, lambda i: (0, 0, 0))] + [any_spec] * 3
    out_shape = [
        jax.ShapeDtypeStruct((seqs, rows, wide), LOW), jax.ShapeDtypeStruct((seqs, rows, hidden), LOW),
        jax.ShapeDtypeStruct((seqs, rows, wide), FAST), jax.ShapeDtypeStruct((seqs, rows, wide), LOW),
        jax.ShapeDtypeStruct((seqs, rows, wide), LOW), jax.ShapeDtypeStruct((vecs.shape[1], wide), FAST),
    ]
    out_specs = [each(x.shape) for x in out_shape[:5]] + [pl.BlockSpec(out_shape[5].shape, lambda i: (0, 0))]
    return pl.pallas_call(
        partial(ff_back_kernel, layer),
        grid=(seqs,),
        in_specs=in_specs,
        out_specs=out_specs,
        out_shape=out_shape,
        scratch_shapes=[
            pltpu.VMEM((hidden, wide), LOW), pltpu.VMEM((wide, hidden), LOW), pltpu.VMEM((wide, wide), LOW),
            pltpu.VMEM((rows, wide), FAST), pltpu.SemaphoreType.DMA((3,)),
        ],
        compiler_params=pltpu.CompilerParams(vmem_limit_bytes=VMEM_MIB["ff_back"] << 20),
        cost_estimate=cost(19),
        name=f"ff_back_{layer}",
    )(*ins)


def attention_back_kernel(layer, start, facts, q, k, v, lse, dc, *refs):
    o_dq, o_near, o_far, o_vec, bias = refs[len(refs) - 5 :]
    rows, wide = q.shape[1], q.shape[2]

    @pl.when(pl.program_id(0) == 0)
    def _():
        o_vec[...] = jnp.zeros_like(o_vec)

    spots = facts.shape[0] - FACTS_TAIL + 2 * layer
    length = facts[start + pl.program_id(0)]
    key = lax.broadcasted_iota(jnp.int32, (2 * rows, rows), 0)
    place = jnp.where(key < rows, facts[spots] + key, facts[spots + 1] + (key - rows))
    bias[...] = jnp.where(place < length, 0.0, MASKED).astype(FAST)
    lower = lax.broadcasted_iota(jnp.int32, (1, 128), 1) < HEAD_DIM
    for pair in range(HEADS // 2):
        lanes = slice(pair * 128, pair * 128 + 128)
        q_pair, k_pair, v_pair, dc_pair = q[0, :, lanes], k[0, :, lanes], v[0, :, lanes], dc[0, :, lanes]
        dk = dv = None
        dq = []
        for side in range(2):
            one = 2 * pair + side
            mask = lower if side == 0 else ~lower
            q_one = jnp.where(mask, q_pair, jnp.zeros_like(q_pair))
            dc_one = jnp.where(mask, dc_pair, jnp.zeros_like(dc_pair))
            weight = jnp.exp(mm_nt(k_pair, q_one) + bias[...] - lse[0, one : one + 1, :])
            product = weight * mm_nt(v_pair, dc_one)
            ds = (product - weight * jnp.sum(product, axis=0, keepdims=True)).astype(LOW)
            dv_one = mm(weight.astype(LOW), dc_one)
            dk_one = mm(ds, q_one)
            dv = dv_one if dv is None else dv + dv_one
            dk = dk_one if dk is None else dk + dk_one
            dq.append(mm_tn(k_pair, ds)[side * HEAD_DIM : (side + 1) * HEAD_DIM])
        dq_pair = (jnp.concatenate(dq, axis=0).T * HEAD_DIM**-0.5).astype(LOW)
        o_dq[0, :, lanes] = dq_pair
        o_vec[0:1, lanes] += column_sum(dq_pair)
        o_vec[1:2, lanes] += column_sum(dv)
        o_near[0, 0, :, lanes] = dk[:rows].astype(LOW)
        o_far[0, 0, :, lanes] = dk[rows:].astype(LOW)
        o_near[0, 1, :, lanes] = dv[:rows].astype(LOW)
        o_far[0, 1, :, lanes] = dv[rows:].astype(LOW)


def blocks(shape, start):
    rest = len(shape) - 1
    return pl.BlockSpec((1,) + tuple(shape[1:]), lambda i: (start + i,) + (0,) * rest)


def chained(ins, in_specs, earlier, places):
    aliases = {}
    if earlier is not None:
        for array, place in zip(earlier, places, strict=True):
            aliases[len(ins)] = place
            ins.append(array)
            in_specs.append(pl.BlockSpec(memory_space=pl.ANY))
    return aliases


def attention_back_call(layer, split, start, count, facts, kept, dc, earlier):
    seqs, rows, wide = dc.shape
    ins = [facts, kept["q"], kept["k"], kept["v"], kept["lse"], dc]
    in_specs = [pl.BlockSpec(memory_space=pltpu.SMEM)] + [blocks(x.shape, start) for x in ins[1:]]
    whole = jax.ShapeDtypeStruct((seqs, rows, wide), LOW)
    both = jax.ShapeDtypeStruct((seqs, 2, rows, wide), LOW)
    single = jax.ShapeDtypeStruct((count, 2, rows, wide), LOW)
    out_shape = [whole, both, single if split else both, jax.ShapeDtypeStruct((8, wide), FAST)]
    out_specs = [
        blocks(whole.shape, start), blocks(both.shape, start), blocks(both.shape, 0 if split else start),
        pl.BlockSpec((8, wide), lambda i: (0, 0)),
    ]
    places = (0, 1) if split else (0, 1, 2)
    aliases = chained(ins, in_specs, earlier and earlier[: len(places)], places)
    return pl.pallas_call(
        partial(attention_back_kernel, layer, start),
        grid=(count,),
        in_specs=in_specs,
        out_specs=out_specs,
        out_shape=out_shape,
        input_output_aliases=aliases,
        scratch_shapes=[pltpu.VMEM((2 * rows, rows), FAST)],
        compiler_params=pltpu.CompilerParams(vmem_limit_bytes=VMEM_MIB["attention_back"] << 20),
        cost_estimate=cost(8 * count),
        name=f"attention_back_{layer}",
    )(*ins)


def input_back_kernel(layer, split, dq, near, *refs):
    got, refs = (refs[0], refs[1:]) if split else (None, refs)
    dz1, *refs = refs
    weights, refs = refs[:3], refs[3:]
    if split:
        o_own, o_pair, o_sent, w_q, w_k, w_v, sems = refs[len(refs) - 7 :]
    else:
        o_own, w_q, w_k, w_v, sems = refs[len(refs) - 5 :]
    first = pl.program_id(0) == 0
    held = (w_q, w_k, w_v)
    copies = [pltpu.make_async_copy(weights[i].at[layer], held[i], sems.at[i]) for i in range(3)]

    @pl.when(first)
    def _():
        for copy in copies:
            copy.start()

    if split:
        dk = (near[0, 0].astype(FAST) + got[0, 0].astype(FAST)).astype(LOW)
        dv = (near[0, 1].astype(FAST) + got[0, 1].astype(FAST)).astype(LOW)
        o_pair[0, 0] = dk
        o_pair[0, 1] = dv
    else:
        dk, dv = near[0, 0], near[0, 1]

    @pl.when(first)
    def _():
        for copy in copies:
            copy.wait()

    far = mm_nt(dk, w_k[...]) + mm_nt(dv, w_v[...])
    here = dz1[0] + mm_nt(dq[0], w_q[...])
    if split:
        o_sent[0] = far.astype(LOW)
        o_own[0] = here
    else:
        o_own[0] = here + far


def input_back_call(layer, split, start, count, dq, near, got, dz1, weights, earlier):
    seqs, rows, wide = dq.shape
    ins = [dq, near]
    in_specs = [blocks(dq.shape, start), blocks(near.shape, start)]
    if split:
        ins.append(got)
        in_specs.append(blocks(got.shape, 0))
    ins += [dz1, *weights]
    in_specs += [blocks(dz1.shape, start)] + [pl.BlockSpec(memory_space=pl.ANY)] * 3
    out_shape = [jax.ShapeDtypeStruct((seqs, rows, wide), FAST)]
    out_specs = [blocks(dz1.shape, start)]
    if split:
        out_shape += [
            jax.ShapeDtypeStruct((seqs, 2, rows, wide), LOW), jax.ShapeDtypeStruct((count, rows, wide), LOW)
        ]
        out_specs += [blocks(out_shape[1].shape, start), blocks(out_shape[2].shape, 0)]
    places = (0, 1) if split else (0,)
    aliases = chained(ins, in_specs, earlier and earlier[: len(places)], places)
    return pl.pallas_call(
        partial(input_back_kernel, layer, split),
        grid=(count,),
        in_specs=in_specs,
        out_specs=out_specs,
        out_shape=out_shape,
        input_output_aliases=aliases,
        scratch_shapes=[pltpu.VMEM((wide, wide), LOW)] * 3 + [pltpu.SemaphoreType.DMA((3,))],
        compiler_params=pltpu.CompilerParams(vmem_limit_bytes=VMEM_MIB["input_back"] << 20),
        cost_estimate=cost(2 + 3 * count),
        name=f"input_back_{layer}",
    )(*ins)


def wgrad_kernel(count, place_ref, *refs):
    lefts, rights, (o_kept, o_sent) = refs[:count], refs[count : 2 * count], refs[2 * count :]
    pairs, rows = o_kept.shape[1], o_kept.shape[2]

    def write(o_even, o_odd):
        for i in range(count):
            full = mm_tn(lefts[i][...], rights[i][...])
            for pair in range(pairs):
                start = 2 * pair * rows
                o_even[i, pair] = full[start : start + rows].astype(LOW)
                o_odd[i, pair] = full[start + rows : start + 2 * rows].astype(LOW)

    @pl.when(place_ref[0] == 0)
    def _():
        write(o_kept, o_sent)

    @pl.when(place_ref[0] == 1)
    def _():
        write(o_sent, o_kept)


def wgrad_call(name, place, devices, lefts, rights, chunk):
    tokens, height = lefts[0].shape
    width = rights[0].shape[1]
    count = len(lefts)
    rows = height // devices
    steps = height // chunk
    shape = jax.ShapeDtypeStruct((count, devices // 2, rows, width), LOW)
    out_spec = pl.BlockSpec((count, devices // 2 // steps, rows, width), lambda i: (0, i, 0, 0))
    return pl.pallas_call(
        partial(wgrad_kernel, count),
        grid=(steps,),
        in_specs=[pl.BlockSpec(memory_space=pltpu.SMEM)]
        + [pl.BlockSpec((tokens, chunk), lambda i: (0, i))] * count
        + [pl.BlockSpec((tokens, width), lambda i: (0, 0))] * count,
        out_specs=[out_spec] * 2,
        out_shape=[shape] * 2,
        compiler_params=pltpu.CompilerParams(vmem_limit_bytes=VMEM_MIB["wgrad"] << 20),
        cost_estimate=cost(3 + 2 * count * height * width / 1e6),
        name=f"wgrad_{name}",
    )(place, *lefts, *rights)


def step_kernel(plan, bits, *refs):
    count = len(plan)
    for i, (outer, inner, digit) in enumerate(plan):
        kept, got = refs[2 * i], refs[2 * i + 1]
        o_kept, o_sent = refs[2 * count + 2 * i], refs[2 * count + 2 * i + 1]
        mine = bits[digit]
        for group in range(kept.shape[0]):
            for a in range(outer):
                for out, side in ((o_kept, mine), (o_sent, 1 - mine)):
                    source = pl.ds((2 * a + side) * inner, inner)
                    total = kept[group, source].astype(FAST) + got[group, source].astype(FAST)
                    out[group, a * inner : (a + 1) * inner] = total.astype(LOW)


def step_call(values, gots, plan, bits):
    steps = 1 if any(value.shape[3] % 384 for value in values) else 3
    ins, in_specs, out_specs, out_shape, moved = [], [], [], [], 0
    for value, got in zip(values, gots, strict=True):
        groups, parts, rows, columns = value.shape
        whole = pl.BlockSpec((groups, parts, rows, columns // steps), lambda i: (0, 0, 0, i))
        half = pl.BlockSpec((groups, parts // 2, rows, columns // steps), lambda i: (0, 0, 0, i))
        ins += [value, got]
        in_specs += [whole] * 2
        out_specs += [half] * 2
        out_shape += [jax.ShapeDtypeStruct((groups, parts // 2, rows, columns), LOW)] * 2
        moved += 6 * value.size
    return pl.pallas_call(
        partial(step_kernel, plan),
        grid=(steps,),
        in_specs=[pl.BlockSpec(memory_space=pltpu.SMEM)] + in_specs,
        out_specs=out_specs,
        out_shape=out_shape,
        compiler_params=pltpu.CompilerParams(vmem_limit_bytes=VMEM_MIB["step"] << 20),
        cost_estimate=cost(1 + moved / 3e6),
        name="exchange_step",
    )(bits, *ins)


def lanes_kernel(plan, bits, *refs):
    count = len(refs) // 2 - len(plan)
    ins, outs = refs[: 2 * count], refs[2 * count :]
    for lane, (outer, inner, digit) in enumerate(plan):
        mine = bits[digit]
        for out, side in ((outs[2 * lane], mine), (outs[2 * lane + 1], 1 - mine)):
            groups, parts, rows, columns = out.shape
            first = 0
            for i in range(count):
                kept, got = ins[2 * i], ins[2 * i + 1]
                wide = kept.shape[3] // len(plan)
                cols = slice(lane * wide, (lane + 1) * wide)
                for group in range(kept.shape[0]):
                    for part in range(parts):
                        source = (2 * (part // inner) + side) * inner + part % inner
                        total = kept[group, source, :, cols].astype(FAST) + got[group, source, :, cols].astype(FAST)
                        if groups == 1:
                            total = [total[:, at : at + columns] for at in range(0, wide, columns)]
                            total = total[0] if len(total) == 1 else jnp.concatenate(total, axis=0)
                            out[0, part, first : first + total.shape[0], :] = total.astype(LOW)
                        else:
                            out[first + group, part] = total.astype(LOW)
                first += rows // count if groups == 1 else kept.shape[0]


def lanes_call(values, gots, plan, bits, stacked):
    lanes = len(plan)
    parts = values[0].shape[1]
    columns = min(value.shape[3] for value in values) // lanes
    if stacked:
        shape = (1, parts // 2, sum(v.shape[2] * (v.shape[3] // lanes // columns) for v in values), columns)
    else:
        shape = (sum(v.shape[0] for v in values), parts // 2, values[0].shape[2], columns)
    whole = lambda v: pl.BlockSpec((v.shape[0], parts // 2) + v.shape[2:], lambda i: (0, i, 0, 0))
    half = pl.BlockSpec((shape[0], parts // 4) + shape[2:], lambda i: (0, i, 0, 0))
    ins = [array for pair in zip(values, gots, strict=True) for array in pair]
    return pl.pallas_call(
        partial(lanes_kernel, tuple((outer // 2, inner, digit) for outer, inner, digit in plan)),
        grid=(2,),
        in_specs=[pl.BlockSpec(memory_space=pltpu.SMEM)] + [whole(v) for v in ins],
        out_specs=[half] * (2 * lanes),
        out_shape=[jax.ShapeDtypeStruct(shape, LOW)] * (2 * lanes),
        compiler_params=pltpu.CompilerParams(vmem_limit_bytes=VMEM_MIB["lanes"] << 20),
        cost_estimate=cost(6),
        name="exchange_lanes",
    )(bits, *ins)


def finish_kernel(lanes, *refs):
    ins, (o_down, o_up, *o_four) = refs[: 4 * lanes + 6], refs[4 * lanes + 6 :]
    total = lambda i, group: ins[2 * i][group, 0].astype(FAST) + ins[2 * i + 1][group, 0].astype(FAST)
    rows_down, rows, wide = o_down.shape[1], o_up.shape[1], o_down.shape[2] // lanes
    for lane in range(lanes):
        both = total(lane, 0)
        cols = slice(lane * wide, (lane + 1) * wide)
        o_down[0, :, cols] = both[:rows_down]
        for part in range(FF_PARTS):
            at = (lane * FF_PARTS + part) * wide
            first = rows_down + part * rows
            o_up[0, :, at : at + wide] = both[first : first + rows]
        for group, out in enumerate(o_four):
            out[0, :, cols] = total(lanes + lane, group)
    o_down[1] = total(2 * lanes, 0)
    o_up[1] = total(2 * lanes + 1, 0)
    for group, out in enumerate(o_four):
        out[1] = total(2 * lanes + 2, group)


def finish_call(both, four, down_two, up_two, four_two):
    rows_down, wide = down_two.value.shape[2:]
    rows, hidden = up_two.value.shape[2:]
    sums = [*both, *four, down_two, up_two, four_two]
    square = jax.ShapeDtypeStruct((2, rows, wide), FAST)
    return pl.pallas_call(
        partial(finish_kernel, len(both)),
        out_shape=[
            jax.ShapeDtypeStruct((2, rows_down, wide), FAST), jax.ShapeDtypeStruct((2, rows, hidden), FAST),
            *[square] * four_two.value.shape[0],
        ],
        compiler_params=pltpu.CompilerParams(vmem_limit_bytes=VMEM_MIB["finish"] << 20),
        name="finish",
    )(*[array for one in sums for array in (one.value, one.got)])


def local(
    tokens, lengths, w_query, b_query, w_key, w_value, b_value, w_out, b_out, gain_one, shift_one,
    w_up, b_up, w_down, b_down, gain_two, shift_two, cotangent,
):
    seqs, rows, wide = tokens.shape
    hidden = w_up.shape[2]
    sizes = (seqs, rows, wide, hidden)
    weights = (w_query, w_key, w_value, w_out, w_up, w_down)
    vecs = vectors_call(b_query, b_value, b_out, gain_one, shift_one, b_down, gain_two, shift_two, b_up)
    devices = lax.axis_size("batch") * lax.axis_size("seq")
    seq_index = lax.axis_index("seq").astype(jnp.int32)
    spots = [(seq_index ^ flip) * rows for flip in (0, 1, 2, 3)]
    facts = jnp.concatenate([lengths, jnp.stack(spots)]).astype(jnp.int32)
    bits = jnp.stack([lax.axis_index(axis) >> bit & 1 for axis, bit in digit_list()]).astype(jnp.int32)
    flat = lambda value: value.reshape(seqs * rows, value.shape[-1])
    cuts = [(0, 2), (2, seqs - 2)]

    kept_one, kept_two, nears = None, None, []
    other = swapped_2(tokens, "seq", 0)
    for start, count in cuts:
        low, kept_one, _ = forward_call(
            0, False, start, count, facts, (tokens, 0), (tokens, 0), (other, 0), (tokens, 0), vecs, weights, kept_one, sizes
        )
        low, kept_one["r2"] = tie(low, kept_one["r2"])
        nears.append(swapped_2(low, "seq", 1))
    for near, (start, count) in zip(nears, cuts, strict=True):
        if kept_two is not None:
            near, kept_two["r2"] = tie(near, kept_two["r2"])
        else:
            near, kept_one["r2"] = tie(near, kept_one["r2"])
        far = swapped_2(near, "seq", 0)
        _, kept_two, _ = forward_call(
            1, True, start, count, facts, (kept_one["low"], 0), (near, start), (far, start),
            (kept_one["extra"], 0), vecs, weights, kept_two, sizes,
        )
    final = kept_two["low"]

    back_weights = (w_query, w_key, w_value)
    near_first, far_first, across_first = digit_orders()
    wgrad = partial(wgrad_call, place=bits, devices=devices)
    half = wide // 2

    kept = kept_two
    dy, df, dz1, da, dc, vec_two = ff_back_call(1, cotangent, kept, vecs, w_down, w_up, w_out)
    down_two = wgrad("down", lefts=[flat(kept["act"])], rights=[flat(dy)], chunk=wide)
    down_two, dc = Sum.begin(down_two, near_first, bits, dc)
    att = attention_back_call(1, True, 0, 2, facts, kept, dc, None)
    att = join(att, down_two)
    vec_q = att[3]
    (dc, far) = advance((dc, att[2]), down_two)
    got = swapped_2(far, "seq", 0)
    att = attention_back_call(1, True, 2, seqs - 2, facts, kept, dc, att)
    vec_q += att[3]
    att, got, df = tie(att, got, df)
    got_late = swapped_2(att[2], "seq", 0)
    ends = input_back_call(1, True, 0, 2, att[0], att[1], got, dz1, back_weights, None)
    ends, df = tie(ends, df)
    arrived = [swapped_2(ends[2], "seq", 1)]
    up_two = wgrad("up", lefts=[flat(kept["hid"])], rights=[flat(df)], chunk=half)
    up_two, (got_late, dz1) = Sum.begin(up_two, near_first, bits, (got_late, dz1))
    ends = input_back_call(1, True, 2, seqs - 2, att[0], att[1], got_late, dz1, back_weights, ends)
    ends = tie(*ends)
    arrived.append(swapped_2(ends[2], "seq", 1))
    ends = join(ends, up_two, down_two)
    pair = advance(ends[1], up_two, down_two)
    near = kept["extra"]
    four_two = wgrad(
        "four",
        lefts=[flat(kept["ctx"]), flat(kept_one["low"]), flat(near), flat(near)],
        rights=[flat(da), flat(att[0]), flat(pair[:, 0]), flat(pair[:, 1])],
        chunk=half,
    )
    four_two, arrived = Sum.begin(four_two, across_first, bits, arrived)
    vec_two = (vec_two, vec_q)
    middle = ends[0] + jnp.concatenate(arrived).astype(FAST)

    kept = kept_one
    ff = ff_back_call(0, middle, kept, vecs, w_down, w_up, w_out)
    dy, df, dz1, da, dc, vec_one = join(ff, down_two, four_two)
    dy = advance(dy, down_two, four_two)
    down_one = wgrad("down", lefts=[flat(kept["act"])], rights=[flat(dy)], chunk=wide)
    down_one, df = Sum.begin(down_one, near_first, bits, df)
    up_one = wgrad("up", lefts=[flat(kept["hid"])], rights=[flat(df)], chunk=half)
    up_one, dc = join((up_one, dc), down_one, down_two, up_two)
    up_one, dc = Sum.begin(up_one, near_first, bits, dc)
    dc = advance(dc, down_two, up_two)
    att = attention_back_call(0, False, 0, 1, facts, kept, dc, None)
    vec_q = att[3]
    att, dc = join((att, dc), up_one, up_two, down_two)
    lanes_one, dc = lanes_of(dc, down_one, up_one, stacked=True)
    dc = advance(dc, up_two)
    att = attention_back_call(0, False, 1, seqs - 1, facts, kept, dc, att)
    vec_q += att[3]
    early = [four_two, up_two, down_two]
    att, da, vec_q = join((att, da, vec_q), *lanes_one, *early)
    vectors = Whole([(vec_one, vec_q), vec_two])
    far, da = advance((att[2], da), *lanes_one, *early)
    far, da = vectors.send((far, da))
    got = swapped_2(far, "seq", 0)
    rest_one = wgrad("rest", lefts=[flat(kept["ctx"]), flat(tokens)], rights=[flat(da), flat(att[0])], chunk=half)
    rest_one, got = join((rest_one, got), vectors)
    rest_one, got = Sum.begin(rest_one, across_first, bits, got)
    got = vectors.send(got)
    pair = (att[1].astype(FAST) + got.astype(FAST)).astype(LOW)
    pairs_one = wgrad("pair", lefts=[flat(tokens)] * 2, rights=[flat(pair[:, 0]), flat(pair[:, 1])], chunk=half)
    pairs_one, dz1 = join((pairs_one, dz1), *lanes_one, rest_one, vectors, *early)
    pairs_one, dz1 = Sum.begin(pairs_one, near_first, bits, dz1)
    dz1 = advance(dz1, *lanes_one, *early)
    dz1 = vectors.send(dz1)
    ends = input_back_call(0, False, 0, 2, att[0], pair, None, dz1, back_weights, None)
    (dz1, ends) = join((dz1, ends), *lanes_one, pairs_one, vectors, *early)
    last_one, dz1 = lanes_of(dz1, rest_one, pairs_one, stacked=False)
    dz1 = advance(dz1, *lanes_one, *early)
    dz1 = vectors.send(dz1)
    ends = input_back_call(0, False, 2, seqs - 2, att[0], pair, None, dz1, back_weights, ends)
    live = [*last_one, *lanes_one, *early]
    result = join(ends[0], *live, vectors)
    while any(one.order for one in live):
        result = advance(result, *live)
        result = vectors.send(result)
        result = join(result, *live, vectors)
    vectors.send(())
    sums = finish_call(lanes_one, last_one, down_two, up_two, four_two)
    return (final, result) + gathered(sums, vectors.value, devices)


def tie(*values):
    return lax.optimization_barrier(values)


def digit_list():
    return [
        (axis, bit) for axis in ("seq", "batch") for bit in range(lax.axis_size(axis).bit_length() - 1)
    ]


def digit_orders():
    low = lax.axis_size("seq").bit_length() - 1
    high = lax.axis_size("batch").bit_length() - 1
    core, across = ("seq", 0), [("seq", bit) for bit in range(1, low)]
    near, far, late = [("batch", 0)], [("batch", 1)], [("batch", bit) for bit in range(2, high)]
    return (
        [core] + near + far + across + late,
        [core] + far + near + across + late,
        [core] + across + near + far + late,
    )


def lane_orders():
    digits = digit_list()[1:]
    across, near, far, late = digits[:1], digits[1:2], digits[2:3], digits[3:]
    return across + near + far + late, near + far + across + late, far + across + near + late


def join(values, *sums):
    live = [one for one in sums if one.got is not None]
    values, gots = lax.optimization_barrier((values, [one.got for one in live]))
    for one, got in zip(live, gots, strict=True):
        one.got = got
    return values


def advance(hold, *sums):
    live = [one for one in sums if one.order]
    if not live:
        return hold
    plan, routes = [], []
    for one in live:
        digit = one.order.pop(0)
        above = one.digits.index(digit)
        one.digits.remove(digit)
        plan.append((1 << above, 1 << len(one.digits) - above, digit_list().index(digit)))
        routes.append(digit)
    halves = step_call([one.value for one in live], [one.got for one in live], tuple(plan), live[0].bits)
    outs, hold = tie(halves[1::2], hold)
    for one, value, out, route in zip(live, halves[::2], outs, routes, strict=True):
        one.value = value
        one.got = swapped_2(out, *route)
    return hold


def lanes_of(hold, *sums, stacked):
    digits = sums[0].digits
    plan, lanes = [], []
    for order in lane_orders():
        above = digits.index(order[0])
        plan.append((1 << above, 1 << len(digits) - 1 - above, digit_list().index(order[0])))
    halves = lanes_call([one.value for one in sums], [one.got for one in sums], tuple(plan), sums[0].bits, stacked)
    outs, hold = tie(halves[1::2], hold)
    for value, out, order in zip(halves[::2], outs, lane_orders(), strict=True):
        one = Sum()
        one.value, one.bits, one.order = value, sums[0].bits, list(order[1:])
        one.digits = [digit for digit in digits if digit != order[0]]
        one.got = swapped_2(out, *order[0])
        lanes.append(one)
    return lanes, hold


class Sum:
    @classmethod
    def begin(cls, halves, order, bits, hold):
        one = cls()
        (one.value, out), hold = tie(halves, hold)
        one.bits = bits
        one.digits = list(reversed(digit_list()))[:-1]
        one.order = list(order[1:])
        one.got = swapped_2(out, *order[0])
        return one, hold


class Whole:
    def __init__(self, layers):
        rows = [jnp.concatenate([vec_low[:2], vec[2:]]) for vec, vec_low in layers]
        self.value = jnp.stack(rows)
        self.got = None
        self.order = digit_list()

    def send(self, hold):
        if self.got is not None:
            self.value = self.value + self.got
            self.got = None
        if self.order:
            self.value, hold = tie(self.value, hold)
            self.got = swapped_2(self.value, *self.order.pop(0))
        return hold


VECTORS = (1, 4, 6, 7, 8, 12, 13, 14)


def gathered(sums, vectors, devices):
    outs = [None] * 15
    for which, value in zip((11, 9, 5, 0, 2, 3), sums, strict=True):
        outs[which] = value
    mine = lax.axis_index("batch") * lax.axis_size("seq") + lax.axis_index("seq")
    width = vectors.shape[2] // devices
    small = lax.dynamic_slice_in_dim(vectors[:, :8], mine * width, width, axis=2)
    for place, which in enumerate(VECTORS):
        outs[which] = small[:, place]
    large = vectors[:, 8:].reshape(vectors.shape[0], -1)
    width = large.shape[1] // devices
    outs[10] = lax.dynamic_slice_in_dim(large, mine * width, width, axis=1)
    return tuple(outs)


def solution(mesh):
    in_specs = (
        P("batch", "seq", None),
        P("batch"),
        P(),
        P(),
        P(),
        P(),
        P(),
        P(),
        P(),
        P(),
        P(),
        P(),
        P(),
        P(),
        P(),
        P(),
        P(),
        P("batch", "seq", None),
    )
    out_specs = (
        P("batch", "seq", None),
        P("batch", "seq", None),
        P(None, ("batch", "seq"), None),
        P(None, ("batch", "seq")),
        P(None, ("batch", "seq"), None),
        P(None, ("batch", "seq"), None),
        P(None, ("batch", "seq")),
        P(None, ("batch", "seq"), None),
        P(None, ("batch", "seq")),
        P(None, ("batch", "seq")),
        P(None, ("batch", "seq")),
        P(None, ("batch", "seq"), None),
        P(None, ("batch", "seq")),
        P(None, ("batch", "seq"), None),
        P(None, ("batch", "seq")),
        P(None, ("batch", "seq")),
        P(None, ("batch", "seq")),
    )
    return jax.shard_map(local, mesh=mesh, in_specs=in_specs, out_specs=out_specs, check_vma=False)
```
